32 devices in a mesh: seq: 8 (over z, y), tensor: 4 (over x, core).
Axes of the slice: x: 2, y: 2, z: 4, core: 2. Of those that a mesh axis runs over, the one named last changes fastest.
Arguments:
- inputs: bfloat16 [6144, 2560], P(('seq', 'tensor')), may hold values from -6 to 6
- segments: int32 [6144], replicated, may hold values from 0 to 31, as said below
- positions: int32 [6144], P('seq'), may hold values from 0 to 4046, as said below
- gain_attn: float32 [2560], P('seq'), may hold values from 0.5 to 1.5
- query_weight: float32 [2560, 2560], P('seq', 'tensor'), may hold values from -0.125 to 0.125
- key_weight: float32 [2560, 640], P('seq', 'tensor'), may hold values from -0.125 to 0.125
- value_weight: float32 [2560, 640], P('seq', 'tensor'), may hold values from -0.125 to 0.125
- out_weight: float32 [2560, 2560], P('tensor', 'seq'), may hold values from -2 to 2
- gain_mlp: float32 [2560], P('seq'), may hold values from 0.5 to 1.5
- gate_weight: float32 [2560, 6912], P('seq', 'tensor'), may hold values from -0.125 to 0.125
- up_weight: float32 [2560, 6912], P('seq', 'tensor'), may hold values from -0.125 to 0.125
- down_weight: float32 [6912, 2560], P('tensor', 'seq'), may hold values from -0.078125 to 0.078125
- cotangent: bfloat16 [6144, 2560], P(('seq', 'tensor')), may hold values from -6 to 6
Outputs:
- output: bfloat16 [6144, 2560], P(('seq', 'tensor'))
- input_grad: bfloat16 [6144, 2560], P(('seq', 'tensor'))
- gain_attn_grad: float32 [2560], P('seq')
- query_weight_grad: float32 [2560, 2560], P('seq', 'tensor')
- key_weight_grad: float32 [2560, 640], P('seq', 'tensor')
- value_weight_grad: float32 [2560, 640], P('seq', 'tensor')
- out_weight_grad: float32 [2560, 2560], P('tensor', 'seq')
- gain_mlp_grad: float32 [2560], P('seq')
- gate_weight_grad: float32 [2560, 6912], P('seq', 'tensor')
- up_weight_grad: float32 [2560, 6912], P('seq', 'tensor')
- down_weight_grad: float32 [6912, 2560], P('tensor', 'seq')
The draws below stay inside these ranges and needn't reach their ends.
Inputs may be any that keep to these rules, and one draw needn't show every extreme that they name: `segments`: tokens k * 3072 to (k + 1) * 3072 - 1 form packed sequence k. Each sequence is cut into documents of consecutive tokens; within a sequence document numbers rise by one from each document to the next, and every number of a sequence is larger than every number of an earlier one; the first sequence starts at 0 and the last document of the last sequence carries the largest number. No document crosses a sequence's end. A document holds 200 to 2000 tokens, except the last one of a sequence, which may hold fewer; the first document of the first sequence holds exactly 2000. `positions`: A token's position is its index within its document plus an offset of 0 to 2047 shared by the whole document; the first document of the first sequence has offset 2047.
All inputs are finite; a program needn't handle non-finite values.
Results may differ from the reference program's by a relative error of at most 0.023.
Values may be sent and summed in bfloat16 or wider, within the bound.
No kernel may reach another device: no remote copies, remote signals or barrier semaphores. Data moves between devices by JAX's collectives and lax.ppermute only.
A program may use at most 256 MiB of HBM per device.

```python
import jax
import jax.numpy as jnp
from jax import lax

D = 2560
FF = 6912
HEADS = 32
KV = 8
HD = 80
SEQS = 2
DOC_MOST = 2000
DOC_LEAST = 200
TOKENS = 6144
LENGTH = 3072


def documents(key):
    doc_count = LENGTH // DOC_LEAST + 1
    first_key, second_key = jax.random.split(key)
    sizes = jax.random.randint(first_key, (SEQS, doc_count), DOC_LEAST, DOC_MOST + 1, dtype=jnp.int32)
    sizes = sizes.at[0, 0].set(DOC_MOST)
    starts = jnp.cumsum(sizes, axis=1) - sizes
    places = jnp.arange(LENGTH, dtype=jnp.int32)
    within = jnp.sum((starts[:, None, 1:] <= places[None, :, None]).astype(jnp.int32), axis=2)
    begins = jnp.take_along_axis(starts, within, axis=1)
    offsets = jax.random.randint(second_key, (SEQS, doc_count), 0, 2048, dtype=jnp.int32)
    offsets = offsets.at[0, 0].set(2047)
    shifted = jnp.take_along_axis(offsets, within, axis=1)
    used = within[:, -1] + 1
    seq_numbers = jnp.arange(SEQS, dtype=jnp.int32)
    bases = jnp.where(seq_numbers == 0, 0, (seq_numbers + 1) * doc_count - used)
    labels = within + bases[:, None]
    return (labels.reshape(TOKENS), (places[None, :] - begins + shifted).reshape(TOKENS))


def draw_segments(key, part):
    labels, places = documents(key)
    return labels


def draw_positions(key, part):
    labels, places = documents(key)
    return places


def raised(drawn, rng, source, target, blocks, factor):
    owner, partner = [(jnp.arange(drawn.shape[position]) // (drawn.shape[position] // blocks)).reshape([-1 if axis == position else 1 for axis in range(drawn.ndim)]) for position in (source, target)]
    chosen = jax.random.permutation(rng, blocks)[partner]
    strong = (owner == chosen) | (owner == (partner + blocks // 2) % blocks)
    return jnp.where(strong, factor * drawn, drawn)


def steps_of(own_key, extent, cuts, smallest, top_value):
    def one(dim, parts):
        draws = jax.random.uniform(jax.random.fold_in(jax.random.fold_in(own_key, 6), dim), (parts,), jnp.float32, smallest / len(cuts), top_value / len(cuts))
        return jnp.repeat(jnp.exp(draws), extent[dim] // parts).reshape((-1,) + (1,) * (len(extent) - dim - 1))

    loudness = one(*cuts[0])
    for cut in cuts[1:]:
        loudness = loudness * one(*cut)
    return loudness


def scatter_about(rng, shape, spread, reach, cuts=(), kind=jnp.bfloat16):
    entries = jax.random.normal(rng, shape, jnp.float32) * spread
    if len(cuts) > 0:
        entries = steps_of(rng, shape, cuts, -0.22, 0.18) * entries
    return jnp.clip(entries, min=-reach, max=reach).astype(kind)


def heavy_noise(stream_key, dims, deviation, reach, cuts, heavy, kind=jnp.bfloat16):
    drawn = deviation * jax.random.normal(stream_key, dims, jnp.float32)
    if cuts:
        drawn = drawn * steps_of(stream_key, dims, cuts, -0.22, 0.18)
    return jnp.clip(raised(drawn, jax.random.fold_in(stream_key, 3), *heavy), -reach, reach).astype(kind)


def setup_inputs(seed: int = 0) -> dict:
    splits = jax.random.split(jax.random.key(seed), 14)
    inputs = heavy_noise(splits[0], (TOKENS, D), 1.0, 6.0, ((0, 32),), (0, 1, 32, 2.75))
    segments = draw_segments(jax.random.fold_in(splits[13], 71), 0)
    positions = draw_positions(jax.random.fold_in(splits[13], 71), 0)
    gain_attn = jnp.clip(1.0 + 0.1 * jax.random.normal(splits[3], (D,), jnp.float32), 0.5, 1.5)
    query_weight = scatter_about(splits[4], (D, HEADS * HD), D ** -0.5, 0.125, ((0, 8), (1, 4)), jnp.float32)
    key_weight = scatter_about(splits[5], (D, KV * HD), D ** -0.5, 0.125, ((0, 8), (1, 4)), jnp.float32)
    value_weight = scatter_about(splits[6], (D, KV * HD), D ** -0.5, 0.125, ((0, 8), (1, 4)), jnp.float32)
    out_weight = scatter_about(splits[7], (HEADS * HD, D), (max(HEADS * HD // 256, 1)) ** -0.5, 2.0, ((0, 4), (1, 8)), jnp.float32)
    gain_mlp = jnp.clip(1.0 + 0.1 * jax.random.normal(splits[8], (D,), jnp.float32), 0.5, 1.5)
    gate_weight = scatter_about(splits[9], (D, FF), D ** -0.5, 0.125, ((0, 8), (1, 4)), jnp.float32)
    up_weight = scatter_about(splits[10], (D, FF), D ** -0.5, 0.125, ((0, 8), (1, 4)), jnp.float32)
    down_weight = scatter_about(splits[11], (FF, D), FF ** -0.5, 0.078125, ((0, 4), (1, 8)), jnp.float32)
    cotangent = heavy_noise(splits[12], (TOKENS, D), 1.0, 6.0, ((0, 32),), (0, 1, 32, 2.75))
    return {"inputs": inputs, "segments": segments, "positions": positions, "gain_attn": gain_attn, "query_weight": query_weight, "key_weight": key_weight, "value_weight": value_weight, "out_weight": out_weight, "gain_mlp": gain_mlp, "gate_weight": gate_weight, "up_weight": up_weight, "down_weight": down_weight, "cotangent": cotangent}


@jax.custom_vjp
def low(v):
    return lax.optimization_barrier(v.astype(jnp.bfloat16)).astype(jnp.float32)

@jax.custom_vjp
def low_back(v):
    return v

def low_keep(v):
    return (low(v), None)

def low_pass(kept, grad):
    return (grad,)

def back_keep(v):
    return (v, None)

def back_low(kept, grad):
    return (low(grad),)
low.defvjp(low_keep, low_pass)
low_back.defvjp(back_keep, back_low)
eps = 1e-05
rope_base = 10000.0

def matmul(left_side, right_side):
    return jnp.dot(left_side, right_side, precision=lax.Precision.HIGHEST, preferred_element_type=jnp.float32)

def rms_norm(values, gain_vec):
    return values * lax.rsqrt(lax.optimization_barrier(jnp.mean(values * values, axis=-1, keepdims=True)) + eps) * gain_vec

def rope_tables(positions):
    half_width = HD // 2
    frequency = rope_base ** (-(jnp.arange(half_width, dtype=jnp.float32) * 2.0 / HD))
    angles = positions.astype(jnp.float32)[:, None] * frequency[None, :]
    return (jnp.cos(angles)[:, None, :], jnp.sin(angles)[:, None, :])

def rotate(values, cos_tab, sine_tab):
    half_width = HD // 2
    front_half = values[..., :half_width]
    back_half = values[..., half_width:]
    return jnp.concatenate([front_half * cos_tab - back_half * sine_tab, back_half * cos_tab + front_half * sine_tab], axis=-1)

def attention(queries, keys_in, values_in, segments):
    all_rows = queries.shape[0]
    group_size = HEADS // KV
    block_rows = min(all_rows, 512)
    blocks = all_rows // block_rows
    back_rows = DOC_MOST
    score_scale = HD ** (-0.5)
    query_blocks = queries.reshape(blocks, block_rows, KV, group_size, HD)
    keys_pad = jnp.concatenate([jnp.zeros((back_rows, KV * HD), jnp.float32), keys_in]).reshape(-1, KV, HD)
    values_pad = jnp.concatenate([jnp.zeros((back_rows, KV * HD), jnp.float32), values_in]).reshape(-1, KV, HD)
    segs_pad = jnp.concatenate([jnp.full((back_rows,), -1, jnp.int32), segments.astype(jnp.int32)])

    def one_block(packed):
        number, query_blk = packed
        first_row = (number * block_rows).astype(jnp.int32)
        key_blk = lax.dynamic_slice_in_dim(keys_pad, first_row, back_rows + block_rows, 0)
        value_blk = lax.dynamic_slice_in_dim(values_pad, first_row, back_rows + block_rows, 0)
        key_segs = lax.dynamic_slice_in_dim(segs_pad, first_row, back_rows + block_rows, 0)
        query_segs = lax.dynamic_slice_in_dim(segments.astype(jnp.int32), first_row, block_rows, 0)
        query_places = first_row + jnp.arange(block_rows, dtype=jnp.int32)
        key_places = first_row - back_rows + jnp.arange(back_rows + block_rows, dtype=jnp.int32)
        allowed = (query_segs[:, None] == key_segs[None, :]) & (key_places[None, :] <= query_places[:, None])
        scores = jnp.einsum('qcgd,kcd->cgqk', query_blk, key_blk, precision=lax.Precision.HIGHEST) * score_scale
        scores = low_back(scores)
        scores = jnp.where(allowed, scores, -1e+30)
        attn_probs = jax.nn.softmax(scores, axis=-1)
        out_blk = jnp.einsum('cgqk,kcd->qcgd', low(attn_probs), value_blk, precision=lax.Precision.HIGHEST)
        return out_blk.reshape(block_rows, KV * group_size * HD)
    result = lax.map(jax.checkpoint(one_block), (jnp.arange(blocks, dtype=jnp.int32), query_blocks))
    return result.reshape(all_rows, HEADS * HD)

def reference(inputs, segments, positions, gain_attn, query_weight, key_weight, value_weight, out_weight, gain_mlp, gate_weight, up_weight, down_weight, cotangent):
    cos_tab, sine_tab = rope_tables(positions)
    all_rows = inputs.shape[0]

    def forward(input_f32, gain_one, weight_q, weight_k, weight_v, weight_o, gain_two, weight_g, weight_u, weight_d):
        h_one = low(rms_norm(input_f32, low(gain_one)))
        q_pre = low_back(matmul(h_one, low(weight_q)))
        k_pre = low_back(matmul(h_one, low(weight_k)))
        v_pre = low_back(matmul(h_one, low(weight_v)))
        queries = low(rotate(q_pre.reshape(all_rows, HEADS, HD), cos_tab, sine_tab).reshape(all_rows, HEADS * HD))
        keys_rot = low(rotate(k_pre.reshape(all_rows, KV, HD), cos_tab, sine_tab).reshape(all_rows, KV * HD))
        values_all = low(v_pre)
        attended = low(low_back(attention(queries, keys_rot, values_all, segments)))
        x_mid = input_f32 + low_back(matmul(attended, low(weight_o)))
        h_two = low(rms_norm(x_mid, low(gain_two)))
        gate_pre = low_back(matmul(h_two, low(weight_g)))
        up_pre = low_back(matmul(h_two, low(weight_u)))
        hidden = low(jax.nn.silu(gate_pre) * up_pre)
        return x_mid + low_back(matmul(hidden, low(weight_d)))
    result, pull = jax.vjp(forward, inputs.astype(jnp.float32), gain_attn, query_weight, key_weight, value_weight, out_weight, gain_mlp, gate_weight, up_weight, down_weight)
    grads = pull(cotangent.astype(jnp.float32))
    return (result.astype(jnp.bfloat16), grads[0].astype(jnp.bfloat16), grads[1], grads[2], grads[3], grads[4], grads[5], grads[6], grads[7], grads[8], grads[9])
```

```python
import functools

import jax
import jax.numpy as jnp
from jax import lax
from jax.experimental import pallas as pl
from jax.experimental.pallas import tpu as pltpu
from jax.sharding import Mesh
from jax.sharding import PartitionSpec as P

HEADS = 32
KV = 8
HD = 80
SEQS = 2
DOC_MOST = 2000
GROUP = HEADS // KV

eps = 1e-05
rope_base = 10000.0
LOG2E = 1.4426950408889634
SCORE_LOG2 = HD ** (-0.5) * LOG2E
SCORE_SCALE = HD ** (-0.5)
LOW = -1e30
BQ = 256
KB = 256
WIDE = jnp.bfloat16
F32 = jnp.float32
VMEM_BYTES = 48 * 1024 * 1024

SWAP = [(0, 1), (1, 0)]


def dot(a, b, ca, cb):
    return lax.dot_general(a, b, (((ca,), (cb,)), ((), ())), preferred_element_type=F32)


def turn_kernel(rotary, heads, index_ref, rows_ref, cos_ref, sin_ref, out_ref):
    own = rows_ref.shape[0] // 8
    half = HD // 2
    for pair in range(4):
        parts = [
            rows_ref[pl.ds(pl.multiple_of(index_ref[2 * pair + k] * own, own), own), :].astype(F32)
            for k in range(2)
        ]
        turned = jnp.concatenate(parts, axis=0).T
        lanes = slice(pair * 2 * own, (pair + 1) * 2 * own)
        cos_tab, sin_tab = cos_ref[:, lanes], sin_ref[:, lanes]
        for h in range(heads):
            front, back = turned[h * HD : h * HD + half], turned[h * HD + half : (h + 1) * HD]
            if h < rotary:
                front, back = front * cos_tab - back * sin_tab, back * cos_tab + front * sin_tab
            out_ref[h * HD : (h + 1) * HD, lanes] = jnp.concatenate([front, back], axis=0).astype(
                out_ref.dtype
            )


def to_columns(rows, index, cos_tab, sin_tab, rotary, heads):
    count = rows.shape[0]
    full = lambda shape: pl.BlockSpec(shape, lambda i, s: (0, 0))
    return pl.pallas_call(
        functools.partial(turn_kernel, rotary, heads),
        grid_spec=pltpu.PrefetchScalarGridSpec(
            num_scalar_prefetch=1,
            grid=(1,),
            in_specs=[full(rows.shape), full(cos_tab.shape), full(sin_tab.shape)],
            out_specs=full((heads * HD, count)),
        ),
        out_shape=jax.ShapeDtypeStruct((heads * HD, count), WIDE),
        compiler_params=pltpu.CompilerParams(vmem_limit_bytes=VMEM_BYTES),
    )(index, rows, cos_tab, sin_tab)


def back_kernel(rotary, heads, index_ref, cols_ref, cos_ref, sin_ref, out_ref):
    own = cols_ref.shape[1] // 8
    half = HD // 2
    width = out_ref.shape[1]
    for pair in range(4):
        lanes = slice(pair * 2 * own, (pair + 1) * 2 * own)
        cos_tab, sin_tab = cos_ref[:, lanes], sin_ref[:, lanes]
        parts = []
        for h in range(heads):
            front = cols_ref[h * HD : h * HD + half, lanes].astype(F32)
            back = cols_ref[h * HD + half : (h + 1) * HD, lanes].astype(F32)
            if h < rotary:
                front, back = front * cos_tab + back * sin_tab, back * cos_tab - front * sin_tab
            parts += [front, back]
        if width > heads * HD:
            parts.append(jnp.zeros((width - heads * HD, 2 * own), F32))
        rows = jnp.concatenate(parts, axis=0).T.astype(out_ref.dtype)
        for k in range(2):
            first = pl.multiple_of(index_ref[2 * pair + k] * own, own)
            out_ref[pl.ds(first, own), :] = rows[k * own : (k + 1) * own]


def to_rows(cols, index, cos_tab, sin_tab, rotary, heads, width):
    count = cols.shape[1]
    full = lambda shape: pl.BlockSpec(shape, lambda i, s: (0, 0))
    return pl.pallas_call(
        functools.partial(back_kernel, rotary, heads),
        grid_spec=pltpu.PrefetchScalarGridSpec(
            num_scalar_prefetch=1,
            grid=(1,),
            in_specs=[full(cols.shape), full(cos_tab.shape), full(sin_tab.shape)],
            out_specs=full((count, width)),
        ),
        out_shape=jax.ShapeDtypeStruct((count, width), WIDE),
        compiler_params=pltpu.CompilerParams(vmem_limit_bytes=VMEM_BYTES),
    )(index, cols, cos_tab, sin_tab)


def allowed_mask(block, starts, own_places):
    places = block * KB + lax.broadcasted_iota(jnp.int32, (KB, 1), 0)
    return (places >= starts) & (places <= own_places)


def attend_kernel(span_before, bounds_ref, q_ref, kv_ref, start_ref, out_ref, log_ref, k_rows, acc):
    step = pl.program_id(0)
    span = kv_ref.shape[1]

    @pl.when(step == 0)
    def _():
        for j in range(span // KB):
            k_rows[j * KB : (j + 1) * KB, :] = (
                kv_ref[0:HD, j * KB : (j + 1) * KB].astype(F32).T.astype(WIDE)
            )

    starts = start_ref[0:1, :]
    own_places = span_before + step * BQ + lax.broadcasted_iota(jnp.int32, (1, BQ), 1)
    acc[...] = jnp.zeros_like(acc)

    def one(masked, block, carry):
        first = pl.multiple_of(block * KB, KB)
        keys = k_rows[pl.ds(first, KB), :]
        values = kv_ref[HD : 2 * HD, pl.ds(first, KB)]
        if masked:
            mask = allowed_mask(block, starts, own_places)
        fresh = []
        for h in range(GROUP):
            top, total = carry[2 * h], carry[2 * h + 1]
            scores = dot(keys, q_ref[h * HD : (h + 1) * HD, :], 1, 0) * SCORE_LOG2
            if masked:
                scores = jnp.where(mask, scores, LOW)
            new_top = jnp.maximum(top, jnp.max(scores, axis=0, keepdims=True))
            probs = jnp.exp2(scores - new_top)
            fade = jnp.exp2(top - new_top)
            total = fade * total + jnp.sum(probs, axis=0, keepdims=True)
            acc[h] = fade * acc[h] + dot(values, probs.astype(WIDE), 1, 0)
            fresh += [new_top, total]
        return tuple(fresh)

    carry = (jnp.full((1, BQ), LOW, F32), jnp.zeros((1, BQ), F32)) * GROUP
    lo, full_lo, full_hi, hi = [bounds_ref[k, step] for k in range(4)]
    carry = lax.fori_loop(lo, full_lo, functools.partial(one, True), carry)
    carry = lax.fori_loop(full_lo, full_hi, functools.partial(one, False), carry)
    carry = lax.fori_loop(full_hi, hi, functools.partial(one, True), carry)
    for h in range(GROUP):
        top, total = carry[2 * h], carry[2 * h + 1]
        out_ref[h * HD : (h + 1) * HD, :] = (acc[h] / total).astype(WIDE)
        log_ref[h : h + 1, :] = top + jnp.log2(total)


def attend(q_cols, kv_cols, starts, bounds):
    count, span = q_cols.shape[1], kv_cols.shape[1]
    return pl.pallas_call(
        functools.partial(attend_kernel, span - count),
        grid_spec=pltpu.PrefetchScalarGridSpec(
            num_scalar_prefetch=1,
            grid=(count // BQ,),
            in_specs=[
                pl.BlockSpec((GROUP * HD, BQ), lambda i, s: (0, i)),
                pl.BlockSpec((2 * HD, span), lambda i, s: (0, 0)),
                pl.BlockSpec((1, BQ), lambda i, s: (0, i)),
            ],
            out_specs=[
                pl.BlockSpec((GROUP * HD, BQ), lambda i, s: (0, i)),
                pl.BlockSpec((8, BQ), lambda i, s: (0, i)),
            ],
            scratch_shapes=[pltpu.VMEM((span, HD), WIDE), pltpu.VMEM((GROUP, HD, BQ), F32)],
        ),
        out_shape=[
            jax.ShapeDtypeStruct((GROUP * HD, count), WIDE),
            jax.ShapeDtypeStruct((8, count), F32),
        ],
        compiler_params=pltpu.CompilerParams(vmem_limit_bytes=VMEM_BYTES),
    )(bounds, q_cols, kv_cols, starts)


def attend_back_kernel(
    span_before,
    bounds_ref,
    q_ref,
    kv_ref,
    start_ref,
    out_ref,
    log_ref,
    grad_ref,
    dq_ref,
    dkv_ref,
    k_rows,
    v_rows,
    q_rows,
    g_rows,
    dk,
    dv,
    probs_all,
    grads_all,
    dq,
):
    step = pl.program_id(0)
    span = kv_ref.shape[1]

    @pl.when(step == 0)
    def _():
        for j in range(span // KB):
            lanes = slice(j * KB, (j + 1) * KB)
            k_rows[lanes, :] = kv_ref[0:HD, lanes].astype(F32).T.astype(WIDE)
            v_rows[lanes, :] = kv_ref[HD : 2 * HD, lanes].astype(F32).T.astype(WIDE)
        dk[...] = jnp.zeros_like(dk)
        dv[...] = jnp.zeros_like(dv)

    starts = start_ref[0:1, :]
    own_places = span_before + step * BQ + lax.broadcasted_iota(jnp.int32, (1, BQ), 1)
    dq[...] = jnp.zeros_like(dq)
    deltas = []
    for h in range(GROUP):
        part = slice(h * HD, (h + 1) * HD)
        q_f32, g_f32 = q_ref[part, :].astype(F32), grad_ref[part, :].astype(F32)
        q_rows[h * BQ : (h + 1) * BQ, :] = q_f32.T.astype(WIDE)
        g_rows[h * BQ : (h + 1) * BQ, :] = g_f32.T.astype(WIDE)
        deltas.append(jnp.sum(g_f32 * out_ref[part, :].astype(F32), axis=0, keepdims=True))

    def one(masked, block, carry):
        first = pl.multiple_of(block * KB, KB)
        rows = pl.ds(first, KB)
        keys, values = k_rows[rows, :], v_rows[rows, :]
        key_cols = kv_ref[0:HD, rows]
        if masked:
            mask = allowed_mask(block, starts, own_places)
        for h in range(GROUP):
            part = slice(h * HD, (h + 1) * HD)
            lanes = slice(h * BQ, (h + 1) * BQ)
            scores = dot(keys, q_ref[part, :], 1, 0) * SCORE_LOG2 - log_ref[h : h + 1, :]
            if masked:
                scores = jnp.where(mask, scores, LOW)
            probs = jnp.exp2(scores)
            grad_probs = dot(values, grad_ref[part, :], 1, 0)
            grad_scores = (probs * (grad_probs - deltas[h])).astype(WIDE)
            probs_all[:, lanes] = probs.astype(WIDE)
            grads_all[:, lanes] = grad_scores
            dq[h] += dot(key_cols, grad_scores, 1, 0)
        dv[rows, :] += dot(probs_all[...], g_rows[...], 1, 0)
        dk[rows, :] += dot(grads_all[...], q_rows[...], 1, 0)
        return carry

    lo, full_lo, full_hi, hi = [bounds_ref[k, step] for k in range(4)]
    lax.fori_loop(lo, full_lo, functools.partial(one, True), 0)
    lax.fori_loop(full_lo, full_hi, functools.partial(one, False), 0)
    lax.fori_loop(full_hi, hi, functools.partial(one, True), 0)
    for h in range(GROUP):
        dq_ref[h * HD : (h + 1) * HD, :] = dq[h] * SCORE_SCALE

    @pl.when(step == pl.num_programs(0) - 1)
    def _():
        for j in range(span // KB):
            lanes = slice(j * KB, (j + 1) * KB)
            dkv_ref[0:HD, lanes] = dk[lanes, :].T * SCORE_SCALE
            dkv_ref[HD : 2 * HD, lanes] = dv[lanes, :].T


def attend_back(q_cols, kv_cols, starts, bounds, out_cols, logs, grad_cols):
    count, span = q_cols.shape[1], kv_cols.shape[1]
    wide_block = pl.BlockSpec((GROUP * HD, BQ), lambda i, s: (0, i))
    return pl.pallas_call(
        functools.partial(attend_back_kernel, span - count),
        grid_spec=pltpu.PrefetchScalarGridSpec(
            num_scalar_prefetch=1,
            grid=(count // BQ,),
            in_specs=[
                wide_block,
                pl.BlockSpec((2 * HD, span), lambda i, s: (0, 0)),
                pl.BlockSpec((1, BQ), lambda i, s: (0, i)),
                wide_block,
                pl.BlockSpec((8, BQ), lambda i, s: (0, i)),
                wide_block,
            ],
            out_specs=[wide_block, pl.BlockSpec((2 * HD, span), lambda i, s: (0, 0))],
            scratch_shapes=[
                pltpu.VMEM((span, HD), WIDE),
                pltpu.VMEM((span, HD), WIDE),
                pltpu.VMEM((GROUP * BQ, HD), WIDE),
                pltpu.VMEM((GROUP * BQ, HD), WIDE),
                pltpu.VMEM((span, HD), F32),
                pltpu.VMEM((span, HD), F32),
                pltpu.VMEM((KB, GROUP * BQ), WIDE),
                pltpu.VMEM((KB, GROUP * BQ), WIDE),
                pltpu.VMEM((GROUP, HD, BQ), F32),
            ],
        ),
        out_shape=[
            jax.ShapeDtypeStruct((GROUP * HD, count), F32),
            jax.ShapeDtypeStruct((2 * HD, span), F32),
        ],
        compiler_params=pltpu.CompilerParams(vmem_limit_bytes=VMEM_BYTES),
    )(bounds, q_cols, kv_cols, starts, out_cols, logs, grad_cols)


def shifted(block, distance):
    count = lax.axis_size("z")
    route = [(i - distance, i) for i in range(count) if 0 <= i - distance < count]
    return lax.ppermute(block, "z", route)


def gather_plane(block):
    half = block.shape[0] // 2
    over_x = lax.ppermute(block, "x", SWAP)
    over_y = lax.ppermute(block, "y", SWAP)
    far_top = lax.ppermute(over_y[:half], "x", SWAP)
    far_low = lax.ppermute(over_x[half:], "y", SWAP)
    mine = [block, over_x, over_y, far_top, far_low]
    other = [lax.ppermute(part, "c", SWAP) for part in mine]
    return jnp.concatenate(mine + other, axis=0)


def sum_plane(term):
    own = term.shape[0] // 8
    half = own // 2
    low = term.astype(WIDE)
    got = lax.ppermute(low[4 * own :], "c", SWAP)
    total = low[: 4 * own].astype(F32) + got.astype(F32)
    far = total[3 * own :].astype(WIDE)
    top = lax.ppermute(far[:half], "x", SWAP)
    bottom = lax.ppermute(far[half:], "y", SWAP)
    to_x = jnp.concatenate(
        [total[own : own + half], total[own + half : 2 * own] + bottom.astype(F32)], axis=0
    ).astype(WIDE)
    to_y = jnp.concatenate(
        [total[2 * own : 2 * own + half] + top.astype(F32), total[2 * own + half : 3 * own]],
        axis=0,
    ).astype(WIDE)
    over_x = lax.ppermute(to_x, "x", SWAP)
    over_y = lax.ppermute(to_y, "y", SWAP)
    return total[:own] + over_x.astype(F32) + over_y.astype(F32)


def share_columns(block, first_y):
    half = block.shape[1] // 2
    keep = jnp.where(first_y, block[:, :half], block[:, half:])
    give = jnp.where(first_y, block[:, half:], block[:, :half])
    got = lax.ppermute(give, "y", SWAP)
    return jnp.concatenate([jnp.where(first_y, keep, got), jnp.where(first_y, got, keep)], axis=0)


def unshare_columns(block, first_y):
    half = block.shape[0] // 2
    keep = jnp.where(first_y, block[:half], block[half:])
    give = jnp.where(first_y, block[half:], block[:half])
    got = lax.ppermute(give, "y", SWAP)
    return jnp.where(first_y, keep, got), jnp.where(first_y, got, keep)


def gather_z(block):
    return lax.all_gather(block, "z", axis=0, tiled=True)


def sum_z(block):
    return lax.psum_scatter(block.astype(WIDE), "z", scatter_dimension=0, tiled=True)


def padded(block, multiple=128):
    extra = -block.shape[1] % multiple
    return jnp.pad(block, ((0, 0), (0, extra))) if extra else block


def norm_back(gradient, normed, inverse, gain_vec):
    scaled = gradient * gain_vec
    return inverse * (scaled - normed * jnp.mean(scaled * normed, axis=-1, keepdims=True))


def per_device(
    inputs,
    segments,
    positions,
    gain_attn,
    query_weight,
    key_weight,
    value_weight,
    out_weight,
    gain_mlp,
    gate_weight,
    up_weight,
    down_weight,
    cotangent,
):
    own = inputs.shape[0]
    count = 8 * own
    length = segments.shape[0] // SEQS
    reach = (DOC_MOST - 2) // count + 1
    if length % count == 0:
        reach = min(reach, length // count - 1)
    span = (reach + 1) * count
    z, y = lax.axis_index("z"), lax.axis_index("y")
    x, c = lax.axis_index("x"), lax.axis_index("c")
    first_y = y == 0

    w_q, w_k, w_v, w_g, w_u = [
        w.astype(WIDE) for w in (query_weight, key_weight, value_weight, gate_weight, up_weight)
    ]
    w_o, w_d = out_weight.T.astype(WIDE), down_weight.T.astype(WIDE)
    nq, nk, nf = w_q.shape[1] // 2, w_k.shape[1] // 2, w_g.shape[1] // 2
    rows_w = w_q.shape[0]
    gains = gather_z(
        lax.all_gather(jnp.stack([gain_attn, gain_mlp], 1).astype(WIDE), "y", axis=0, tiled=True)
    ).astype(F32)
    gain_first, gain_second = gains[:, 0], gains[:, 1]
    halves = lambda w: (w[:, : w.shape[1] // 2], w[:, w.shape[1] // 2 :])
    interleave = lambda *ws: jnp.concatenate(
        [padded(jnp.concatenate([halves(w)[i] for w in ws], axis=1)) for i in range(2)], axis=1
    )
    full_a = gather_z(share_columns(interleave(w_q, w_k, w_v), first_y))
    full_o = gather_z(share_columns(w_o, first_y))
    full_g = gather_z(share_columns(interleave(w_g), first_y))
    full_u = gather_z(share_columns(interleave(w_u), first_y))
    full_d = gather_z(share_columns(interleave(w_d), first_y))

    other_positions = lax.ppermute(positions, "y", SWAP)
    token_positions = jnp.where(
        first_y,
        jnp.concatenate([positions, other_positions]),
        jnp.concatenate([other_positions, positions]),
    )
    frequency = rope_base ** (-(jnp.arange(HD // 2, dtype=F32) * 2.0 / HD))
    angles = frequency[:, None] * token_positions.astype(F32)[None, :]
    cos_tab, sin_tab = jnp.cos(angles), jnp.sin(angles)
    places = jnp.arange(8, dtype=jnp.int32)
    flips = places ^ (y * 4 + x * 2 + c).astype(jnp.int32)
    index = (flips % 2) * 4 + flips // 2
    padded_segs = jnp.concatenate([jnp.full((reach * count,), -1, jnp.int32), segments])
    key_segs = lax.dynamic_slice_in_dim(padded_segs, z * count, span, 0)
    query_segs = lax.dynamic_slice_in_dim(segments, z * count, count, 0)
    starts = jnp.sum((key_segs[:, None] < query_segs[None, :]).astype(jnp.int32), axis=0)
    first_rows = jnp.arange(count // BQ, dtype=jnp.int32) * BQ
    lo = starts[first_rows] // KB
    hi = (reach * count + first_rows + BQ + KB - 1) // KB
    full_lo = jnp.clip((starts[first_rows + BQ - 1] + KB - 1) // KB, lo, hi)
    full_hi = jnp.clip((reach * count + first_rows + 1) // KB, full_lo, hi)
    bounds = jnp.stack([lo, full_lo, full_hi, hi])
    starts = starts[None, :]

    x_all = gather_plane(inputs).astype(F32)
    inverse_all = lax.rsqrt(jnp.mean(x_all * x_all, axis=-1, keepdims=True) + eps)
    h_one = (x_all * inverse_all * gain_first).astype(WIDE)
    qkv = dot(h_one, full_a, 1, 0)
    turned = to_columns(qkv, index, cos_tab, sin_tab, GROUP + 1, GROUP + 2)
    q_cols, kv_own = turned[: GROUP * HD], turned[GROUP * HD :]
    kv_cols = jnp.concatenate(
        [shifted(kv_own, distance) for distance in range(reach, 0, -1)] + [kv_own], axis=1
    )
    out_cols, logs = attend(q_cols, kv_cols, starts, bounds)
    attended = to_rows(out_cols, index, cos_tab, sin_tab, 0, GROUP, GROUP * HD)
    input_f32 = inputs.astype(F32)
    inverse_one = lax.rsqrt(jnp.mean(input_f32 * input_f32, axis=-1, keepdims=True) + eps)
    normed_one = input_f32 * inverse_one
    x_mid = input_f32 + sum_plane(dot(attended, full_o, 1, 1))

    inverse_two = lax.rsqrt(jnp.mean(x_mid * x_mid, axis=-1, keepdims=True) + eps)
    normed_two = x_mid * inverse_two
    h_two = gather_plane((normed_two * gain_second).astype(WIDE))
    grad_mix = gather_plane(cotangent)
    gate_pre = dot(h_two, full_g, 1, 0)
    up_pre = dot(h_two, full_u, 1, 0)
    sigmoid_gate = jax.nn.sigmoid(gate_pre)
    hidden = (gate_pre * sigmoid_gate * up_pre).astype(WIDE)
    output = (x_mid + sum_plane(dot(hidden, full_d, 1, 1))).astype(WIDE)

    grad_hidden = dot(grad_mix, full_d, 1, 0)
    grad_gate = (
        grad_hidden * up_pre * sigmoid_gate * (1.0 + gate_pre * (1.0 - sigmoid_gate))
    ).astype(WIDE)
    grad_up = (grad_hidden * gate_pre * sigmoid_gate).astype(WIDE)
    grad_h_two = sum_plane(dot(grad_gate, full_g, 1, 1) + dot(grad_up, full_u, 1, 1))
    down_grad = sum_z(dot(grad_mix, hidden, 0, 0))
    gate_grad = sum_z(dot(h_two, grad_gate, 0, 0))
    up_grad = sum_z(dot(h_two, grad_up, 0, 0))
    grad_mid = cotangent.astype(F32) + norm_back(grad_h_two, normed_two, inverse_two, gain_second)
    grad_branch = gather_plane(grad_mid.astype(WIDE))

    grad_attended = dot(grad_branch, full_o, 1, 0).astype(WIDE)
    out_grad = sum_z(dot(grad_branch, attended, 0, 0))
    grad_cols = to_columns(grad_attended, index, cos_tab, sin_tab, 0, GROUP)
    dq_cols, dkv_cols = attend_back(q_cols, kv_cols, starts, bounds, out_cols, logs, grad_cols)
    dkv_own = dkv_cols[:, reach * count :]
    for distance in range(1, reach + 1):
        first = (reach - distance) * count
        dkv_own = dkv_own + shifted(
            dkv_cols[:, first : first + count].astype(WIDE), -distance
        ).astype(F32)
    grad_qkv = to_rows(
        jnp.concatenate([dq_cols, dkv_own], axis=0),
        index,
        cos_tab,
        sin_tab,
        GROUP + 1,
        GROUP + 2,
        full_a.shape[1],
    )
    grad_h_one = sum_plane(dot(grad_qkv, full_a, 1, 1))
    qkv_grad = sum_z(dot(h_one, grad_qkv, 0, 0))
    input_grad = (grad_mid + norm_back(grad_h_one, normed_one, inverse_one, gain_first)).astype(
        WIDE
    )

    def columns(summed, width):
        one, two = unshare_columns(summed, first_y)
        return jnp.concatenate([one[:, :width], two[:, :width]], axis=1).astype(F32)

    down_out = columns(down_grad, nf).T
    gate_out = columns(gate_grad, nf)
    up_out = columns(up_grad, nf)
    o_out = columns(out_grad, nq).T
    one, two = unshare_columns(qkv_grad, first_y)
    pick = lambda a, b: jnp.concatenate([one[:, a:b], two[:, a:b]], axis=1).astype(F32)
    q_out, k_out, v_out = pick(0, nq), pick(nq, nq + nk), pick(nq + nk, nq + 2 * nk)

    def row_sums(weight, grad):
        return jnp.sum(weight.astype(F32) * grad, axis=1)

    gain_sums = jnp.stack(
        [
            row_sums(w_q, q_out) + row_sums(w_k, k_out) + row_sums(w_v, v_out),
            row_sums(w_g, gate_out) + row_sums(w_u, up_out),
        ]
    )
    gain_sums = gain_sums + lax.ppermute(gain_sums, "x", SWAP)
    gain_sums = gain_sums + lax.ppermute(gain_sums, "c", SWAP)
    gain_one_out = gain_sums[0] / gain_attn.astype(WIDE).astype(F32)
    gain_two_out = gain_sums[1] / gain_mlp.astype(WIDE).astype(F32)
    return (
        output,
        input_grad,
        gain_one_out,
        q_out,
        k_out,
        v_out,
        o_out,
        gain_two_out,
        gate_out,
        up_out,
        down_out,
    )


def solution(mesh):
    seq, tensor = mesh.shape["seq"], mesh.shape["tensor"]
    grid = Mesh(
        mesh.devices.reshape(seq // 2, 2, tensor // 2, 2), ("z", "y", "x", "c")
    )
    rows, cols = ("z", "y"), ("x", "c")
    tokens, weight, weight_t = P(rows + cols, None), P(rows, cols), P(cols, rows)
    in_specs = (
        tokens,
        P(),
        P(rows),
        P(rows),
        weight,
        weight,
        weight,
        weight_t,
        P(rows),
        weight,
        weight,
        weight_t,
        tokens,
    )
    out_specs = (
        tokens,
        tokens,
        P(rows),
        weight,
        weight,
        weight,
        weight_t,
        P(rows),
        weight,
        weight,
        weight_t,
    )
    return jax.shard_map(
        per_device, mesh=grid, in_specs=in_specs, out_specs=out_specs, check_vma=False
    )
```

```python
import functools

import jax
import jax.numpy as jnp
from jax import lax
from jax.experimental import pallas as pl
from jax.experimental.pallas import tpu as pltpu
from jax.sharding import Mesh
from jax.sharding import PartitionSpec as P

HEADS = 32
KV = 8
HD = 80
SEQS = 2
DOC_MOST = 2000
GROUP = HEADS // KV

eps = 1e-05
rope_base = 10000.0
LOG2E = 1.4426950408889634
SCORE_LOG2 = HD ** (-0.5) * LOG2E
SCORE_SCALE = HD ** (-0.5)
LOW = -1e30
BQ = 256
CHUNK = 384
KB = 256
WIDE = jnp.bfloat16
F32 = jnp.float32
VMEM_BYTES = 48 * 1024 * 1024

SWAP = [(0, 1), (1, 0)]


def dot(a, b, ca, cb):
    return lax.dot_general(a, b, (((ca,), (cb,)), ((), ())), preferred_element_type=F32)


def turn_kernel(rotary, heads, index_ref, rows_ref, cos_ref, sin_ref, out_ref):
    own = rows_ref.shape[0] // 8
    half = HD // 2
    for pair in range(4):
        parts = [
            rows_ref[pl.ds(pl.multiple_of(index_ref[2 * pair + k] * own, own), own), :].astype(F32)
            for k in range(2)
        ]
        turned = jnp.concatenate(parts, axis=0).T
        lanes = slice(pair * 2 * own, (pair + 1) * 2 * own)
        cos_tab, sin_tab = cos_ref[:, lanes], sin_ref[:, lanes]
        for h in range(heads):
            front, back = turned[h * HD : h * HD + half], turned[h * HD + half : (h + 1) * HD]
            if h < rotary:
                front, back = front * cos_tab - back * sin_tab, back * cos_tab + front * sin_tab
            out_ref[h * HD : (h + 1) * HD, lanes] = jnp.concatenate([front, back], axis=0).astype(
                out_ref.dtype
            )


def to_columns(rows, index, cos_tab, sin_tab, rotary, heads):
    count = rows.shape[0]
    full = lambda shape: pl.BlockSpec(shape, lambda i, s: (0, 0))
    return pl.pallas_call(
        functools.partial(turn_kernel, rotary, heads),
        grid_spec=pltpu.PrefetchScalarGridSpec(
            num_scalar_prefetch=1,
            grid=(1,),
            in_specs=[full(rows.shape), full(cos_tab.shape), full(sin_tab.shape)],
            out_specs=full((heads * HD, count)),
        ),
        out_shape=jax.ShapeDtypeStruct((heads * HD, count), WIDE),
        compiler_params=pltpu.CompilerParams(vmem_limit_bytes=VMEM_BYTES),
        cost_estimate=pl.CostEstimate(flops=10**6, bytes_accessed=10**5, transcendentals=0),
    )(index, rows, cos_tab, sin_tab)


def back_kernel(rotary, heads, index_ref, cols_ref, cos_ref, sin_ref, out_ref):
    own = cols_ref.shape[1] // 8
    half = HD // 2
    width = out_ref.shape[1]
    for pair in range(4):
        lanes = slice(pair * 2 * own, (pair + 1) * 2 * own)
        cos_tab, sin_tab = cos_ref[:, lanes], sin_ref[:, lanes]
        parts = []
        for h in range(heads):
            front = cols_ref[h * HD : h * HD + half, lanes].astype(F32)
            back = cols_ref[h * HD + half : (h + 1) * HD, lanes].astype(F32)
            if h < rotary:
                front, back = front * cos_tab + back * sin_tab, back * cos_tab - front * sin_tab
            parts += [front, back]
        if width > heads * HD:
            parts.append(jnp.zeros((width - heads * HD, 2 * own), F32))
        rows = jnp.concatenate(parts, axis=0).T.astype(out_ref.dtype)
        for k in range(2):
            first = pl.multiple_of(index_ref[2 * pair + k] * own, own)
            out_ref[pl.ds(first, own), :] = rows[k * own : (k + 1) * own]


def to_rows(cols, index, cos_tab, sin_tab, rotary, heads, width):
    count = cols.shape[1]
    full = lambda shape: pl.BlockSpec(shape, lambda i, s: (0, 0))
    return pl.pallas_call(
        functools.partial(back_kernel, rotary, heads),
        grid_spec=pltpu.PrefetchScalarGridSpec(
            num_scalar_prefetch=1,
            grid=(1,),
            in_specs=[full(cols.shape), full(cos_tab.shape), full(sin_tab.shape)],
            out_specs=full((count, width)),
        ),
        out_shape=jax.ShapeDtypeStruct((count, width), WIDE),
        compiler_params=pltpu.CompilerParams(vmem_limit_bytes=VMEM_BYTES),
        cost_estimate=pl.CostEstimate(flops=10**6, bytes_accessed=10**5, transcendentals=0),
    )(index, cols, cos_tab, sin_tab)


def allowed_mask(block, starts, own_places):
    places = block * KB + lax.broadcasted_iota(jnp.int32, (KB, 1), 0)
    return (places >= starts) & (places <= own_places)


def attend_kernel(span_before, bounds_ref, q_ref, kv_ref, start_ref, out_ref, log_ref, k_rows, acc):
    step = pl.program_id(0)
    span = kv_ref.shape[1]

    @pl.when(step == 0)
    def _():
        for j in range(span // KB):
            k_rows[j * KB : (j + 1) * KB, :] = (
                kv_ref[0:HD, j * KB : (j + 1) * KB].astype(F32).T.astype(WIDE)
            )

    starts = start_ref[0:1, :]
    own_places = span_before + step * BQ + lax.broadcasted_iota(jnp.int32, (1, BQ), 1)
    acc[...] = jnp.zeros_like(acc)

    def one(masked, block, carry):
        first = pl.multiple_of(block * KB, KB)
        keys = k_rows[pl.ds(first, KB), :]
        values = kv_ref[HD : 2 * HD, pl.ds(first, KB)]
        if masked:
            mask = allowed_mask(block, starts, own_places)
        fresh = []
        for h in range(GROUP):
            top, total = carry[2 * h], carry[2 * h + 1]
            scores = dot(keys, q_ref[h * HD : (h + 1) * HD, :], 1, 0) * SCORE_LOG2
            if masked:
                scores = jnp.where(mask, scores, LOW)
            new_top = jnp.maximum(top, jnp.max(scores, axis=0, keepdims=True))
            probs = jnp.exp2(scores - new_top)
            fade = jnp.exp2(top - new_top)
            total = fade * total + jnp.sum(probs, axis=0, keepdims=True)
            acc[h] = fade * acc[h] + dot(values, probs.astype(WIDE), 1, 0)
            fresh += [new_top, total]
        return tuple(fresh)

    carry = (jnp.full((1, BQ), LOW, F32), jnp.zeros((1, BQ), F32)) * GROUP
    lo, full_lo, full_hi, hi = [bounds_ref[k, step] for k in range(4)]
    carry = lax.fori_loop(lo, full_lo, functools.partial(one, True), carry)
    carry = lax.fori_loop(full_lo, full_hi, functools.partial(one, False), carry)
    carry = lax.fori_loop(full_hi, hi, functools.partial(one, True), carry)
    for h in range(GROUP):
        top, total = carry[2 * h], carry[2 * h + 1]
        out_ref[h * HD : (h + 1) * HD, :] = (acc[h] / total).astype(WIDE)
        log_ref[h : h + 1, :] = top + jnp.log2(total)


def attend(q_cols, kv_cols, starts, bounds):
    count, span = q_cols.shape[1], kv_cols.shape[1]
    return pl.pallas_call(
        functools.partial(attend_kernel, span - count),
        grid_spec=pltpu.PrefetchScalarGridSpec(
            num_scalar_prefetch=1,
            grid=(count // BQ,),
            in_specs=[
                pl.BlockSpec((GROUP * HD, BQ), lambda i, s: (0, i)),
                pl.BlockSpec((2 * HD, span), lambda i, s: (0, 0)),
                pl.BlockSpec((1, BQ), lambda i, s: (0, i)),
            ],
            out_specs=[
                pl.BlockSpec((GROUP * HD, BQ), lambda i, s: (0, i)),
                pl.BlockSpec((8, BQ), lambda i, s: (0, i)),
            ],
            scratch_shapes=[pltpu.VMEM((span, HD), WIDE), pltpu.VMEM((GROUP, HD, BQ), F32)],
        ),
        out_shape=[
            jax.ShapeDtypeStruct((GROUP * HD, count), WIDE),
            jax.ShapeDtypeStruct((8, count), F32),
        ],
        compiler_params=pltpu.CompilerParams(vmem_limit_bytes=VMEM_BYTES),
        cost_estimate=pl.CostEstimate(flops=10**6, bytes_accessed=10**5, transcendentals=0),
    )(bounds, q_cols, kv_cols, starts)


def attend_back_kernel(
    span_before,
    bounds_ref,
    q_ref,
    kv_ref,
    start_ref,
    out_ref,
    log_ref,
    grad_ref,
    dq_ref,
    dkv_ref,
    k_rows,
    v_rows,
    q_rows,
    g_rows,
    dk,
    dv,
    probs_all,
    grads_all,
    dq,
):
    step = pl.program_id(0)
    span = kv_ref.shape[1]

    @pl.when(step == 0)
    def _():
        for j in range(span // KB):
            lanes = slice(j * KB, (j + 1) * KB)
            k_rows[lanes, :] = kv_ref[0:HD, lanes].astype(F32).T.astype(WIDE)
            v_rows[lanes, :] = kv_ref[HD : 2 * HD, lanes].astype(F32).T.astype(WIDE)
        dk[...] = jnp.zeros_like(dk)
        dv[...] = jnp.zeros_like(dv)

    starts = start_ref[0:1, :]
    own_places = span_before + step * BQ + lax.broadcasted_iota(jnp.int32, (1, BQ), 1)
    dq[...] = jnp.zeros_like(dq)
    deltas = []
    for h in range(GROUP):
        part = slice(h * HD, (h + 1) * HD)
        q_f32, g_f32 = q_ref[part, :].astype(F32), grad_ref[part, :].astype(F32)
        q_rows[h * BQ : (h + 1) * BQ, :] = q_f32.T.astype(WIDE)
        g_rows[h * BQ : (h + 1) * BQ, :] = g_f32.T.astype(WIDE)
        deltas.append(jnp.sum(g_f32 * out_ref[part, :].astype(F32), axis=0, keepdims=True))

    def one(masked, block, carry):
        first = pl.multiple_of(block * KB, KB)
        rows = pl.ds(first, KB)
        keys, values = k_rows[rows, :], v_rows[rows, :]
        key_cols = kv_ref[0:HD, rows]
        if masked:
            mask = allowed_mask(block, starts, own_places)
        for h in range(GROUP):
            part = slice(h * HD, (h + 1) * HD)
            lanes = slice(h * BQ, (h + 1) * BQ)
            scores = dot(keys, q_ref[part, :], 1, 0) * SCORE_LOG2 - log_ref[h : h + 1, :]
            if masked:
                scores = jnp.where(mask, scores, LOW)
            probs = jnp.exp2(scores)
            grad_probs = dot(values, grad_ref[part, :], 1, 0)
            grad_scores = (probs * (grad_probs - deltas[h])).astype(WIDE)
            probs_all[:, lanes] = probs.astype(WIDE)
            grads_all[:, lanes] = grad_scores
            dq[h] += dot(key_cols, grad_scores, 1, 0)
        dv[rows, :] += dot(probs_all[...], g_rows[...], 1, 0)
        dk[rows, :] += dot(grads_all[...], q_rows[...], 1, 0)
        return carry

    lo, full_lo, full_hi, hi = [bounds_ref[k, step] for k in range(4)]
    lax.fori_loop(lo, full_lo, functools.partial(one, True), 0)
    lax.fori_loop(full_lo, full_hi, functools.partial(one, False), 0)
    lax.fori_loop(full_hi, hi, functools.partial(one, True), 0)
    for h in range(GROUP):
        dq_ref[h * HD : (h + 1) * HD, :] = dq[h] * SCORE_SCALE

    @pl.when(step == pl.num_programs(0) - 1)
    def _():
        for j in range(span // KB):
            lanes = slice(j * KB, (j + 1) * KB)
            dkv_ref[0:HD, lanes] = dk[lanes, :].T * SCORE_SCALE
            dkv_ref[HD : 2 * HD, lanes] = dv[lanes, :].T


def attend_back(q_cols, kv_cols, starts, bounds, out_cols, logs, grad_cols):
    count, span = q_cols.shape[1], kv_cols.shape[1]
    wide_block = pl.BlockSpec((GROUP * HD, BQ), lambda i, s: (0, i))
    return pl.pallas_call(
        functools.partial(attend_back_kernel, span - count),
        grid_spec=pltpu.PrefetchScalarGridSpec(
            num_scalar_prefetch=1,
            grid=(count // BQ,),
            in_specs=[
                wide_block,
                pl.BlockSpec((2 * HD, span), lambda i, s: (0, 0)),
                pl.BlockSpec((1, BQ), lambda i, s: (0, i)),
                wide_block,
                pl.BlockSpec((8, BQ), lambda i, s: (0, i)),
                wide_block,
            ],
            out_specs=[wide_block, pl.BlockSpec((2 * HD, span), lambda i, s: (0, 0))],
            scratch_shapes=[
                pltpu.VMEM((span, HD), WIDE),
                pltpu.VMEM((span, HD), WIDE),
                pltpu.VMEM((GROUP * BQ, HD), WIDE),
                pltpu.VMEM((GROUP * BQ, HD), WIDE),
                pltpu.VMEM((span, HD), F32),
                pltpu.VMEM((span, HD), F32),
                pltpu.VMEM((KB, GROUP * BQ), WIDE),
                pltpu.VMEM((KB, GROUP * BQ), WIDE),
                pltpu.VMEM((GROUP, HD, BQ), F32),
            ],
        ),
        out_shape=[
            jax.ShapeDtypeStruct((GROUP * HD, count), F32),
            jax.ShapeDtypeStruct((2 * HD, span), F32),
        ],
        compiler_params=pltpu.CompilerParams(vmem_limit_bytes=VMEM_BYTES),
        cost_estimate=pl.CostEstimate(flops=10**6, bytes_accessed=10**5, transcendentals=0),
    )(bounds, q_cols, kv_cols, starts, out_cols, logs, grad_cols)


def project_kernel(x_ref, gain_ref, weight_ref, h_ref, out_ref):
    x = x_ref[...].astype(F32)
    inverse = lax.rsqrt(jnp.mean(x * x, axis=-1, keepdims=True) + eps)
    h = (x * inverse * gain_ref[...]).astype(WIDE)
    h_ref[...] = h
    out_ref[...] = dot(h, weight_ref[...], 1, 0)


def project(x_all, gain_row, weights, rows=256):
    count, model = x_all.shape
    width = weights.shape[1]
    return pl.pallas_call(
        project_kernel,
        grid=(count // rows,),
        in_specs=[
            pl.BlockSpec((rows, model), lambda i: (i, 0)),
            pl.BlockSpec((1, model), lambda i: (0, 0)),
            pl.BlockSpec(weights.shape, lambda i: (0, 0), pipeline_mode=pl.Buffered(1)),
        ],
        out_specs=[
            pl.BlockSpec((rows, model), lambda i: (i, 0)),
            pl.BlockSpec((rows, width), lambda i: (i, 0)),
        ],
        out_shape=[
            jax.ShapeDtypeStruct((count, model), WIDE),
            jax.ShapeDtypeStruct((count, width), F32),
        ],
        compiler_params=pltpu.CompilerParams(vmem_limit_bytes=VMEM_BYTES),
        cost_estimate=pl.CostEstimate(flops=10**6, bytes_accessed=10**5, transcendentals=0),
    )(x_all, gain_row, weights)


def hidden_kernel(h_ref, cot_ref, weight_ref, out_ref):
    width = weight_ref.shape[1] // 3
    gate = dot(h_ref[...], weight_ref[:, width : 2 * width], 1, 0)
    up = dot(h_ref[...], weight_ref[:, 2 * width :], 1, 0)
    grad = dot(cot_ref[...], weight_ref[:, :width], 1, 0)
    sigma = 1.0 / (1.0 + jnp.exp(-gate))
    silu = gate * sigma
    out_ref[:, :width] = (silu * up).astype(WIDE)
    out_ref[:, width : 2 * width] = (grad * up * sigma * (1.0 + gate * (1.0 - sigma))).astype(WIDE)
    out_ref[:, 2 * width :] = (grad * silu).astype(WIDE)


def hidden_units(h_two, cot, weights, rows=256):
    count, model = h_two.shape
    return pl.pallas_call(
        hidden_kernel,
        grid=(count // rows,),
        in_specs=[
            pl.BlockSpec((rows, model), lambda i: (i, 0)),
            pl.BlockSpec((rows, model), lambda i: (i, 0)),
            pl.BlockSpec(weights.shape, lambda i: (0, 0), pipeline_mode=pl.Buffered(1)),
        ],
        out_specs=pl.BlockSpec((rows, weights.shape[1]), lambda i: (i, 0)),
        out_shape=jax.ShapeDtypeStruct((count, weights.shape[1]), WIDE),
        compiler_params=pltpu.CompilerParams(vmem_limit_bytes=VMEM_BYTES),
        cost_estimate=pl.CostEstimate(flops=10**6, bytes_accessed=10**5, transcendentals=0),
    )(h_two, cot, weights)


def rows_kernel(spans, has_prior, *refs):
    out_ref = refs[-1]
    total = refs[-2][...].astype(F32) if has_prior else None
    for k, (lo, hi) in enumerate(spans):
        part = dot(refs[2 * k][:, lo:hi], refs[2 * k + 1][:, lo:hi], 1, 1)
        total = part if total is None else total + part
    out_ref[...] = total.astype(out_ref.dtype)


def row_products(pairs, spans, first, count, prior=None, rows=256):
    model = pairs[0][1].shape[0]
    at = first // rows
    operands, specs = [], []
    for a, b in pairs:
        operands += [a, b]
        specs += [
            pl.BlockSpec((rows, a.shape[1]), lambda i: (i + at, 0)),
            pl.BlockSpec(b.shape, lambda i: (0, 0), pipeline_mode=pl.Buffered(1)),
        ]
    if prior is not None:
        operands.append(prior)
        specs.append(pl.BlockSpec((rows, model), lambda i: (i, 0)))
    return pl.pallas_call(
        functools.partial(rows_kernel, spans, prior is not None),
        grid=(count // rows,),
        in_specs=specs,
        out_specs=pl.BlockSpec((rows, model), lambda i: (i, 0)),
        out_shape=jax.ShapeDtypeStruct((count, model), WIDE),
        compiler_params=pltpu.CompilerParams(vmem_limit_bytes=VMEM_BYTES),
        cost_estimate=pl.CostEstimate(flops=10**6, bytes_accessed=10**5, transcendentals=0),
    )(*operands)


def grads_kernel(spans, *refs):
    out_ref = refs[-1]
    for k, (lo, hi, at) in enumerate(spans):
        out_ref[:, at : at + hi - lo] = dot(refs[2 * k][...], refs[2 * k + 1][:, lo:hi], 0, 0).astype(
            WIDE
        )
    end = max(at + hi - lo for lo, hi, at in spans)
    if end < out_ref.shape[1]:
        out_ref[:, end:] = jnp.zeros((out_ref.shape[0], out_ref.shape[1] - end), WIDE)


def column_products(pairs, spans, width, rows=256):
    count, model = pairs[0][0].shape
    operands, specs = [], []
    for a, b in pairs:
        operands += [a, b]
        specs += [
            pl.BlockSpec((count, rows), lambda i: (0, i)),
            pl.BlockSpec(b.shape, lambda i: (0, 0), pipeline_mode=pl.Buffered(1)),
        ]
    return pl.pallas_call(
        functools.partial(grads_kernel, spans),
        grid=(model // rows,),
        in_specs=specs,
        out_specs=pl.BlockSpec((rows, width), lambda i: (i, 0)),
        out_shape=jax.ShapeDtypeStruct((model, width), WIDE),
        compiler_params=pltpu.CompilerParams(vmem_limit_bytes=VMEM_BYTES),
        cost_estimate=pl.CostEstimate(flops=10**6, bytes_accessed=10**5, transcendentals=0),
    )(*operands)


def hidden_grads(h_two, cot, acts):
    width = acts.shape[1] // 3
    return column_products(
        [(cot, acts), (h_two, acts)],
        [(0, width, 0), (width, 3 * width, width)],
        3 * width,
    )


def tied(value, *others):
    return lax.optimization_barrier((value, *others))[0]


def together(*values):
    return lax.optimization_barrier(values)


def shifted(block, distance, period):
    count = lax.axis_size("z")
    route = [
        (i - distance, i)
        for i in range(count)
        if 0 <= i - distance < count and (i - distance) // period == i // period
    ]
    return lax.ppermute(block, "z", route)


def over(block, axis):
    return lax.ppermute(block, axis, SWAP)


def across(block):
    return lax.ppermute(block, ("y", "x"), [(i, 3 - i) for i in range(4)])


def plane_step_one(block):
    return over(block, "x"), over(block, "y")


def plane_step_two(over_x, over_y):
    half = over_x.shape[0] // 2
    return over(over_y[:half], "x"), over(over_x[half:], "y")


def plane_join(*mine):
    return jnp.concatenate(list(mine) + [over(part, "c") for part in mine], axis=0)


def core_sum(own, term, prior=None):
    half = 4 * own
    got = over(term(half, half).astype(WIDE), "c")
    mine = term(0, half)
    return (mine.astype(F32) + got.astype(F32)).astype(WIDE)


def product(a, b):
    return lambda first, count: dot(a[first : first + count], b, 1, 1)


def plane_sum_one(total):
    own = total.shape[0] // 4
    half = own // 2
    return over(total[3 * own : 3 * own + half], "x"), over(total[3 * own + half :], "y")


def plane_sum_two(total, top, bottom):
    own = total.shape[0] // 4
    half = own // 2
    wide = lambda a, b: (a.astype(F32) + b.astype(F32)).astype(WIDE)
    to_x = jnp.concatenate(
        [total[own : own + half], wide(total[own + half : 2 * own], bottom)], axis=0
    )
    to_y = jnp.concatenate(
        [wide(total[2 * own : 2 * own + half], top), total[2 * own + half : 3 * own]], axis=0
    )
    return over(to_x, "x"), over(to_y, "y")


def added(total, *parts):
    own = total.shape[0] // 4
    return sum((part.astype(F32) for part in parts), total[:own].astype(F32))


def kept_columns(block, first_y):
    half = block.shape[1] // 2
    keep = jnp.where(first_y, block[:, :half], block[:, half:])
    give = jnp.where(first_y, block[:, half:], block[:, :half])
    return keep, give


def both_rows(keep, got, first_y):
    return jnp.concatenate([jnp.where(first_y, keep, got), jnp.where(first_y, got, keep)], axis=0)


def share_columns(block, first_y, *after):
    keep, give = kept_columns(block, first_y)
    if after:
        give = tied(give, *after)
    return both_rows(keep, over(give, "y"), first_y)


def unshare_columns(block, first_y):
    half = block.shape[0] // 2
    keep = jnp.where(first_y, block[:half], block[half:])
    give = jnp.where(first_y, block[half:], block[:half])
    got = over(give, "y")
    return jnp.where(first_y, keep, got), jnp.where(first_y, got, keep)


def gather_z(block):
    return lax.all_gather(block, "z", axis=0, tiled=True)


def sum_z(block):
    return lax.psum_scatter(block.astype(WIDE), "z", scatter_dimension=0, tiled=True)


def padded(block, multiple=128):
    extra = -block.shape[1] % multiple
    return jnp.pad(block, ((0, 0), (0, extra))) if extra else block


def norm_back(gradient, normed, inverse, gain_vec):
    scaled = gradient * gain_vec
    return inverse * (scaled - normed * jnp.mean(scaled * normed, axis=-1, keepdims=True))


def per_device(
    inputs,
    segments,
    positions,
    gain_attn,
    query_weight,
    key_weight,
    value_weight,
    out_weight,
    gain_mlp,
    gate_weight,
    up_weight,
    down_weight,
    cotangent,
):
    own = inputs.shape[0]
    count = 8 * own
    length = segments.shape[0] // SEQS
    reach = (DOC_MOST - 2) // count + 1
    period = lax.axis_size("z")
    if length % count == 0:
        period = length // count
        reach = min(reach, period - 1)
    span = (reach + 1) * count
    z, y = lax.axis_index("z"), lax.axis_index("y")
    x, c = lax.axis_index("x"), lax.axis_index("c")
    first_y = y == 0

    w_q, w_k, w_v, w_g, w_u = [
        w.astype(WIDE) for w in (query_weight, key_weight, value_weight, gate_weight, up_weight)
    ]
    w_o, w_d = out_weight.T.astype(WIDE), down_weight.T.astype(WIDE)
    nq, nk, nf = w_q.shape[1] // 2, w_k.shape[1] // 2, w_g.shape[1] // 2
    rows_w = w_q.shape[0]
    halves = lambda w: (w[:, : w.shape[1] // 2], w[:, w.shape[1] // 2 :])
    gain_pair = jnp.stack([gain_attn, gain_mlp] * 2, 1).astype(WIDE)
    near_a = share_columns(
        jnp.concatenate(
            [
                padded(jnp.concatenate([halves(w)[i] for w in (w_q, w_k, w_v, gain_pair)], axis=1))
                for i in range(2)
            ],
            axis=1,
        ),
        first_y,
    )
    chunks = (slice(0, CHUNK), slice(CHUNK, nf))
    triple = lambda cut: jnp.concatenate(
        [padded(halves(w)[i][:, cut]) for i in range(2) for w in (w_d, w_g, w_u)], axis=1
    )
    x_parts = over(inputs, "x"), over(tied(inputs, near_a), "y")
    x_parts += plane_step_two(*x_parts)
    x_all = plane_join(inputs, *x_parts)
    cot_parts = plane_step_one(tied(cotangent, *x_parts))
    near_o = share_columns(w_o, first_y, *x_parts)
    near_c = [share_columns(triple(cut), first_y, *x_parts) for cut in chunks]
    full_a, full_o = gather_z(near_a), gather_z(near_o)
    full_c = [gather_z(near) for near in near_c]
    first_gain = nq + 2 * nk
    gains = full_a[:, first_gain : first_gain + 2].astype(F32)
    gain_first, gain_second = gains[:, 0], gains[:, 1]

    other_positions = lax.ppermute(positions, "y", SWAP)
    token_positions = jnp.where(
        first_y,
        jnp.concatenate([positions, other_positions]),
        jnp.concatenate([other_positions, positions]),
    )
    frequency = rope_base ** (-(jnp.arange(HD // 2, dtype=F32) * 2.0 / HD))
    angles = frequency[:, None] * token_positions.astype(F32)[None, :]
    cos_tab, sin_tab = jnp.cos(angles), jnp.sin(angles)
    places = jnp.arange(8, dtype=jnp.int32)
    flips = places ^ (y * 4 + x * 2 + c).astype(jnp.int32)
    index = (flips % 2) * 4 + flips // 2
    padded_segs = jnp.concatenate([jnp.full((reach * count,), -1, jnp.int32), segments])
    key_segs = lax.dynamic_slice_in_dim(padded_segs, z * count, span, 0)
    query_segs = lax.dynamic_slice_in_dim(segments, z * count, count, 0)
    starts = jnp.sum((key_segs[:, None] < query_segs[None, :]).astype(jnp.int32), axis=0)
    first_rows = jnp.arange(count // BQ, dtype=jnp.int32) * BQ
    lo = starts[first_rows] // KB
    hi = (reach * count + first_rows + BQ + KB - 1) // KB
    full_lo = jnp.clip((starts[first_rows + BQ - 1] + KB - 1) // KB, lo, hi)
    full_hi = jnp.clip((reach * count + first_rows + 1) // KB, full_lo, hi)
    bounds = jnp.stack([lo, full_lo, full_hi, hi])
    starts = starts[None, :]

    h_one, qkv = project(x_all, gain_first[None, :], full_a)
    turned = to_columns(qkv, index, cos_tab, sin_tab, GROUP + 1, GROUP + 2)
    q_cols, kv_own = turned[: GROUP * HD], turned[GROUP * HD :]
    far_kv = [shifted(kv_own, distance, period) for distance in range(reach, 0, -1)]
    kv_cols = jnp.concatenate(far_kv + [kv_own], axis=1)
    kv_cols, full_o, *near_all = together(kv_cols, full_o, *near_c, *cot_parts)
    cot_parts = near_all[len(near_c) :]
    cot_far = plane_step_two(*cot_parts)
    out_cols, logs = attend(q_cols, kv_cols, starts, bounds)
    out_cols, *cot_far = together(out_cols, *cot_far)
    attended = to_rows(out_cols, index, cos_tab, sin_tab, 0, GROUP, GROUP * HD)
    grad_mix = plane_join(cotangent, *cot_parts, *cot_far)
    input_f32 = inputs.astype(F32)
    inverse_one = lax.rsqrt(jnp.mean(input_f32 * input_f32, axis=-1, keepdims=True) + eps)
    normed_one = input_f32 * inverse_one
    mid_total = core_sum(own, product(attended, full_o))
    mid_far = plane_sum_one(mid_total)
    mid_near = plane_sum_two(mid_total, *mid_far)
    x_mid = input_f32 + added(mid_total, *mid_near)

    inverse_two = lax.rsqrt(jnp.mean(x_mid * x_mid, axis=-1, keepdims=True) + eps)
    normed_two = x_mid * inverse_two
    h_own = (normed_two * gain_second).astype(WIDE)
    h_parts = plane_step_one(h_own)
    h_parts += plane_step_two(*h_parts)
    h_two, grad_mix = together(plane_join(h_own, *h_parts), grad_mix)
    half = 4 * own
    acts = [hidden_units(h_two, grad_mix, full_c[0])]
    width = [full.shape[1] // 3 for full in full_c]
    later = lambda k: (width[k], 3 * width[k])
    back_other = row_products([(acts[0], full_c[0])], [later(0)], half, half)
    back_mine = row_products([(acts[0], full_c[0])], [later(0)], 0, half)
    grads = [hidden_grads(h_two, grad_mix, acts[0])]
    full_c[1], back_mine, back_other, *grads = together(full_c[1], back_mine, back_other, *grads)
    sums = [sum_z(grads[0])]
    acts.append(hidden_units(h_two, grad_mix, full_c[1]))
    back_other = row_products([(acts[1], full_c[1])], [later(1)], half, half, back_other)
    got = over(back_other, "c")
    back_mine = row_products([(acts[1], full_c[1])], [later(1)], 0, half, back_mine)
    back_total = (back_mine.astype(F32) + got.astype(F32)).astype(WIDE)
    back_far = plane_sum_one(back_total)
    grads.append(hidden_grads(h_two, grad_mix, acts[1]))
    back_near = plane_sum_two(back_total, *back_far)
    *back_near, grads[1] = together(*back_near, grads[1])
    sums.append(sum_z(grads[1]))
    grad_h_two = added(back_total, *back_near)
    grad_mid = cotangent.astype(F32) + norm_back(grad_h_two, normed_two, inverse_two, gain_second)
    branch_own = grad_mid.astype(WIDE)
    branch_parts = plane_step_one(branch_own)
    acts_later = [tied(part, branch_own) for part in acts]
    hidden_pairs = list(zip(acts_later, full_c))
    out_other = row_products(hidden_pairs, [(0, w) for w in width], half, half)
    *branch_parts, out_other = together(*branch_parts, out_other)
    out_got = over(out_other, "c")
    branch_far = plane_step_two(*branch_parts)
    hidden_pairs = [(tied(part, *branch_parts), full) for part, full in zip(acts, full_c)]
    out_mine = row_products(hidden_pairs, [(0, w) for w in width], 0, half)
    *branch_far, out_mine, out_got = together(*branch_far, out_mine, out_got)
    out_total = (out_mine.astype(F32) + out_got.astype(F32)).astype(WIDE)
    grad_branch = plane_join(branch_own, *branch_parts, *branch_far)
    grad_branch, out_total, sums[0] = together(grad_branch, out_total, sums[0])

    grad_attended = dot(grad_branch, full_o, 1, 0).astype(WIDE)
    grad_cols = to_columns(grad_attended, index, cos_tab, sin_tab, 0, GROUP)
    out_total, sums[0] = together(out_total, sums[0], grad_cols)[:2]
    out_sends = [
        over(out_total[own : 2 * own], "x"),
        over(out_total[2 * own : 3 * own], "y"),
        across(out_total[3 * own :]),
    ]
    owned = [unshare_columns(sums[0], first_y)]
    dq_cols, dkv_cols = attend_back(q_cols, kv_cols, starts, bounds, out_cols, logs, grad_cols)
    dkv_own = dkv_cols[:, reach * count :]
    for distance in range(1, reach + 1):
        first = (reach - distance) * count
        dkv_own = dkv_own + shifted(
            dkv_cols[:, first : first + count].astype(WIDE), -distance, period
        ).astype(F32)
    grad_qkv = to_rows(
        jnp.concatenate([dq_cols, dkv_own], axis=0),
        index,
        cos_tab,
        sin_tab,
        GROUP + 1,
        GROUP + 2,
        full_a.shape[1],
    )
    qkv_part = column_products([(h_one, grad_qkv)], [(0, full_a.shape[1], 0)], full_a.shape[1])
    grad_qkv, qkv_part = together(grad_qkv, qkv_part)
    one_total = core_sum(own, product(grad_qkv, full_a))
    one_total, qkv_part, sums[1] = together(one_total, qkv_part, sums[1])
    qkv_grad = sum_z(qkv_part)
    one_far = plane_sum_one(one_total)
    out_part = column_products([(grad_branch, tied(attended, qkv_part))], [(0, nq, 0)], nq)
    *one_far, to_x, to_y, to_xy = together(*one_far, *out_sends)
    out_sends = to_x, to_y, to_xy
    output = (x_mid + added(out_total, *out_sends)).astype(WIDE)
    one_near = plane_sum_two(one_total, *one_far)
    *one_near, qkv_grad, out_part = together(*one_near, qkv_grad, out_part)
    out_grad = sum_z(out_part)
    grad_h_one = added(one_total, *one_near)
    input_grad = (grad_mid + norm_back(grad_h_one, normed_one, inverse_one, gain_first)).astype(
        WIDE
    )

    owned.append(unshare_columns(sums[1], first_y))
    kept = [CHUNK, nf - CHUNK]

    def unit_columns(k):
        return jnp.concatenate(
            [
                owned[j][i][:, k * width[j] : k * width[j] + kept[j]]
                for i in range(2)
                for j in range(2)
            ],
            axis=1,
        ).astype(F32)

    down_out, gate_out, up_out = unit_columns(0).T, unit_columns(1), unit_columns(2)
    one, two = unshare_columns(qkv_grad, first_y)
    pick = lambda a, b: jnp.concatenate([one[:, a:b], two[:, a:b]], axis=1).astype(F32)
    q_out, k_out, v_out = pick(0, nq), pick(nq, nq + nk), pick(nq + nk, nq + 2 * nk)
    o_out = jnp.concatenate(unshare_columns(out_grad, first_y), axis=1).T.astype(F32)

    def row_sums(weight, grad):
        return jnp.sum(weight.astype(F32) * grad, axis=1)

    gain_sums = jnp.stack(
        [
            row_sums(w_q, q_out) + row_sums(w_k, k_out) + row_sums(w_v, v_out),
            row_sums(w_g, gate_out) + row_sums(w_u, up_out),
        ]
    )
    gain_sums = gain_sums + lax.ppermute(gain_sums, "x", SWAP)
    gain_sums = gain_sums + lax.ppermute(gain_sums, "c", SWAP)
    gain_one_out = gain_sums[0] / gain_attn.astype(WIDE).astype(F32)
    gain_two_out = gain_sums[1] / gain_mlp.astype(WIDE).astype(F32)
    return (
        output,
        input_grad,
        gain_one_out,
        q_out,
        k_out,
        v_out,
        o_out,
        gain_two_out,
        gate_out,
        up_out,
        down_out,
    )


def solution(mesh):
    seq, tensor = mesh.shape["seq"], mesh.shape["tensor"]
    grid = Mesh(
        mesh.devices.reshape(seq // 2, 2, tensor // 2, 2), ("z", "y", "x", "c")
    )
    rows, cols = ("z", "y"), ("x", "c")
    tokens, weight, weight_t = P(rows + cols, None), P(rows, cols), P(cols, rows)
    in_specs = (
        tokens,
        P(),
        P(rows),
        P(rows),
        weight,
        weight,
        weight,
        weight_t,
        P(rows),
        weight,
        weight,
        weight_t,
        tokens,
    )
    out_specs = (
        tokens,
        tokens,
        P(rows),
        weight,
        weight,
        weight,
        weight_t,
        P(rows),
        weight,
        weight,
        weight_t,
    )
    return jax.shard_map(
        per_device, mesh=grid, in_specs=in_specs, out_specs=out_specs, check_vma=False
    )
```

```python
import functools

import jax
import jax.numpy as jnp
from jax import lax
from jax.experimental import pallas as pl
from jax.experimental.pallas import tpu as pltpu
from jax.sharding import Mesh
from jax.sharding import PartitionSpec as P

HEADS = 32
KV = 8
HD = 80
SEQS = 2
DOC_MOST = 2000
GROUP = HEADS // KV

eps = 1e-05
rope_base = 10000.0
LOG2E = 1.4426950408889634
SCORE_LOG2 = HD ** (-0.5) * LOG2E
SCORE_SCALE = HD ** (-0.5)
LOW = -1e30
BQ = 256
CHUNK = 384
KB = 256
WIDE = jnp.bfloat16
F32 = jnp.float32
VMEM_BYTES = 48 * 1024 * 1024

SWAP = [(0, 1), (1, 0)]


def dot(a, b, ca, cb):
    return lax.dot_general(a, b, (((ca,), (cb,)), ((), ())), preferred_element_type=F32)


def turn_kernel(rotary, heads, index_ref, rows_ref, cos_ref, sin_ref, out_ref):
    own = rows_ref.shape[0] // 8
    half = HD // 2
    for pair in range(4):
        parts = [
            rows_ref[pl.ds(pl.multiple_of(index_ref[2 * pair + k] * own, own), own), :].astype(F32)
            for k in range(2)
        ]
        turned = jnp.concatenate(parts, axis=0).T
        lanes = slice(pair * 2 * own, (pair + 1) * 2 * own)
        cos_tab, sin_tab = cos_ref[:, lanes], sin_ref[:, lanes]
        for h in range(heads):
            front, back = turned[h * HD : h * HD + half], turned[h * HD + half : (h + 1) * HD]
            if h < rotary:
                front, back = front * cos_tab - back * sin_tab, back * cos_tab + front * sin_tab
            out_ref[h * HD : (h + 1) * HD, lanes] = jnp.concatenate([front, back], axis=0).astype(
                out_ref.dtype
            )


def to_columns(rows, index, cos_tab, sin_tab, rotary, heads):
    count = rows.shape[0]
    full = lambda shape: pl.BlockSpec(shape, lambda i, s: (0, 0))
    return pl.pallas_call(
        functools.partial(turn_kernel, rotary, heads),
        grid_spec=pltpu.PrefetchScalarGridSpec(
            num_scalar_prefetch=1,
            grid=(1,),
            in_specs=[full(rows.shape), full(cos_tab.shape), full(sin_tab.shape)],
            out_specs=full((heads * HD, count)),
        ),
        out_shape=jax.ShapeDtypeStruct((heads * HD, count), WIDE),
        compiler_params=pltpu.CompilerParams(vmem_limit_bytes=VMEM_BYTES),
        cost_estimate=pl.CostEstimate(flops=10**6, bytes_accessed=10**5, transcendentals=0),
    )(index, rows, cos_tab, sin_tab)


def back_kernel(rotary, heads, index_ref, cols_ref, cos_ref, sin_ref, out_ref):
    own = cols_ref.shape[1] // 8
    half = HD // 2
    width = out_ref.shape[1]
    for pair in range(4):
        lanes = slice(pair * 2 * own, (pair + 1) * 2 * own)
        cos_tab, sin_tab = cos_ref[:, lanes], sin_ref[:, lanes]
        parts = []
        for h in range(heads):
            front = cols_ref[h * HD : h * HD + half, lanes].astype(F32)
            back = cols_ref[h * HD + half : (h + 1) * HD, lanes].astype(F32)
            if h < rotary:
                front, back = front * cos_tab + back * sin_tab, back * cos_tab - front * sin_tab
            parts += [front, back]
        if width > heads * HD:
            parts.append(jnp.zeros((width - heads * HD, 2 * own), F32))
        rows = jnp.concatenate(parts, axis=0).T.astype(out_ref.dtype)
        for k in range(2):
            first = pl.multiple_of(index_ref[2 * pair + k] * own, own)
            out_ref[pl.ds(first, own), :] = rows[k * own : (k + 1) * own]


def to_rows(cols, index, cos_tab, sin_tab, rotary, heads, width):
    count = cols.shape[1]
    full = lambda shape: pl.BlockSpec(shape, lambda i, s: (0, 0))
    return pl.pallas_call(
        functools.partial(back_kernel, rotary, heads),
        grid_spec=pltpu.PrefetchScalarGridSpec(
            num_scalar_prefetch=1,
            grid=(1,),
            in_specs=[full(cols.shape), full(cos_tab.shape), full(sin_tab.shape)],
            out_specs=full((count, width)),
        ),
        out_shape=jax.ShapeDtypeStruct((count, width), WIDE),
        compiler_params=pltpu.CompilerParams(vmem_limit_bytes=VMEM_BYTES),
        cost_estimate=pl.CostEstimate(flops=10**6, bytes_accessed=10**5, transcendentals=0),
    )(index, cols, cos_tab, sin_tab)


def allowed_mask(block, starts, own_places):
    places = block * KB + lax.broadcasted_iota(jnp.int32, (KB, 1), 0)
    return (places >= starts) & (places <= own_places)


def attend_kernel(span_before, bounds_ref, q_ref, kv_ref, start_ref, out_ref, log_ref, k_rows, acc):
    step = pl.program_id(0)
    span = kv_ref.shape[1]

    @pl.when(step == 0)
    def _():
        for j in range(span // KB):
            k_rows[j * KB : (j + 1) * KB, :] = (
                kv_ref[0:HD, j * KB : (j + 1) * KB].astype(F32).T.astype(WIDE)
            )

    starts = start_ref[0:1, :]
    own_places = span_before + step * BQ + lax.broadcasted_iota(jnp.int32, (1, BQ), 1)
    acc[...] = jnp.zeros_like(acc)

    def one(masked, block, carry):
        first = pl.multiple_of(block * KB, KB)
        keys = k_rows[pl.ds(first, KB), :]
        values = kv_ref[HD : 2 * HD, pl.ds(first, KB)]
        if masked:
            mask = allowed_mask(block, starts, own_places)
        fresh = []
        for h in range(GROUP):
            top, total = carry[2 * h], carry[2 * h + 1]
            scores = dot(keys, q_ref[h * HD : (h + 1) * HD, :], 1, 0) * SCORE_LOG2
            if masked:
                scores = jnp.where(mask, scores, LOW)
            new_top = jnp.maximum(top, jnp.max(scores, axis=0, keepdims=True))
            probs = jnp.exp2(scores - new_top)
            fade = jnp.exp2(top - new_top)
            total = fade * total + jnp.sum(probs, axis=0, keepdims=True)
            acc[h] = fade * acc[h] + dot(values, probs.astype(WIDE), 1, 0)
            fresh += [new_top, total]
        return tuple(fresh)

    carry = (jnp.full((1, BQ), LOW, F32), jnp.zeros((1, BQ), F32)) * GROUP
    lo, full_lo, full_hi, hi = [bounds_ref[k, step] for k in range(4)]
    carry = lax.fori_loop(lo, full_lo, functools.partial(one, True), carry)
    carry = lax.fori_loop(full_lo, full_hi, functools.partial(one, False), carry)
    carry = lax.fori_loop(full_hi, hi, functools.partial(one, True), carry)
    for h in range(GROUP):
        top, total = carry[2 * h], carry[2 * h + 1]
        out_ref[h * HD : (h + 1) * HD, :] = (acc[h] / total).astype(WIDE)
        log_ref[h : h + 1, :] = top + jnp.log2(total)


def attend(q_cols, kv_cols, starts, bounds):
    count, span = q_cols.shape[1], kv_cols.shape[1]
    return pl.pallas_call(
        functools.partial(attend_kernel, span - count),
        grid_spec=pltpu.PrefetchScalarGridSpec(
            num_scalar_prefetch=1,
            grid=(count // BQ,),
            in_specs=[
                pl.BlockSpec((GROUP * HD, BQ), lambda i, s: (0, i)),
                pl.BlockSpec((2 * HD, span), lambda i, s: (0, 0)),
                pl.BlockSpec((1, BQ), lambda i, s: (0, i)),
            ],
            out_specs=[
                pl.BlockSpec((GROUP * HD, BQ), lambda i, s: (0, i)),
                pl.BlockSpec((8, BQ), lambda i, s: (0, i)),
            ],
            scratch_shapes=[pltpu.VMEM((span, HD), WIDE), pltpu.VMEM((GROUP, HD, BQ), F32)],
        ),
        out_shape=[
            jax.ShapeDtypeStruct((GROUP * HD, count), WIDE),
            jax.ShapeDtypeStruct((8, count), F32),
        ],
        compiler_params=pltpu.CompilerParams(vmem_limit_bytes=VMEM_BYTES),
        cost_estimate=pl.CostEstimate(flops=10**6, bytes_accessed=10**5, transcendentals=0),
    )(bounds, q_cols, kv_cols, starts)


def attend_back_kernel(
    span_before,
    bounds_ref,
    q_ref,
    kv_ref,
    start_ref,
    out_ref,
    log_ref,
    grad_ref,
    dq_ref,
    dkv_ref,
    k_rows,
    v_rows,
    q_rows,
    g_rows,
    dk,
    dv,
    probs_all,
    grads_all,
    dq,
):
    step = pl.program_id(0)
    span = kv_ref.shape[1]

    @pl.when(step == 0)
    def _():
        for j in range(span // KB):
            lanes = slice(j * KB, (j + 1) * KB)
            k_rows[lanes, :] = kv_ref[0:HD, lanes].astype(F32).T.astype(WIDE)
            v_rows[lanes, :] = kv_ref[HD : 2 * HD, lanes].astype(F32).T.astype(WIDE)
        dk[...] = jnp.zeros_like(dk)
        dv[...] = jnp.zeros_like(dv)

    starts = start_ref[0:1, :]
    own_places = span_before + step * BQ + lax.broadcasted_iota(jnp.int32, (1, BQ), 1)
    dq[...] = jnp.zeros_like(dq)
    deltas = []
    for h in range(GROUP):
        part = slice(h * HD, (h + 1) * HD)
        q_f32, g_f32 = q_ref[part, :].astype(F32), grad_ref[part, :].astype(F32)
        q_rows[h * BQ : (h + 1) * BQ, :] = q_f32.T.astype(WIDE)
        g_rows[h * BQ : (h + 1) * BQ, :] = g_f32.T.astype(WIDE)
        deltas.append(jnp.sum(g_f32 * out_ref[part, :].astype(F32), axis=0, keepdims=True))

    def one(masked, block, carry):
        first = pl.multiple_of(block * KB, KB)
        rows = pl.ds(first, KB)
        keys, values = k_rows[rows, :], v_rows[rows, :]
        key_cols = kv_ref[0:HD, rows]
        if masked:
            mask = allowed_mask(block, starts, own_places)
        for h in range(GROUP):
            part = slice(h * HD, (h + 1) * HD)
            lanes = slice(h * BQ, (h + 1) * BQ)
            scores = dot(keys, q_ref[part, :], 1, 0) * SCORE_LOG2 - log_ref[h : h + 1, :]
            if masked:
                scores = jnp.where(mask, scores, LOW)
            probs = jnp.exp2(scores)
            grad_probs = dot(values, grad_ref[part, :], 1, 0)
            grad_scores = (probs * (grad_probs - deltas[h])).astype(WIDE)
            probs_all[:, lanes] = probs.astype(WIDE)
            grads_all[:, lanes] = grad_scores
            dq[h] += dot(key_cols, grad_scores, 1, 0)
        dv[rows, :] += dot(probs_all[...], g_rows[...], 1, 0)
        dk[rows, :] += dot(grads_all[...], q_rows[...], 1, 0)
        return carry

    lo, full_lo, full_hi, hi = [bounds_ref[k, step] for k in range(4)]
    lax.fori_loop(lo, full_lo, functools.partial(one, True), 0)
    lax.fori_loop(full_lo, full_hi, functools.partial(one, False), 0)
    lax.fori_loop(full_hi, hi, functools.partial(one, True), 0)
    for h in range(GROUP):
        dq_ref[h * HD : (h + 1) * HD, :] = dq[h] * SCORE_SCALE

    @pl.when(step == pl.num_programs(0) - 1)
    def _():
        for j in range(span // KB):
            lanes = slice(j * KB, (j + 1) * KB)
            dkv_ref[0:HD, lanes] = dk[lanes, :].T * SCORE_SCALE
            dkv_ref[HD : 2 * HD, lanes] = dv[lanes, :].T


def attend_back(q_cols, kv_cols, starts, bounds, out_cols, logs, grad_cols):
    count, span = q_cols.shape[1], kv_cols.shape[1]
    wide_block = pl.BlockSpec((GROUP * HD, BQ), lambda i, s: (0, i))
    return pl.pallas_call(
        functools.partial(attend_back_kernel, span - count),
        grid_spec=pltpu.PrefetchScalarGridSpec(
            num_scalar_prefetch=1,
            grid=(count // BQ,),
            in_specs=[
                wide_block,
                pl.BlockSpec((2 * HD, span), lambda i, s: (0, 0)),
                pl.BlockSpec((1, BQ), lambda i, s: (0, i)),
                wide_block,
                pl.BlockSpec((8, BQ), lambda i, s: (0, i)),
                wide_block,
            ],
            out_specs=[wide_block, pl.BlockSpec((2 * HD, span), lambda i, s: (0, 0))],
            scratch_shapes=[
                pltpu.VMEM((span, HD), WIDE),
                pltpu.VMEM((span, HD), WIDE),
                pltpu.VMEM((GROUP * BQ, HD), WIDE),
                pltpu.VMEM((GROUP * BQ, HD), WIDE),
                pltpu.VMEM((span, HD), F32),
                pltpu.VMEM((span, HD), F32),
                pltpu.VMEM((KB, GROUP * BQ), WIDE),
                pltpu.VMEM((KB, GROUP * BQ), WIDE),
                pltpu.VMEM((GROUP, HD, BQ), F32),
            ],
        ),
        out_shape=[
            jax.ShapeDtypeStruct((GROUP * HD, count), F32),
            jax.ShapeDtypeStruct((2 * HD, span), F32),
        ],
        compiler_params=pltpu.CompilerParams(vmem_limit_bytes=VMEM_BYTES),
        cost_estimate=pl.CostEstimate(flops=10**6, bytes_accessed=10**5, transcendentals=0),
    )(bounds, q_cols, kv_cols, starts, out_cols, logs, grad_cols)


TINY = pl.CostEstimate(flops=10**6, bytes_accessed=10**5, transcendentals=0)
ANY = pl.BlockSpec(memory_space=pl.ANY)


def params():
    return pltpu.CompilerParams(vmem_limit_bytes=VMEM_BYTES)


def join_kernel(*refs):
    *parts, out, whole, sems = refs
    pairs, first = [], 0
    for k, part in enumerate(parts):
        rows = pl.ds(first, part.shape[0])
        pairs.append(
            (
                pltpu.make_async_copy(part, whole.at[rows, :], sems.at[0, k]),
                pltpu.make_async_copy(whole.at[rows, :], out.at[rows, :], sems.at[1, k]),
            )
        )
        first += part.shape[0]
    for copy_in, _ in pairs:
        copy_in.start()
    for copy_in, copy_out in pairs:
        copy_in.wait()
        copy_out.start()
    for _, copy_out in pairs:
        copy_out.wait()


def join(parts):
    rows = sum(part.shape[0] for part in parts)
    return pl.pallas_call(
        join_kernel,
        in_specs=[ANY] * len(parts),
        out_specs=ANY,
        out_shape=jax.ShapeDtypeStruct((rows, parts[0].shape[1]), parts[0].dtype),
        scratch_shapes=[
            pltpu.VMEM((rows, parts[0].shape[1]), parts[0].dtype),
            pltpu.SemaphoreType.DMA((2, len(parts))),
        ],
        compiler_params=params(),
        cost_estimate=TINY,
    )(*parts)


def project_kernel(x_ref, gain_ref, weight_ref, h_ref, out_ref):
    x = x_ref[...].astype(F32)
    inverse = lax.rsqrt(jnp.mean(x * x, axis=-1, keepdims=True) + eps)
    h = (x * inverse * gain_ref[...]).astype(WIDE)
    h_ref[...] = h
    out_ref[...] = dot(h, weight_ref[...], 1, 0)


def project(x_all, gain_row, weights, rows=256):
    count, model = x_all.shape
    width = weights.shape[1]
    return pl.pallas_call(
        project_kernel,
        grid=(count // rows,),
        in_specs=[
            pl.BlockSpec((rows, model), lambda i: (i, 0)),
            pl.BlockSpec((1, model), lambda i: (0, 0)),
            pl.BlockSpec(weights.shape, lambda i: (0, 0), pipeline_mode=pl.Buffered(1)),
        ],
        out_specs=[
            pl.BlockSpec((rows, model), lambda i: (i, 0)),
            pl.BlockSpec((rows, width), lambda i: (i, 0)),
        ],
        out_shape=[
            jax.ShapeDtypeStruct((count, model), WIDE),
            jax.ShapeDtypeStruct((count, width), F32),
        ],
        compiler_params=pltpu.CompilerParams(vmem_limit_bytes=VMEM_BYTES),
        cost_estimate=pl.CostEstimate(flops=10**6, bytes_accessed=10**5, transcendentals=0),
    )(x_all, gain_row, weights)


def narrow_kernel(a_ref, weight_ref, out_ref):
    out_ref[...] = dot(a_ref[...], weight_ref[...], 1, 0).astype(out_ref.dtype)


def whole(array):
    return pl.BlockSpec(array.shape, lambda i: (0, 0), pipeline_mode=pl.Buffered(1))


def narrow(a, weight, rows=256):
    count, model = a.shape
    return pl.pallas_call(
        narrow_kernel,
        grid=(count // rows,),
        in_specs=[pl.BlockSpec((rows, model), lambda i: (i, 0)), whole(weight)],
        out_specs=pl.BlockSpec((rows, weight.shape[1]), lambda i: (i, 0)),
        out_shape=jax.ShapeDtypeStruct((count, weight.shape[1]), WIDE),
        compiler_params=params(),
        cost_estimate=TINY,
    )(a, weight)


def units_kernel(has_prior, h_ref, cot_ref, weight_ref, *refs):
    *prior, acts_ref, back_ref, out_ref = refs
    width = weight_ref.shape[1] // 3
    down_w, gate_w, up_w = [weight_ref[:, k * width : (k + 1) * width] for k in range(3)]
    gate = dot(h_ref[...], gate_w, 1, 0)
    up = dot(h_ref[...], up_w, 1, 0)
    grad = dot(cot_ref[...], down_w, 1, 0)
    sigma = 1.0 / (1.0 + jnp.exp(-gate))
    silu = gate * sigma
    hidden = (silu * up).astype(WIDE)
    grad_gate = (grad * up * sigma * (1.0 + gate * (1.0 - sigma))).astype(WIDE)
    grad_up = (grad * silu).astype(WIDE)
    acts_ref[:, :width] = hidden
    acts_ref[:, width : 2 * width] = grad_gate
    acts_ref[:, 2 * width :] = grad_up
    back = dot(grad_gate, gate_w, 1, 1) + dot(grad_up, up_w, 1, 1)
    out = dot(hidden, down_w, 1, 1)
    if has_prior:
        back, out = back + prior[0][...].astype(F32), out + prior[1][...].astype(F32)
    back_ref[...] = back.astype(WIDE)
    out_ref[...] = out.astype(WIDE)


def hidden_units(h_two, cot, weights, first, count, prior=(), rows=256):
    model, width = h_two.shape[1], weights.shape[1]
    at = first // rows
    block = lambda n: pl.BlockSpec((rows, n), lambda i: (i, 0))
    shape = lambda n: jax.ShapeDtypeStruct((count, n), WIDE)
    return pl.pallas_call(
        functools.partial(units_kernel, bool(prior)),
        grid=(count // rows,),
        in_specs=[pl.BlockSpec((rows, model), lambda i: (i + at, 0))] * 2
        + [whole(weights)]
        + [block(model)] * len(prior),
        out_specs=[block(width), block(model), block(model)],
        out_shape=[shape(width), shape(model), shape(model)],
        compiler_params=params(),
        cost_estimate=TINY,
    )(h_two, cot, weights, *prior)


def unit_grads_kernel(h_ref, cot_ref, mine_ref, other_ref, out_ref):
    half, width = mine_ref.shape[0], mine_ref.shape[1] // 3
    for a_ref, columns in ((cot_ref, slice(0, width)), (h_ref, slice(width, 3 * width))):
        out_ref[:, columns] = (
            dot(a_ref[:half, :], mine_ref[:, columns], 0, 0)
            + dot(a_ref[half:, :], other_ref[:, columns], 0, 0)
        ).astype(WIDE)


def unit_grads(h_two, cot, mine, other, rows=256):
    count, model = h_two.shape
    width = mine.shape[1]
    return pl.pallas_call(
        unit_grads_kernel,
        grid=(model // rows,),
        in_specs=[pl.BlockSpec((count, rows), lambda i: (0, i))] * 2 + [whole(mine), whole(other)],
        out_specs=pl.BlockSpec((rows, width), lambda i: (i, 0)),
        out_shape=jax.ShapeDtypeStruct((model, width), WIDE),
        compiler_params=params(),
        cost_estimate=TINY,
    )(h_two, cot, mine, other)


def grads_kernel(a_ref, b_ref, out_ref):
    out_ref[...] = dot(a_ref[...], b_ref[...], 0, 0).astype(WIDE)


def weight_grads(a, b, rows=256):
    count, model = a.shape
    width = b.shape[1]
    return pl.pallas_call(
        grads_kernel,
        grid=(model // rows,),
        in_specs=[pl.BlockSpec((count, rows), lambda i: (0, i)), whole(b)],
        out_specs=pl.BlockSpec((rows, width), lambda i: (i, 0)),
        out_shape=jax.ShapeDtypeStruct((model, width), WIDE),
        compiler_params=params(),
        cost_estimate=TINY,
    )(a, b)


def tied(value, *others):
    return lax.optimization_barrier((value, *others))[0]


def together(*values):
    return lax.optimization_barrier(values)


def shifted(block, distance, period):
    count = lax.axis_size("z")
    route = [
        (i - distance, i)
        for i in range(count)
        if 0 <= i - distance < count and (i - distance) // period == i // period
    ]
    return lax.ppermute(block, "z", route)


def over(block, axis):
    return lax.ppermute(block, axis, SWAP)


def across(block):
    return lax.ppermute(block, ("y", "x"), [(i, 3 - i) for i in range(4)])


def plane_step_one(block):
    return over(block, "x"), over(block, "y")


def plane_step_two(over_x, over_y):
    half = over_x.shape[0] // 2
    return over(over_y[:half], "x"), over(over_x[half:], "y")


def plane_join(*mine):
    return join(list(mine) + [over(part, "c") for part in mine])


def added_pair(one, two):
    return (one.astype(F32) + two.astype(F32)).astype(WIDE)


def landed(values, *flights):
    held = [getattr(holder, field) for holder, field in flights]
    values, held = lax.optimization_barrier((values, held))
    for (holder, field), value in zip(flights, held):
        setattr(holder, field, value)
    return values


def plane_sum_one(total):
    own = total.shape[0] // 4
    half = own // 2
    return over(total[3 * own : 3 * own + half], "x"), over(total[3 * own + half :], "y")


def plane_sum_two(total, top, bottom):
    own = total.shape[0] // 4
    half = own // 2
    wide = lambda a, b: (a.astype(F32) + b.astype(F32)).astype(WIDE)
    to_x = jnp.concatenate(
        [total[own : own + half], wide(total[own + half : 2 * own], bottom)], axis=0
    )
    to_y = jnp.concatenate(
        [wide(total[2 * own : 2 * own + half], top), total[2 * own + half : 3 * own]], axis=0
    )
    return over(to_x, "x"), over(to_y, "y")


def added(total, *parts):
    own = total.shape[0] // 4
    return sum((part.astype(F32) for part in parts), total[:own].astype(F32))


def kept_columns(block, first_y):
    half = block.shape[1] // 2
    keep = jnp.where(first_y, block[:, :half], block[:, half:])
    give = jnp.where(first_y, block[:, half:], block[:, :half])
    return keep, give


def both_rows(keep, got, first_y):
    return jnp.concatenate([jnp.where(first_y, keep, got), jnp.where(first_y, got, keep)], axis=0)


def share_columns(block, first_y, *after):
    keep, give = kept_columns(block, first_y)
    if after:
        give = tied(give, *after)
    return both_rows(keep, over(give, "y"), first_y)


class Unshare:
    def __init__(self, block, first_y):
        half = block.shape[0] // 2
        self.first_y = first_y
        self.keep = jnp.where(first_y, block[:half], block[half:])
        self.got = over(jnp.where(first_y, block[half:], block[:half]), "y")

    def both(self):
        return (
            jnp.where(self.first_y, self.keep, self.got),
            jnp.where(self.first_y, self.got, self.keep),
        )


def gather_z(block):
    return lax.all_gather(block, "z", axis=0, tiled=True)


def sum_z(block):
    return lax.psum_scatter(block.astype(WIDE), "z", scatter_dimension=0, tiled=True)


def padded(block, multiple=128):
    extra = -block.shape[1] % multiple
    return jnp.pad(block, ((0, 0), (0, extra))) if extra else block


def norm_back(gradient, normed, inverse, gain_vec):
    scaled = gradient * gain_vec
    return inverse * (scaled - normed * jnp.mean(scaled * normed, axis=-1, keepdims=True))


def per_device(
    inputs,
    segments,
    positions,
    gain_attn,
    query_weight,
    key_weight,
    value_weight,
    out_weight,
    gain_mlp,
    gate_weight,
    up_weight,
    down_weight,
    cotangent,
):
    own = inputs.shape[0]
    half, count = 4 * own, 8 * own
    length = segments.shape[0] // SEQS
    reach = (DOC_MOST - 2) // count + 1
    period = lax.axis_size("z")
    if length % count == 0:
        period = length // count
        reach = min(reach, period - 1)
    span = (reach + 1) * count
    z, y = lax.axis_index("z"), lax.axis_index("y")
    x, c = lax.axis_index("x"), lax.axis_index("c")
    first_y = y == 0

    w_q, w_k, w_v, w_g, w_u = [
        w.astype(WIDE) for w in (query_weight, key_weight, value_weight, gate_weight, up_weight)
    ]
    w_o, w_d = out_weight.T.astype(WIDE), down_weight.T.astype(WIDE)
    nq, nk, nf = w_q.shape[1] // 2, w_k.shape[1] // 2, w_g.shape[1] // 2
    rows_w = w_q.shape[0]
    halves = lambda w: (w[:, : w.shape[1] // 2], w[:, w.shape[1] // 2 :])
    gain_pair = jnp.stack([gain_attn, gain_mlp] * 2, 1).astype(WIDE)
    near_a = share_columns(
        jnp.concatenate(
            [
                padded(jnp.concatenate([halves(w)[i] for w in (w_q, w_k, w_v, gain_pair)], axis=1))
                for i in range(2)
            ],
            axis=1,
        ),
        first_y,
    )
    chunks = (slice(0, CHUNK), slice(CHUNK, nf))
    triple = lambda cut: jnp.concatenate(
        [padded(halves(w)[i][:, cut]) for i in range(2) for w in (w_d, w_g, w_u)], axis=1
    )
    x_one = over(inputs, "x"), over(tied(inputs, near_a), "y")
    x_two = plane_step_two(*x_one)
    x_all = plane_join(inputs, *x_one, *x_two)
    cot_one = plane_step_one(tied(cotangent, *x_two))
    near_o = share_columns(w_o, first_y, *x_two)
    near_c = [share_columns(triple(cut), first_y, *x_two) for cut in chunks]
    full_a, full_o = gather_z(near_a), gather_z(near_o)
    full_c = [gather_z(near) for near in near_c]
    first_gain = nq + 2 * nk
    gains = full_a[:, first_gain : first_gain + 2].astype(F32)
    gain_first, gain_second = gains[:, 0], gains[:, 1]

    other_positions = lax.ppermute(positions, "y", SWAP)
    token_positions = jnp.where(
        first_y,
        jnp.concatenate([positions, other_positions]),
        jnp.concatenate([other_positions, positions]),
    )
    frequency = rope_base ** (-(jnp.arange(HD // 2, dtype=F32) * 2.0 / HD))
    angles = frequency[:, None] * token_positions.astype(F32)[None, :]
    cos_tab, sin_tab = jnp.cos(angles), jnp.sin(angles)
    places = jnp.arange(8, dtype=jnp.int32)
    flips = places ^ (y * 4 + x * 2 + c).astype(jnp.int32)
    index = (flips % 2) * 4 + flips // 2
    padded_segs = jnp.concatenate([jnp.full((reach * count,), -1, jnp.int32), segments])
    key_segs = lax.dynamic_slice_in_dim(padded_segs, z * count, span, 0)
    query_segs = lax.dynamic_slice_in_dim(segments, z * count, count, 0)
    starts = jnp.sum((key_segs[:, None] < query_segs[None, :]).astype(jnp.int32), axis=0)
    first_rows = jnp.arange(count // BQ, dtype=jnp.int32) * BQ
    lo = starts[first_rows] // KB
    hi = (reach * count + first_rows + BQ + KB - 1) // KB
    full_lo = jnp.clip((starts[first_rows + BQ - 1] + KB - 1) // KB, lo, hi)
    full_hi = jnp.clip((reach * count + first_rows + 1) // KB, full_lo, hi)
    bounds = jnp.stack([lo, full_lo, full_hi, hi])
    starts = starts[None, :]

    h_one, qkv = project(x_all, gain_first[None, :], full_a)
    turned = to_columns(qkv, index, cos_tab, sin_tab, GROUP + 1, GROUP + 2)
    q_cols, kv_own = turned[: GROUP * HD], turned[GROUP * HD :]
    far_kv = [shifted(kv_own, distance, period) for distance in range(reach, 0, -1)]
    kv_cols = jnp.concatenate(far_kv + [kv_own], axis=1)
    kv_cols, full_o, cot_one, _ = lax.optimization_barrier((kv_cols, full_o, cot_one, near_c))
    cot_two = plane_step_two(*cot_one)
    out_cols, logs = attend(q_cols, kv_cols, starts, bounds)
    out_cols, *cot_two = together(out_cols, *cot_two)
    attended = to_rows(out_cols, index, cos_tab, sin_tab, 0, GROUP, GROUP * HD)
    grad_mix = plane_join(cotangent, *cot_one, *cot_two)
    input_f32 = inputs.astype(F32)
    inverse_one = lax.rsqrt(jnp.mean(input_f32 * input_f32, axis=-1, keepdims=True) + eps)
    normed_one = input_f32 * inverse_one
    mid_got = over(dot(attended[half:], full_o, 1, 1).astype(WIDE), "c")
    mid_total = (dot(attended[:half], full_o, 1, 1) + mid_got.astype(F32)).astype(WIDE)
    mid_far = plane_sum_one(mid_total)
    mid_near = plane_sum_two(mid_total, *mid_far)
    x_mid = input_f32 + added(mid_total, *mid_near)

    inverse_two = lax.rsqrt(jnp.mean(x_mid * x_mid, axis=-1, keepdims=True) + eps)
    normed_two = x_mid * inverse_two
    h_own = (normed_two * gain_second).astype(WIDE)
    h_step = plane_step_one(h_own)
    h_two = plane_join(h_own, *h_step, *plane_step_two(*h_step))
    h_two, grad_mix = together(h_two, grad_mix)
    other_1 = hidden_units(h_two, grad_mix, full_c[0], half, half)
    mine_1 = hidden_units(h_two, grad_mix, full_c[0], 0, half)
    term_1 = unit_grads(h_two, grad_mix, mine_1[0], other_1[0])
    full_c[1], other_1, mine_1, term_1 = lax.optimization_barrier(
        (full_c[1], other_1, mine_1, term_1)
    )
    sums = [sum_z(term_1)]
    acts_other, back_other, out_other = hidden_units(
        h_two, grad_mix, full_c[1], half, half, other_1[1:]
    )
    back_got, out_got = over(back_other, "c"), over(out_other, "c")
    acts_mine, back_mine, out_mine = hidden_units(h_two, grad_mix, full_c[1], 0, half, mine_1[1:])
    back_total = added_pair(back_mine, back_got)
    back_far = plane_sum_one(back_total)
    term_2 = unit_grads(h_two, grad_mix, acts_mine, acts_other)
    back_near = plane_sum_two(back_total, *back_far)
    *back_near, term_2 = together(*back_near, term_2)
    sums.append(sum_z(term_2))
    grad_h_two = added(back_total, *back_near)
    grad_mid = cotangent.astype(F32) + norm_back(grad_h_two, normed_two, inverse_two, gain_second)
    branch_own = grad_mid.astype(WIDE)
    branch_one = plane_step_one(branch_own)
    branch_two = plane_step_two(*branch_one)
    out_total = added_pair(out_mine, out_got)
    grad_branch = plane_join(branch_own, *branch_one, *branch_two)
    grad_branch, out_total, sums[0] = together(grad_branch, out_total, sums[0])

    grad_attended = narrow(grad_branch, full_o)
    grad_cols = to_columns(grad_attended, index, cos_tab, sin_tab, 0, GROUP)
    grad_cols, out_total, sums[0] = together(grad_cols, out_total, sums[0])
    out_sends = [
        over(out_total[own : 2 * own], "x"),
        over(out_total[2 * own : 3 * own], "y"),
        across(out_total[3 * own :]),
    ]
    dq_cols, dkv_cols = attend_back(q_cols, kv_cols, starts, bounds, out_cols, logs, grad_cols)
    dkv_cols, *out_sends = together(dkv_cols, *out_sends)
    output = (x_mid + added(out_total, *out_sends)).astype(WIDE)
    owned = [Unshare(tied(sums[0], dkv_cols), first_y)]
    dkv_own = dkv_cols[:, reach * count :]
    for distance in range(1, reach + 1):
        first = (reach - distance) * count
        dkv_own = dkv_own + shifted(
            dkv_cols[:, first : first + count].astype(WIDE), -distance, period
        ).astype(F32)
    dkv_own = landed(dkv_own, (owned[0], "got"))
    grad_qkv = to_rows(
        jnp.concatenate([dq_cols, dkv_own], axis=0),
        index,
        cos_tab,
        sin_tab,
        GROUP + 1,
        GROUP + 2,
        full_a.shape[1],
    )
    qkv_part = weight_grads(h_one, grad_qkv)
    grad_qkv, qkv_part = together(grad_qkv, qkv_part)
    one_got = over(dot(grad_qkv[half:], full_a, 1, 1).astype(WIDE), "c")
    one_total = (dot(grad_qkv[:half], full_a, 1, 1) + one_got.astype(F32)).astype(WIDE)
    one_total, qkv_part, sums[1] = together(one_total, qkv_part, sums[1])
    qkv_grad = sum_z(qkv_part)
    owned.append(Unshare(sums[1], first_y))
    one_far = plane_sum_one(one_total)
    out_term = weight_grads(grad_branch, tied(attended, qkv_part))
    *one_far, out_term = together(*one_far, out_term)
    one_near = plane_sum_two(one_total, *one_far)
    *one_near, qkv_grad, out_term = together(*one_near, qkv_grad, out_term)
    out_grad = sum_z(out_term)
    owned_o = Unshare(out_grad, first_y)
    grad_h_one = added(one_total, *one_near)
    input_grad = (grad_mid + norm_back(grad_h_one, normed_one, inverse_one, gain_first)).astype(
        WIDE
    )

    input_grad, out_term = landed((input_grad, out_term), (owned[0], "got"), (owned[1], "got"))
    owned = [part.both() for part in owned]
    kept = [CHUNK, nf - CHUNK]
    width = [full.shape[1] // 3 for full in full_c]

    def unit_columns(k):
        return jnp.concatenate(
            [
                owned[j][i][:, k * width[j] : k * width[j] + kept[j]]
                for i in range(2)
                for j in range(2)
            ],
            axis=1,
        ).astype(F32)

    down_out, gate_out, up_out = unit_columns(0).T, unit_columns(1), unit_columns(2)
    one, two = Unshare(qkv_grad, first_y).both()
    pick = lambda a, b: jnp.concatenate([one[:, a:b], two[:, a:b]], axis=1).astype(F32)
    q_out, k_out, v_out = pick(0, nq), pick(nq, nq + nk), pick(nq + nk, nq + 2 * nk)
    o_out = jnp.concatenate(owned_o.both(), axis=1).T.astype(F32)

    def row_sums(weight, grad):
        return jnp.sum(weight.astype(F32) * grad, axis=1)

    gain_sums = jnp.stack(
        [
            row_sums(w_q, q_out) + row_sums(w_k, k_out) + row_sums(w_v, v_out),
            row_sums(w_g, gate_out) + row_sums(w_u, up_out),
        ]
    )
    gain_sums = gain_sums + lax.ppermute(gain_sums, "x", SWAP)
    gain_sums = gain_sums + lax.ppermute(gain_sums, "c", SWAP)
    gain_one_out = gain_sums[0] / gain_attn.astype(WIDE).astype(F32)
    gain_two_out = gain_sums[1] / gain_mlp.astype(WIDE).astype(F32)
    return (
        output,
        input_grad,
        gain_one_out,
        q_out,
        k_out,
        v_out,
        o_out,
        gain_two_out,
        gate_out,
        up_out,
        down_out,
    )


def solution(mesh):
    seq, tensor = mesh.shape["seq"], mesh.shape["tensor"]
    grid = Mesh(
        mesh.devices.reshape(seq // 2, 2, tensor // 2, 2), ("z", "y", "x", "c")
    )
    rows, cols = ("z", "y"), ("x", "c")
    tokens, weight, weight_t = P(rows + cols, None), P(rows, cols), P(cols, rows)
    in_specs = (
        tokens,
        P(),
        P(rows),
        P(rows),
        weight,
        weight,
        weight,
        weight_t,
        P(rows),
        weight,
        weight,
        weight_t,
        tokens,
    )
    out_specs = (
        tokens,
        tokens,
        P(rows),
        weight,
        weight,
        weight,
        weight_t,
        P(rows),
        weight,
        weight,
        weight_t,
    )
    return jax.shard_map(
        per_device, mesh=grid, in_specs=in_specs, out_specs=out_specs, check_vma=False
    )
```

```python
import functools

import jax
import jax.numpy as jnp
from jax import lax
from jax.experimental import pallas as pl
from jax.experimental.pallas import tpu as pltpu
from jax.sharding import Mesh
from jax.sharding import PartitionSpec as P

HEADS = 32
KV = 8
HD = 80
SEQS = 2
DOC_MOST = 2000
GROUP = HEADS // KV

eps = 1e-05
rope_base = 10000.0
LOG2E = 1.4426950408889634
SCORE_LOG2 = HD ** (-0.5) * LOG2E
SCORE_SCALE = HD ** (-0.5)
LOW = -1e30
BQ = 256
CHUNK = 384
KB = 256
WIDE = jnp.bfloat16
F32 = jnp.float32
VMEM_BYTES = 48 * 1024 * 1024

SWAP = [(0, 1), (1, 0)]


def dot(a, b, ca, cb):
    return lax.dot_general(a, b, (((ca,), (cb,)), ((), ())), preferred_element_type=F32)


def turn_kernel(rotary, heads, index_ref, rows_ref, cos_ref, sin_ref, out_ref):
    own = rows_ref.shape[0] // 8
    half = HD // 2
    for pair in range(4):
        parts = [
            rows_ref[pl.ds(pl.multiple_of(index_ref[2 * pair + k] * own, own), own), :].astype(F32)
            for k in range(2)
        ]
        turned = jnp.concatenate(parts, axis=0).T
        lanes = slice(pair * 2 * own, (pair + 1) * 2 * own)
        cos_tab, sin_tab = cos_ref[:, lanes], sin_ref[:, lanes]
        for h in range(heads):
            front, back = turned[h * HD : h * HD + half], turned[h * HD + half : (h + 1) * HD]
            if h < rotary:
                front, back = front * cos_tab - back * sin_tab, back * cos_tab + front * sin_tab
            out_ref[h * HD : (h + 1) * HD, lanes] = jnp.concatenate([front, back], axis=0).astype(
                out_ref.dtype
            )


def to_columns(rows, index, cos_tab, sin_tab, rotary, heads):
    count = rows.shape[0]
    full = lambda shape: pl.BlockSpec(shape, lambda i, s: (0, 0))
    return pl.pallas_call(
        functools.partial(turn_kernel, rotary, heads),
        grid_spec=pltpu.PrefetchScalarGridSpec(
            num_scalar_prefetch=1,
            grid=(1,),
            in_specs=[full(rows.shape), full(cos_tab.shape), full(sin_tab.shape)],
            out_specs=full((heads * HD, count)),
        ),
        out_shape=jax.ShapeDtypeStruct((heads * HD, count), WIDE),
        compiler_params=pltpu.CompilerParams(vmem_limit_bytes=VMEM_BYTES),
        cost_estimate=pl.CostEstimate(flops=10**6, bytes_accessed=10**5, transcendentals=0),
    )(index, rows, cos_tab, sin_tab)


def back_kernel(rotary, heads, index_ref, cols_ref, cos_ref, sin_ref, out_ref):
    own = cols_ref.shape[1] // 8
    half = HD // 2
    width = out_ref.shape[1]
    for pair in range(4):
        lanes = slice(pair * 2 * own, (pair + 1) * 2 * own)
        cos_tab, sin_tab = cos_ref[:, lanes], sin_ref[:, lanes]
        parts = []
        for h in range(heads):
            front = cols_ref[h * HD : h * HD + half, lanes].astype(F32)
            back = cols_ref[h * HD + half : (h + 1) * HD, lanes].astype(F32)
            if h < rotary:
                front, back = front * cos_tab + back * sin_tab, back * cos_tab - front * sin_tab
            parts += [front, back]
        if width > heads * HD:
            parts.append(jnp.zeros((width - heads * HD, 2 * own), F32))
        rows = jnp.concatenate(parts, axis=0).T.astype(out_ref.dtype)
        for k in range(2):
            first = pl.multiple_of(index_ref[2 * pair + k] * own, own)
            out_ref[pl.ds(first, own), :] = rows[k * own : (k + 1) * own]


def to_rows(cols, index, cos_tab, sin_tab, rotary, heads, width):
    count = cols.shape[1]
    full = lambda shape: pl.BlockSpec(shape, lambda i, s: (0, 0))
    return pl.pallas_call(
        functools.partial(back_kernel, rotary, heads),
        grid_spec=pltpu.PrefetchScalarGridSpec(
            num_scalar_prefetch=1,
            grid=(1,),
            in_specs=[full(cols.shape), full(cos_tab.shape), full(sin_tab.shape)],
            out_specs=full((count, width)),
        ),
        out_shape=jax.ShapeDtypeStruct((count, width), WIDE),
        compiler_params=pltpu.CompilerParams(vmem_limit_bytes=VMEM_BYTES),
        cost_estimate=pl.CostEstimate(flops=10**6, bytes_accessed=10**5, transcendentals=0),
    )(index, cols, cos_tab, sin_tab)


def allowed_mask(block, starts, own_places):
    places = block * KB + lax.broadcasted_iota(jnp.int32, (KB, 1), 0)
    return (places >= starts) & (places <= own_places)


def attend_kernel(places, bounds_ref, q_ref, kv_ref, start_ref, *refs):
    first_query, first_key = places
    *prior, out_ref, log_ref, k_rows, acc = refs
    step = pl.program_id(0)
    span = kv_ref.shape[1]

    @pl.when(step == 0)
    def _():
        for j in range(span // KB):
            k_rows[j * KB : (j + 1) * KB, :] = (
                kv_ref[0:HD, j * KB : (j + 1) * KB].astype(F32).T.astype(WIDE)
            )

    starts = start_ref[0:1, :]
    own_places = first_query + step * BQ + lax.broadcasted_iota(jnp.int32, (1, BQ), 1)
    if prior:
        for h in range(GROUP):
            acc[h] = prior[0][h * HD : (h + 1) * HD, :]
    else:
        acc[...] = jnp.zeros_like(acc)

    def one(masked, block, carry):
        first = pl.multiple_of(block * KB - first_key, KB)
        keys = k_rows[pl.ds(first, KB), :]
        values = kv_ref[HD : 2 * HD, pl.ds(first, KB)]
        if masked:
            mask = allowed_mask(block, starts, own_places)
        fresh = []
        for h in range(GROUP):
            top, total = carry[2 * h], carry[2 * h + 1]
            scores = dot(keys, q_ref[h * HD : (h + 1) * HD, :], 1, 0) * SCORE_LOG2
            if masked:
                scores = jnp.where(mask, scores, LOW)
            new_top = jnp.maximum(top, jnp.max(scores, axis=0, keepdims=True))
            probs = jnp.exp2(scores - new_top)
            fade = jnp.exp2(top - new_top)
            total = fade * total + jnp.sum(probs, axis=0, keepdims=True)
            acc[h] = fade * acc[h] + dot(values, probs.astype(WIDE), 1, 0)
            fresh += [new_top, total]
        return tuple(fresh)

    carry = (jnp.full((1, BQ), LOW, F32), jnp.zeros((1, BQ), F32)) * GROUP
    if prior:
        carry = sum(((prior[1][h : h + 1, :], jnp.ones((1, BQ), F32)) for h in range(GROUP)), ())
    lo, full_lo, full_hi, hi = [bounds_ref[k, step] for k in range(4)]
    carry = lax.fori_loop(lo, full_lo, functools.partial(one, True), carry)
    carry = lax.fori_loop(full_lo, full_hi, functools.partial(one, False), carry)
    carry = lax.fori_loop(full_hi, hi, functools.partial(one, True), carry)
    for h in range(GROUP):
        top, total = carry[2 * h], carry[2 * h + 1]
        out_ref[h * HD : (h + 1) * HD, :] = (acc[h] / total).astype(out_ref.dtype)
        log_ref[h : h + 1, :] = top + jnp.log2(total)


def attend(q_cols, kv_cols, starts, bounds, places, prior, out_type):
    count, span = q_cols.shape[1], kv_cols.shape[1]
    wide_block = pl.BlockSpec((GROUP * HD, BQ), lambda i, s: (0, i))
    log_block = pl.BlockSpec((8, BQ), lambda i, s: (0, i))
    return pl.pallas_call(
        functools.partial(attend_kernel, places),
        grid_spec=pltpu.PrefetchScalarGridSpec(
            num_scalar_prefetch=1,
            grid=(count // BQ,),
            in_specs=[
                wide_block,
                pl.BlockSpec((2 * HD, span), lambda i, s: (0, 0)),
                pl.BlockSpec((1, BQ), lambda i, s: (0, i)),
            ]
            + [wide_block, log_block][: len(prior)],
            out_specs=[wide_block, log_block],
            scratch_shapes=[pltpu.VMEM((span, HD), WIDE), pltpu.VMEM((GROUP, HD, BQ), F32)],
        ),
        out_shape=[
            jax.ShapeDtypeStruct((GROUP * HD, count), out_type),
            jax.ShapeDtypeStruct((8, count), F32),
        ],
        compiler_params=pltpu.CompilerParams(vmem_limit_bytes=VMEM_BYTES),
        cost_estimate=pl.CostEstimate(flops=10**6, bytes_accessed=10**5, transcendentals=0),
    )(bounds, q_cols, kv_cols, starts, *prior)


def attend_back_kernel(places, bounds_ref, q_ref, kv_ref, start_ref, out_ref, log_ref, grad_ref, *refs):
    first_query, first_key = places
    *prior, dq_ref, dkv_ref, k_rows, v_rows, q_rows, g_rows, dk, dv, probs_all, grads_all, dq = refs
    step = pl.program_id(0)
    span = kv_ref.shape[1]

    @pl.when(step == 0)
    def _():
        for j in range(span // KB):
            lanes = slice(j * KB, (j + 1) * KB)
            k_rows[lanes, :] = kv_ref[0:HD, lanes].astype(F32).T.astype(WIDE)
            v_rows[lanes, :] = kv_ref[HD : 2 * HD, lanes].astype(F32).T.astype(WIDE)
        dk[...] = jnp.zeros_like(dk)
        dv[...] = jnp.zeros_like(dv)

    starts = start_ref[0:1, :]
    own_places = first_query + step * BQ + lax.broadcasted_iota(jnp.int32, (1, BQ), 1)
    dq[...] = jnp.zeros_like(dq)
    deltas = []
    for h in range(GROUP):
        part = slice(h * HD, (h + 1) * HD)
        q_f32, g_f32 = q_ref[part, :].astype(F32), grad_ref[part, :].astype(F32)
        q_rows[h * BQ : (h + 1) * BQ, :] = q_f32.T.astype(WIDE)
        g_rows[h * BQ : (h + 1) * BQ, :] = g_f32.T.astype(WIDE)
        deltas.append(jnp.sum(g_f32 * out_ref[part, :].astype(F32), axis=0, keepdims=True))

    def one(masked, block, carry):
        first = pl.multiple_of(block * KB - first_key, KB)
        rows = pl.ds(first, KB)
        keys, values = k_rows[rows, :], v_rows[rows, :]
        key_cols = kv_ref[0:HD, rows]
        if masked:
            mask = allowed_mask(block, starts, own_places)
        for h in range(GROUP):
            part = slice(h * HD, (h + 1) * HD)
            lanes = slice(h * BQ, (h + 1) * BQ)
            scores = dot(keys, q_ref[part, :], 1, 0) * SCORE_LOG2 - log_ref[h : h + 1, :]
            if masked:
                scores = jnp.where(mask, scores, LOW)
            probs = jnp.exp2(scores)
            grad_probs = dot(values, grad_ref[part, :], 1, 0)
            grad_scores = (probs * (grad_probs - deltas[h])).astype(WIDE)
            probs_all[:, lanes] = probs.astype(WIDE)
            grads_all[:, lanes] = grad_scores
            dq[h] += dot(key_cols, grad_scores, 1, 0)
        dv[rows, :] += dot(probs_all[...], g_rows[...], 1, 0)
        dk[rows, :] += dot(grads_all[...], q_rows[...], 1, 0)
        return carry

    lo, full_lo, full_hi, hi = [bounds_ref[k, step] for k in range(4)]
    lax.fori_loop(lo, full_lo, functools.partial(one, True), 0)
    lax.fori_loop(full_lo, full_hi, functools.partial(one, False), 0)
    lax.fori_loop(full_hi, hi, functools.partial(one, True), 0)
    for h in range(GROUP):
        part = slice(h * HD, (h + 1) * HD)
        dq_ref[part, :] = dq[h] * SCORE_SCALE + (prior[0][part, :] if prior else 0.0)

    @pl.when(step == pl.num_programs(0) - 1)
    def _():
        for j in range(span // KB):
            lanes = slice(j * KB, (j + 1) * KB)
            dkv_ref[0:HD, lanes] = dk[lanes, :].T * SCORE_SCALE
            dkv_ref[HD : 2 * HD, lanes] = dv[lanes, :].T


def attend_back(q_cols, kv_cols, starts, bounds, places, out_cols, logs, grad_cols, prior=()):
    count, span = q_cols.shape[1], kv_cols.shape[1]
    wide_block = pl.BlockSpec((GROUP * HD, BQ), lambda i, s: (0, i))
    return pl.pallas_call(
        functools.partial(attend_back_kernel, places),
        grid_spec=pltpu.PrefetchScalarGridSpec(
            num_scalar_prefetch=1,
            grid=(count // BQ,),
            in_specs=[
                wide_block,
                pl.BlockSpec((2 * HD, span), lambda i, s: (0, 0)),
                pl.BlockSpec((1, BQ), lambda i, s: (0, i)),
                wide_block,
                pl.BlockSpec((8, BQ), lambda i, s: (0, i)),
                wide_block,
            ]
            + [wide_block] * len(prior),
            out_specs=[wide_block, pl.BlockSpec((2 * HD, span), lambda i, s: (0, 0))],
            scratch_shapes=[
                pltpu.VMEM((span, HD), WIDE),
                pltpu.VMEM((span, HD), WIDE),
                pltpu.VMEM((GROUP * BQ, HD), WIDE),
                pltpu.VMEM((GROUP * BQ, HD), WIDE),
                pltpu.VMEM((span, HD), F32),
                pltpu.VMEM((span, HD), F32),
                pltpu.VMEM((KB, GROUP * BQ), WIDE),
                pltpu.VMEM((KB, GROUP * BQ), WIDE),
                pltpu.VMEM((GROUP, HD, BQ), F32),
            ],
        ),
        out_shape=[
            jax.ShapeDtypeStruct((GROUP * HD, count), F32),
            jax.ShapeDtypeStruct((2 * HD, span), F32),
        ],
        compiler_params=pltpu.CompilerParams(vmem_limit_bytes=VMEM_BYTES),
        cost_estimate=pl.CostEstimate(flops=10**6, bytes_accessed=10**5, transcendentals=0),
    )(bounds, q_cols, kv_cols, starts, out_cols, logs, grad_cols, *prior)


TINY = pl.CostEstimate(flops=10**6, bytes_accessed=10**5, transcendentals=0)
ANY = pl.BlockSpec(memory_space=pl.ANY)


def params():
    return pltpu.CompilerParams(vmem_limit_bytes=VMEM_BYTES)


def join_kernel(*refs):
    *parts, out, whole, sems = refs
    pairs, first = [], 0
    for k, part in enumerate(parts):
        rows = pl.ds(first, part.shape[0])
        pairs.append(
            (
                pltpu.make_async_copy(part, whole.at[rows, :], sems.at[0, k]),
                pltpu.make_async_copy(whole.at[rows, :], out.at[rows, :], sems.at[1, k]),
            )
        )
        first += part.shape[0]
    for copy_in, _ in pairs:
        copy_in.start()
    for copy_in, copy_out in pairs:
        copy_in.wait()
        copy_out.start()
    for _, copy_out in pairs:
        copy_out.wait()


def join(parts):
    rows = sum(part.shape[0] for part in parts)
    return pl.pallas_call(
        join_kernel,
        in_specs=[ANY] * len(parts),
        out_specs=ANY,
        out_shape=jax.ShapeDtypeStruct((rows, parts[0].shape[1]), parts[0].dtype),
        scratch_shapes=[
            pltpu.VMEM((rows, parts[0].shape[1]), parts[0].dtype),
            pltpu.SemaphoreType.DMA((2, len(parts))),
        ],
        compiler_params=params(),
        cost_estimate=TINY,
    )(*parts)


def project_kernel(x_ref, gain_ref, weight_ref, h_ref, out_ref):
    x = x_ref[...].astype(F32)
    inverse = lax.rsqrt(jnp.mean(x * x, axis=-1, keepdims=True) + eps)
    h = (x * inverse * gain_ref[...]).astype(WIDE)
    h_ref[...] = h
    out_ref[...] = dot(h, weight_ref[...], 1, 0)


def project(x_all, gain_row, weights, rows=256):
    count, model = x_all.shape
    width = weights.shape[1]
    return pl.pallas_call(
        project_kernel,
        grid=(count // rows,),
        in_specs=[
            pl.BlockSpec((rows, model), lambda i: (i, 0)),
            pl.BlockSpec((1, model), lambda i: (0, 0)),
            pl.BlockSpec(weights.shape, lambda i: (0, 0), pipeline_mode=pl.Buffered(1)),
        ],
        out_specs=[
            pl.BlockSpec((rows, model), lambda i: (i, 0)),
            pl.BlockSpec((rows, width), lambda i: (i, 0)),
        ],
        out_shape=[
            jax.ShapeDtypeStruct((count, model), WIDE),
            jax.ShapeDtypeStruct((count, width), F32),
        ],
        compiler_params=pltpu.CompilerParams(vmem_limit_bytes=VMEM_BYTES),
        cost_estimate=pl.CostEstimate(flops=10**6, bytes_accessed=10**5, transcendentals=0),
    )(x_all, gain_row, weights)


def narrow_kernel(a_ref, weight_ref, out_ref):
    out_ref[...] = dot(a_ref[...], weight_ref[...], 1, 0).astype(out_ref.dtype)


def whole(array):
    return pl.BlockSpec(array.shape, lambda i: (0, 0), pipeline_mode=pl.Buffered(1))


def narrow(a, weight, rows=256):
    count, model = a.shape
    return pl.pallas_call(
        narrow_kernel,
        grid=(count // rows,),
        in_specs=[pl.BlockSpec((rows, model), lambda i: (i, 0)), whole(weight)],
        out_specs=pl.BlockSpec((rows, weight.shape[1]), lambda i: (i, 0)),
        out_shape=jax.ShapeDtypeStruct((count, weight.shape[1]), WIDE),
        compiler_params=params(),
        cost_estimate=TINY,
    )(a, weight)


def units_kernel(has_prior, h_ref, cot_ref, weight_ref, *refs):
    *prior, acts_ref, back_ref, out_ref = refs
    width = weight_ref.shape[1] // 3
    down_w, gate_w, up_w = [weight_ref[:, k * width : (k + 1) * width] for k in range(3)]
    gate = dot(h_ref[...], gate_w, 1, 0)
    up = dot(h_ref[...], up_w, 1, 0)
    grad = dot(cot_ref[...], down_w, 1, 0)
    sigma = 1.0 / (1.0 + jnp.exp(-gate))
    silu = gate * sigma
    hidden = (silu * up).astype(WIDE)
    grad_gate = (grad * up * sigma * (1.0 + gate * (1.0 - sigma))).astype(WIDE)
    grad_up = (grad * silu).astype(WIDE)
    acts_ref[:, :width] = hidden
    acts_ref[:, width : 2 * width] = grad_gate
    acts_ref[:, 2 * width :] = grad_up
    back = dot(grad_gate, gate_w, 1, 1) + dot(grad_up, up_w, 1, 1)
    out = dot(hidden, down_w, 1, 1)
    if has_prior:
        back, out = back + prior[0][...].astype(F32), out + prior[1][...].astype(F32)
    back_ref[...] = back.astype(WIDE)
    out_ref[...] = out.astype(WIDE)


def hidden_units(h_two, cot, weights, first, count, prior=(), rows=256):
    model, width = h_two.shape[1], weights.shape[1]
    at = first // rows
    block = lambda n: pl.BlockSpec((rows, n), lambda i: (i, 0))
    shape = lambda n: jax.ShapeDtypeStruct((count, n), WIDE)
    return pl.pallas_call(
        functools.partial(units_kernel, bool(prior)),
        grid=(count // rows,),
        in_specs=[pl.BlockSpec((rows, model), lambda i: (i + at, 0))] * 2
        + [whole(weights)]
        + [block(model)] * len(prior),
        out_specs=[block(width), block(model), block(model)],
        out_shape=[shape(width), shape(model), shape(model)],
        compiler_params=params(),
        cost_estimate=TINY,
    )(h_two, cot, weights, *prior)


def unit_grads_kernel(h_ref, cot_ref, mine_ref, other_ref, out_ref):
    half, width = mine_ref.shape[0], mine_ref.shape[1] // 3
    for a_ref, columns in ((cot_ref, slice(0, width)), (h_ref, slice(width, 3 * width))):
        out_ref[:, columns] = (
            dot(a_ref[:half, :], mine_ref[:, columns], 0, 0)
            + dot(a_ref[half:, :], other_ref[:, columns], 0, 0)
        ).astype(WIDE)


def unit_grads(h_two, cot, mine, other, rows=256):
    count, model = h_two.shape
    width = mine.shape[1]
    return pl.pallas_call(
        unit_grads_kernel,
        grid=(model // rows,),
        in_specs=[pl.BlockSpec((count, rows), lambda i: (0, i))] * 2 + [whole(mine), whole(other)],
        out_specs=pl.BlockSpec((rows, width), lambda i: (i, 0)),
        out_shape=jax.ShapeDtypeStruct((model, width), WIDE),
        compiler_params=params(),
        cost_estimate=TINY,
    )(h_two, cot, mine, other)


def grads_kernel(a_ref, b_ref, out_ref):
    out_ref[...] = dot(a_ref[...], b_ref[...], 0, 0).astype(WIDE)


def weight_grads(a, b, rows=256):
    count, model = a.shape
    width = b.shape[1]
    return pl.pallas_call(
        grads_kernel,
        grid=(model // rows,),
        in_specs=[pl.BlockSpec((count, rows), lambda i: (0, i)), whole(b)],
        out_specs=pl.BlockSpec((rows, width), lambda i: (i, 0)),
        out_shape=jax.ShapeDtypeStruct((model, width), WIDE),
        compiler_params=params(),
        cost_estimate=TINY,
    )(a, b)


def tied(value, *others):
    return lax.optimization_barrier((value, *others))[0]


def together(*values):
    return lax.optimization_barrier(values)


def shifted(block, distance, period):
    count = lax.axis_size("z")
    route = [
        (i - distance, i)
        for i in range(count)
        if 0 <= i - distance < count and (i - distance) // period == i // period
    ]
    return lax.ppermute(block, "z", route)


def over(block, axis):
    return lax.ppermute(block, axis, SWAP)


def across(block):
    return lax.ppermute(block, ("y", "x"), [(i, 3 - i) for i in range(4)])


def plane_step_one(block):
    return over(block, "x"), over(block, "y")


def plane_step_two(over_x, over_y):
    half = over_x.shape[0] // 2
    return over(over_y[:half], "x"), over(over_x[half:], "y")


def plane_join(*mine):
    return join(list(mine) + [over(part, "c") for part in mine])


def added_pair(one, two):
    return (one.astype(F32) + two.astype(F32)).astype(WIDE)


def landed(values, *flights):
    held = [getattr(holder, field) for holder, field in flights]
    values, held = lax.optimization_barrier((values, held))
    for (holder, field), value in zip(flights, held):
        setattr(holder, field, value)
    return values


def plane_sum_one(total):
    own = total.shape[0] // 4
    half = own // 2
    return over(total[3 * own : 3 * own + half], "x"), over(total[3 * own + half :], "y")


def plane_sum_two(total, top, bottom):
    own = total.shape[0] // 4
    half = own // 2
    wide = lambda a, b: (a.astype(F32) + b.astype(F32)).astype(WIDE)
    to_x = jnp.concatenate(
        [total[own : own + half], wide(total[own + half : 2 * own], bottom)], axis=0
    )
    to_y = jnp.concatenate(
        [wide(total[2 * own : 2 * own + half], top), total[2 * own + half : 3 * own]], axis=0
    )
    return over(to_x, "x"), over(to_y, "y")


def added(total, *parts):
    own = total.shape[0] // 4
    return sum((part.astype(F32) for part in parts), total[:own].astype(F32))


def kept_columns(block, first_y):
    half = block.shape[1] // 2
    keep = jnp.where(first_y, block[:, :half], block[:, half:])
    give = jnp.where(first_y, block[:, half:], block[:, :half])
    return keep, give


def both_rows(keep, got, first_y):
    return jnp.concatenate([jnp.where(first_y, keep, got), jnp.where(first_y, got, keep)], axis=0)


def share_columns(block, first_y, *after):
    keep, give = kept_columns(block, first_y)
    if after:
        give = tied(give, *after)
    return both_rows(keep, over(give, "y"), first_y)


class Unshare:
    def __init__(self, block, first_y):
        half = block.shape[0] // 2
        self.first_y = first_y
        self.keep = jnp.where(first_y, block[:half], block[half:])
        self.got = over(jnp.where(first_y, block[half:], block[:half]), "y")

    def both(self):
        return (
            jnp.where(self.first_y, self.keep, self.got),
            jnp.where(self.first_y, self.got, self.keep),
        )


class SpreadGather:
    def __init__(self, block, first_y):
        self.rows, self.first_y = block.shape[0], first_y
        whole = gather_z(block)
        half = whole.shape[1] // 2
        self.keep = jnp.where(first_y, whole[:, :half], whole[:, half:])
        self.got = over(jnp.where(first_y, whole[:, half:], whole[:, :half]), "y")

    def total(self):
        count, width = self.keep.shape[0] // self.rows, self.keep.shape[1]
        sides = [
            jnp.where(self.first_y, a, b).reshape(count, self.rows, width)
            for a, b in ((self.keep, self.got), (self.got, self.keep))
        ]
        return jnp.concatenate(sides, axis=1).reshape(2 * count * self.rows, width)


def spread_sum(term, rows, first_y):
    blocks = term.reshape(-1, 2, rows, term.shape[1])
    pick = lambda a, b: jnp.where(first_y, a, b).reshape(-1, term.shape[1])
    keep = pick(blocks[:, 0], blocks[:, 1])
    got = over(pick(blocks[:, 1], blocks[:, 0]), "y")
    both = jnp.where(
        first_y,
        jnp.concatenate([keep, got], axis=1),
        jnp.concatenate([got, keep], axis=1),
    )
    return both


def gather_z(block):
    return lax.all_gather(block, "z", axis=0, tiled=True)


def sum_z(block):
    return lax.psum_scatter(block.astype(WIDE), "z", scatter_dimension=0, tiled=True)


def padded(block, multiple=128):
    extra = -block.shape[1] % multiple
    return jnp.pad(block, ((0, 0), (0, extra))) if extra else block


def norm_back(gradient, normed, inverse, gain_vec):
    scaled = gradient * gain_vec
    return inverse * (scaled - normed * jnp.mean(scaled * normed, axis=-1, keepdims=True))


def per_device(
    inputs,
    segments,
    positions,
    gain_attn,
    query_weight,
    key_weight,
    value_weight,
    out_weight,
    gain_mlp,
    gate_weight,
    up_weight,
    down_weight,
    cotangent,
):
    own = inputs.shape[0]
    half, count = 4 * own, 8 * own
    length = segments.shape[0] // SEQS
    reach = (DOC_MOST - 2) // count + 1
    period = lax.axis_size("z")
    if length % count == 0:
        period = length // count
        reach = min(reach, period - 1)
    span = (reach + 1) * count
    z, y = lax.axis_index("z"), lax.axis_index("y")
    x, c = lax.axis_index("x"), lax.axis_index("c")
    first_y = y == 0

    w_q, w_k, w_v, w_g, w_u = [
        w.astype(WIDE) for w in (query_weight, key_weight, value_weight, gate_weight, up_weight)
    ]
    w_o, w_d = out_weight.T.astype(WIDE), down_weight.T.astype(WIDE)
    nq, nk, nf = w_q.shape[1] // 2, w_k.shape[1] // 2, w_g.shape[1] // 2
    rows_w = w_q.shape[0]
    halves = lambda w: (w[:, : w.shape[1] // 2], w[:, w.shape[1] // 2 :])
    gain_pair = jnp.stack([gain_attn, gain_mlp] * 2, 1).astype(WIDE)
    chunks = (slice(0, CHUNK), slice(CHUNK, nf))
    triple = lambda cut: jnp.concatenate(
        [padded(halves(w)[i][:, cut]) for i in range(2) for w in (w_d, w_g, w_u)], axis=1
    )
    flow_o = SpreadGather(w_o, first_y)
    near_a = share_columns(
        jnp.concatenate(
            [
                padded(jnp.concatenate([halves(w)[i] for w in (w_q, w_k, w_v, gain_pair)], axis=1))
                for i in range(2)
            ],
            axis=1,
        ),
        first_y,
    )
    full_a = gather_z(near_a)
    x_one = over(inputs, "x"), over(tied(inputs, near_a), "y")
    x_two = plane_step_two(*x_one)
    x_all = plane_join(inputs, *x_one, *x_two)
    near_c = [share_columns(triple(chunks[0]), first_y, x_all)]
    full_c = [gather_z(near_c[0])]
    first_gain = nq + 2 * nk
    gains = full_a[:, first_gain : first_gain + 2].astype(F32)
    gain_first, gain_second = gains[:, 0], gains[:, 1]

    other_positions = lax.ppermute(positions, "y", SWAP)
    token_positions = jnp.where(
        first_y,
        jnp.concatenate([positions, other_positions]),
        jnp.concatenate([other_positions, positions]),
    )
    frequency = rope_base ** (-(jnp.arange(HD // 2, dtype=F32) * 2.0 / HD))
    angles = frequency[:, None] * token_positions.astype(F32)[None, :]
    cos_tab, sin_tab = jnp.cos(angles), jnp.sin(angles)
    places = jnp.arange(8, dtype=jnp.int32)
    flips = places ^ (y * 4 + x * 2 + c).astype(jnp.int32)
    index = (flips % 2) * 4 + flips // 2
    padded_segs = jnp.concatenate([jnp.full((reach * count,), -1, jnp.int32), segments])
    key_segs = lax.dynamic_slice_in_dim(padded_segs, z * count, span, 0)
    query_segs = lax.dynamic_slice_in_dim(segments, z * count, count, 0)
    starts = jnp.sum((key_segs[:, None] < query_segs[None, :]).astype(jnp.int32), axis=0)
    first_rows = jnp.arange(count // BQ, dtype=jnp.int32) * BQ
    lo = starts[first_rows] // KB
    hi = (reach * count + first_rows + BQ + KB - 1) // KB
    full_lo = jnp.clip((starts[first_rows + BQ - 1] + KB - 1) // KB, lo, hi)
    full_hi = jnp.clip((reach * count + first_rows + 1) // KB, full_lo, hi)
    bounds = jnp.stack([lo, full_lo, full_hi, hi])
    own_key = reach * count
    own_bounds = jnp.maximum(bounds, own_key // KB)
    far_bounds = jnp.minimum(bounds, own_key // KB)
    starts = starts[None, :]

    h_one, qkv = project(x_all, gain_first[None, :], full_a)
    near_c.append(share_columns(triple(chunks[1]), first_y, qkv))
    full_c.append(gather_z(near_c[1]))
    turned = to_columns(qkv, index, cos_tab, sin_tab, GROUP + 1, GROUP + 2)
    q_cols, kv_own = turned[: GROUP * HD], turned[GROUP * HD :]
    far_kv = [shifted(kv_own, distance, period) for distance in range(reach, 0, -1)]
    far_kv = [shifted(kv_own, distance, period) for distance in range(reach, 0, -1)]
    kv_own = landed(kv_own, (flow_o, "got"))
    cot_one = plane_step_one(tied(cotangent, kv_own))
    own_part = attend(q_cols, kv_own, starts, own_bounds, (own_key, own_key), (), F32)
    own_part, far_kv, near_0 = lax.optimization_barrier((own_part, far_kv, near_c[0]))
    if reach:
        far_kv = jnp.concatenate(far_kv, axis=1)
        out_cols, logs = attend(q_cols, far_kv, starts, far_bounds, (own_key, 0), own_part, WIDE)
    else:
        out_cols, logs = own_part[0].astype(WIDE), own_part[1]
    out_cols, cot_one, _ = lax.optimization_barrier((out_cols, cot_one, near_c[1]))
    cot_two = plane_step_two(*cot_one)
    full_o = flow_o.total()
    attended = to_rows(out_cols, index, cos_tab, sin_tab, 0, GROUP, GROUP * HD)
    input_f32 = inputs.astype(F32)
    inverse_one = lax.rsqrt(jnp.mean(input_f32 * input_f32, axis=-1, keepdims=True) + eps)
    normed_one = input_f32 * inverse_one
    mid_got = over(dot(attended[half:], full_o, 1, 1).astype(WIDE), "c")
    mid_total = (dot(attended[:half], full_o, 1, 1) + mid_got.astype(F32)).astype(WIDE)
    mid_total, *cot_two = together(mid_total, *cot_two)
    mid_far = plane_sum_one(mid_total)
    mid_near = plane_sum_two(mid_total, *mid_far)
    grad_mix = plane_join(cotangent, *cot_one, *cot_two)
    x_mid = input_f32 + added(mid_total, *mid_near)

    inverse_two = lax.rsqrt(jnp.mean(x_mid * x_mid, axis=-1, keepdims=True) + eps)
    normed_two = x_mid * inverse_two
    h_own = (normed_two * gain_second).astype(WIDE)
    h_step = plane_step_one(h_own)
    h_two = plane_join(h_own, *h_step, *plane_step_two(*h_step))
    h_two, grad_mix = together(h_two, grad_mix)
    other_1 = hidden_units(h_two, grad_mix, full_c[0], half, half)
    mine_1 = hidden_units(h_two, grad_mix, full_c[0], 0, half)
    term_1 = unit_grads(h_two, grad_mix, mine_1[0], other_1[0])
    full_c[1], other_1, mine_1, term_1 = lax.optimization_barrier(
        (full_c[1], other_1, mine_1, term_1)
    )
    sums = [sum_z(term_1)]
    acts_other, back_other, out_other = hidden_units(
        h_two, grad_mix, full_c[1], half, half, other_1[1:]
    )
    back_got, out_got = over(back_other, "c"), over(out_other, "c")
    acts_mine, back_mine, out_mine = hidden_units(h_two, grad_mix, full_c[1], 0, half, mine_1[1:])
    back_total = added_pair(back_mine, back_got)
    back_far = plane_sum_one(back_total)
    term_2 = unit_grads(h_two, grad_mix, acts_mine, acts_other)
    back_near = plane_sum_two(back_total, *back_far)
    *back_near, term_2 = together(*back_near, term_2)
    sums.append(sum_z(term_2))
    grad_h_two = added(back_total, *back_near)
    grad_mid = cotangent.astype(F32) + norm_back(grad_h_two, normed_two, inverse_two, gain_second)
    branch_own = grad_mid.astype(WIDE)
    branch_one = plane_step_one(branch_own)
    branch_two = plane_step_two(*branch_one)
    out_total = added_pair(out_mine, out_got)
    grad_branch = plane_join(branch_own, *branch_one, *branch_two)
    grad_branch, out_total, sums[0] = together(grad_branch, out_total, sums[0])

    grad_attended = narrow(grad_branch, full_o)
    grad_cols = to_columns(grad_attended, index, cos_tab, sin_tab, 0, GROUP)
    grad_cols, out_total, sums[0] = together(grad_cols, out_total, sums[0])
    out_sends = [
        over(out_total[own : 2 * own], "x"),
        over(out_total[2 * own : 3 * own], "y"),
        across(out_total[3 * own :]),
    ]
    back = functools.partial(attend_back, q_cols)
    prior, far_got = (), []
    if reach:
        dq_far, dkv_far = back(
            far_kv, starts, far_bounds, (own_key, 0), out_cols, logs, grad_cols
        )
        prior = (dq_far,)
        far_got = [
            shifted(
                dkv_far[:, (reach - d) * count : (reach - d + 1) * count].astype(WIDE), -d, period
            )
            for d in range(1, reach + 1)
        ]
    dq_cols, dkv_cols = back(
        kv_own, starts, own_bounds, (own_key, own_key), out_cols, logs, grad_cols, prior
    )
    dkv_cols, out_sends, far_got = lax.optimization_barrier((dkv_cols, out_sends, far_got))
    output = (x_mid + added(out_total, *out_sends)).astype(WIDE)
    owned = [Unshare(tied(sums[0], dkv_cols), first_y)]
    dkv_own = sum((part.astype(F32) for part in far_got), dkv_cols)
    out_term = weight_grads(grad_branch, tied(attended, dkv_cols))
    dkv_own, out_term = landed((dkv_own, out_term), (owned[0], "got"))
    out_term = spread_sum(out_term, w_o.shape[0], first_y)
    grad_qkv = to_rows(
        jnp.concatenate([dq_cols, dkv_own], axis=0),
        index,
        cos_tab,
        sin_tab,
        GROUP + 1,
        GROUP + 2,
        full_a.shape[1],
    )
    qkv_part = weight_grads(h_one, grad_qkv)
    grad_qkv, qkv_part, out_term = together(grad_qkv, qkv_part, out_term)
    one_got = over(dot(grad_qkv[half:], full_a, 1, 1).astype(WIDE), "c")
    one_total = (dot(grad_qkv[:half], full_a, 1, 1) + one_got.astype(F32)).astype(WIDE)
    one_total, qkv_part, sums[1] = together(one_total, qkv_part, sums[1])
    qkv_grad = sum_z(qkv_part)
    owned.append(Unshare(sums[1], first_y))
    one_far = plane_sum_one(one_total)
    one_far = landed(one_far, (owned[1], "got"))
    one_near = plane_sum_two(one_total, *one_far)
    out_grad = sum_z(tied(out_term, qkv_grad))
    owned_a = Unshare(qkv_grad, first_y)
    *one_near, qkv_grad = together(*one_near, qkv_grad)
    grad_h_one = added(one_total, *one_near)
    input_grad = (grad_mid + norm_back(grad_h_one, normed_one, inverse_one, gain_first)).astype(
        WIDE
    )

    input_grad = landed(input_grad, (owned_a, "got"))
    owned = [part.both() for part in owned]
    kept = [CHUNK, nf - CHUNK]
    width = [full.shape[1] // 3 for full in full_c]

    def unit_columns(k):
        return jnp.concatenate(
            [
                owned[j][i][:, k * width[j] : k * width[j] + kept[j]]
                for i in range(2)
                for j in range(2)
            ],
            axis=1,
        ).astype(F32)

    down_out, gate_out, up_out = unit_columns(0).T, unit_columns(1), unit_columns(2)
    one, two = owned_a.both()
    pick = lambda a, b: jnp.concatenate([one[:, a:b], two[:, a:b]], axis=1).astype(F32)
    q_out, k_out, v_out = pick(0, nq), pick(nq, nq + nk), pick(nq + nk, nq + 2 * nk)

    def row_sums(weight, grad):
        return jnp.sum(weight.astype(F32) * grad, axis=1)

    gain_sums = jnp.stack(
        [
            row_sums(w_q, q_out) + row_sums(w_k, k_out) + row_sums(w_v, v_out),
            row_sums(w_g, gate_out) + row_sums(w_u, up_out),
        ]
    )
    gain_sums = gain_sums + lax.ppermute(gain_sums, "x", SWAP)
    gain_sums, out_grad = together(gain_sums, out_grad)
    gain_sums = gain_sums + lax.ppermute(gain_sums, "c", SWAP)
    o_out = out_grad.T.astype(F32)
    gain_one_out = gain_sums[0] / gain_attn.astype(WIDE).astype(F32)
    gain_two_out = gain_sums[1] / gain_mlp.astype(WIDE).astype(F32)
    return (
        output,
        input_grad,
        gain_one_out,
        q_out,
        k_out,
        v_out,
        o_out,
        gain_two_out,
        gate_out,
        up_out,
        down_out,
    )


def solution(mesh):
    seq, tensor = mesh.shape["seq"], mesh.shape["tensor"]
    grid = Mesh(
        mesh.devices.reshape(seq // 2, 2, tensor // 2, 2), ("z", "y", "x", "c")
    )
    rows, cols = ("z", "y"), ("x", "c")
    tokens, weight, weight_t = P(rows + cols, None), P(rows, cols), P(cols, rows)
    in_specs = (
        tokens,
        P(),
        P(rows),
        P(rows),
        weight,
        weight,
        weight,
        weight_t,
        P(rows),
        weight,
        weight,
        weight_t,
        tokens,
    )
    out_specs = (
        tokens,
        tokens,
        P(rows),
        weight,
        weight,
        weight,
        weight_t,
        P(rows),
        weight,
        weight,
        weight_t,
    )
    return jax.shard_map(
        per_device, mesh=grid, in_specs=in_specs, out_specs=out_specs, check_vma=False
    )
```

```python
import functools

import jax
import jax.numpy as jnp
from jax import lax
from jax.experimental import pallas as pl
from jax.experimental.pallas import tpu as pltpu
from jax.sharding import Mesh
from jax.sharding import PartitionSpec as P

HEADS = 32
KV = 8
HD = 80
SEQS = 2
DOC_MOST = 2000
GROUP = HEADS // KV

eps = 1e-05
rope_base = 10000.0
LOG2E = 1.4426950408889634
SCORE_LOG2 = HD ** (-0.5) * LOG2E
SCORE_SCALE = HD ** (-0.5)
LOW = -1e30
BQ = 256
CHUNK = 384
KB = 256
WIDE = jnp.bfloat16
F32 = jnp.float32
VMEM_BYTES = 48 * 1024 * 1024

SWAP = [(0, 1), (1, 0)]


def dot(a, b, ca, cb):
    return lax.dot_general(a, b, (((ca,), (cb,)), ((), ())), preferred_element_type=F32)


def turn_kernel(rotary, heads, index_ref, rows_ref, cos_ref, sin_ref, out_ref):
    own = rows_ref.shape[0] // 8
    half = HD // 2
    for pair in range(4):
        parts = [
            rows_ref[pl.ds(pl.multiple_of(index_ref[2 * pair + k] * own, own), own), :].astype(F32)
            for k in range(2)
        ]
        turned = jnp.concatenate(parts, axis=0).T
        lanes = slice(pair * 2 * own, (pair + 1) * 2 * own)
        cos_tab, sin_tab = cos_ref[:, lanes], sin_ref[:, lanes]
        for h in range(heads):
            front, back = turned[h * HD : h * HD + half], turned[h * HD + half : (h + 1) * HD]
            if h < rotary:
                front, back = front * cos_tab - back * sin_tab, back * cos_tab + front * sin_tab
            out_ref[h * HD : (h + 1) * HD, lanes] = jnp.concatenate([front, back], axis=0).astype(
                out_ref.dtype
            )


def to_columns(rows, index, cos_tab, sin_tab, rotary, heads):
    count = rows.shape[0]
    full = lambda shape: pl.BlockSpec(shape, lambda i, s: (0, 0))
    return pl.pallas_call(
        functools.partial(turn_kernel, rotary, heads),
        grid_spec=pltpu.PrefetchScalarGridSpec(
            num_scalar_prefetch=1,
            grid=(1,),
            in_specs=[full(rows.shape), full(cos_tab.shape), full(sin_tab.shape)],
            out_specs=full((heads * HD, count)),
        ),
        out_shape=jax.ShapeDtypeStruct((heads * HD, count), WIDE),
        compiler_params=pltpu.CompilerParams(vmem_limit_bytes=VMEM_BYTES),
        cost_estimate=pl.CostEstimate(flops=10**6, bytes_accessed=10**5, transcendentals=0),
    )(index, rows, cos_tab, sin_tab)


def back_kernel(rotary, heads, index_ref, cols_ref, cos_ref, sin_ref, out_ref):
    own = cols_ref.shape[1] // 8
    half = HD // 2
    width = out_ref.shape[1]
    for pair in range(4):
        lanes = slice(pair * 2 * own, (pair + 1) * 2 * own)
        cos_tab, sin_tab = cos_ref[:, lanes], sin_ref[:, lanes]
        parts = []
        for h in range(heads):
            front = cols_ref[h * HD : h * HD + half, lanes].astype(F32)
            back = cols_ref[h * HD + half : (h + 1) * HD, lanes].astype(F32)
            if h < rotary:
                front, back = front * cos_tab + back * sin_tab, back * cos_tab - front * sin_tab
            parts += [front, back]
        if width > heads * HD:
            parts.append(jnp.zeros((width - heads * HD, 2 * own), F32))
        rows = jnp.concatenate(parts, axis=0).T.astype(out_ref.dtype)
        for k in range(2):
            first = pl.multiple_of(index_ref[2 * pair + k] * own, own)
            out_ref[pl.ds(first, own), :] = rows[k * own : (k + 1) * own]


def to_rows(cols, index, cos_tab, sin_tab, rotary, heads, width):
    count = cols.shape[1]
    full = lambda shape: pl.BlockSpec(shape, lambda i, s: (0, 0))
    return pl.pallas_call(
        functools.partial(back_kernel, rotary, heads),
        grid_spec=pltpu.PrefetchScalarGridSpec(
            num_scalar_prefetch=1,
            grid=(1,),
            in_specs=[full(cols.shape), full(cos_tab.shape), full(sin_tab.shape)],
            out_specs=full((count, width)),
        ),
        out_shape=jax.ShapeDtypeStruct((count, width), WIDE),
        compiler_params=pltpu.CompilerParams(vmem_limit_bytes=VMEM_BYTES),
        cost_estimate=pl.CostEstimate(flops=10**6, bytes_accessed=10**5, transcendentals=0),
    )(index, cols, cos_tab, sin_tab)


def allowed_mask(block, starts, own_places):
    places = block * KB + lax.broadcasted_iota(jnp.int32, (KB, 1), 0)
    return (places >= starts) & (places <= own_places)


def attend_kernel(places, bounds_ref, q_ref, kv_ref, start_ref, *refs):
    first_query, first_key = places
    *prior, out_ref, log_ref, k_rows, acc = refs
    step = pl.program_id(0)
    span = kv_ref.shape[1]

    @pl.when(step == 0)
    def _():
        for j in range(span // KB):
            k_rows[j * KB : (j + 1) * KB, :] = (
                kv_ref[0:HD, j * KB : (j + 1) * KB].astype(F32).T.astype(WIDE)
            )

    starts = start_ref[0:1, :]
    own_places = first_query + step * BQ + lax.broadcasted_iota(jnp.int32, (1, BQ), 1)
    if prior:
        for h in range(GROUP):
            acc[h] = prior[0][h * HD : (h + 1) * HD, :]
    else:
        acc[...] = jnp.zeros_like(acc)

    def one(masked, block, carry):
        first = pl.multiple_of(block * KB - first_key, KB)
        keys = k_rows[pl.ds(first, KB), :]
        values = kv_ref[HD : 2 * HD, pl.ds(first, KB)]
        if masked:
            mask = allowed_mask(block, starts, own_places)
        fresh = []
        for h in range(GROUP):
            top, total = carry[2 * h], carry[2 * h + 1]
            scores = dot(keys, q_ref[h * HD : (h + 1) * HD, :], 1, 0) * SCORE_LOG2
            if masked:
                scores = jnp.where(mask, scores, LOW)
            new_top = jnp.maximum(top, jnp.max(scores, axis=0, keepdims=True))
            probs = jnp.exp2(scores - new_top)
            fade = jnp.exp2(top - new_top)
            total = fade * total + jnp.sum(probs, axis=0, keepdims=True)
            acc[h] = fade * acc[h] + dot(values, probs.astype(WIDE), 1, 0)
            fresh += [new_top, total]
        return tuple(fresh)

    carry = (jnp.full((1, BQ), LOW, F32), jnp.zeros((1, BQ), F32)) * GROUP
    if prior:
        carry = sum(((prior[1][h : h + 1, :], jnp.ones((1, BQ), F32)) for h in range(GROUP)), ())
    lo, full_lo, full_hi, hi = [bounds_ref[k, step] for k in range(4)]
    carry = lax.fori_loop(lo, full_lo, functools.partial(one, True), carry)
    carry = lax.fori_loop(full_lo, full_hi, functools.partial(one, False), carry)
    carry = lax.fori_loop(full_hi, hi, functools.partial(one, True), carry)
    for h in range(GROUP):
        top, total = carry[2 * h], carry[2 * h + 1]
        out_ref[h * HD : (h + 1) * HD, :] = (acc[h] / total).astype(out_ref.dtype)
        log_ref[h : h + 1, :] = top + jnp.log2(total)


def attend(q_cols, kv_cols, starts, bounds, places, prior, out_type):
    count, span = q_cols.shape[1], kv_cols.shape[1]
    wide_block = pl.BlockSpec((GROUP * HD, BQ), lambda i, s: (0, i))
    log_block = pl.BlockSpec((8, BQ), lambda i, s: (0, i))
    return pl.pallas_call(
        functools.partial(attend_kernel, places),
        grid_spec=pltpu.PrefetchScalarGridSpec(
            num_scalar_prefetch=1,
            grid=(count // BQ,),
            in_specs=[
                wide_block,
                pl.BlockSpec((2 * HD, span), lambda i, s: (0, 0)),
                pl.BlockSpec((1, BQ), lambda i, s: (0, i)),
            ]
            + [wide_block, log_block][: len(prior)],
            out_specs=[wide_block, log_block],
            scratch_shapes=[pltpu.VMEM((span, HD), WIDE), pltpu.VMEM((GROUP, HD, BQ), F32)],
        ),
        out_shape=[
            jax.ShapeDtypeStruct((GROUP * HD, count), out_type),
            jax.ShapeDtypeStruct((8, count), F32),
        ],
        compiler_params=pltpu.CompilerParams(vmem_limit_bytes=VMEM_BYTES),
        cost_estimate=pl.CostEstimate(flops=10**6, bytes_accessed=10**5, transcendentals=0),
    )(bounds, q_cols, kv_cols, starts, *prior)


def attend_back_kernel(places, bounds_ref, q_ref, kv_ref, start_ref, out_ref, log_ref, grad_ref, *refs):
    first_query, first_key = places
    *prior, dq_ref, dkv_ref, k_rows, v_rows, q_rows, g_rows, dk, dv, probs_all, grads_all, dq = refs
    step = pl.program_id(0)
    span = kv_ref.shape[1]

    @pl.when(step == 0)
    def _():
        for j in range(span // KB):
            lanes = slice(j * KB, (j + 1) * KB)
            k_rows[lanes, :] = kv_ref[0:HD, lanes].astype(F32).T.astype(WIDE)
            v_rows[lanes, :] = kv_ref[HD : 2 * HD, lanes].astype(F32).T.astype(WIDE)
        dk[...] = jnp.zeros_like(dk)
        dv[...] = jnp.zeros_like(dv)

    starts = start_ref[0:1, :]
    own_places = first_query + step * BQ + lax.broadcasted_iota(jnp.int32, (1, BQ), 1)
    dq[...] = jnp.zeros_like(dq)
    deltas = []
    for h in range(GROUP):
        part = slice(h * HD, (h + 1) * HD)
        q_f32, g_f32 = q_ref[part, :].astype(F32), grad_ref[part, :].astype(F32)
        q_rows[h * BQ : (h + 1) * BQ, :] = q_f32.T.astype(WIDE)
        g_rows[h * BQ : (h + 1) * BQ, :] = g_f32.T.astype(WIDE)
        deltas.append(jnp.sum(g_f32 * out_ref[part, :].astype(F32), axis=0, keepdims=True))

    def one(masked, block, carry):
        first = pl.multiple_of(block * KB - first_key, KB)
        rows = pl.ds(first, KB)
        keys, values = k_rows[rows, :], v_rows[rows, :]
        key_cols = kv_ref[0:HD, rows]
        if masked:
            mask = allowed_mask(block, starts, own_places)
        for h in range(GROUP):
            part = slice(h * HD, (h + 1) * HD)
            lanes = slice(h * BQ, (h + 1) * BQ)
            scores = dot(keys, q_ref[part, :], 1, 0) * SCORE_LOG2 - log_ref[h : h + 1, :]
            if masked:
                scores = jnp.where(mask, scores, LOW)
            probs = jnp.exp2(scores)
            grad_probs = dot(values, grad_ref[part, :], 1, 0)
            grad_scores = (probs * (grad_probs - deltas[h])).astype(WIDE)
            probs_all[:, lanes] = probs.astype(WIDE)
            grads_all[:, lanes] = grad_scores
            dq[h] += dot(key_cols, grad_scores, 1, 0)
        dv[rows, :] += dot(probs_all[...], g_rows[...], 1, 0)
        dk[rows, :] += dot(grads_all[...], q_rows[...], 1, 0)
        return carry

    lo, full_lo, full_hi, hi = [bounds_ref[k, step] for k in range(4)]
    lax.fori_loop(lo, full_lo, functools.partial(one, True), 0)
    lax.fori_loop(full_lo, full_hi, functools.partial(one, False), 0)
    lax.fori_loop(full_hi, hi, functools.partial(one, True), 0)
    for h in range(GROUP):
        part = slice(h * HD, (h + 1) * HD)
        dq_ref[part, :] = dq[h] * SCORE_SCALE + (prior[0][part, :] if prior else 0.0)

    @pl.when(step == pl.num_programs(0) - 1)
    def _():
        for j in range(span // KB):
            lanes = slice(j * KB, (j + 1) * KB)
            dkv_ref[0:HD, lanes] = dk[lanes, :].T * SCORE_SCALE
            dkv_ref[HD : 2 * HD, lanes] = dv[lanes, :].T


def attend_back(q_cols, kv_cols, starts, bounds, places, out_cols, logs, grad_cols, prior=()):
    count, span = q_cols.shape[1], kv_cols.shape[1]
    wide_block = pl.BlockSpec((GROUP * HD, BQ), lambda i, s: (0, i))
    return pl.pallas_call(
        functools.partial(attend_back_kernel, places),
        grid_spec=pltpu.PrefetchScalarGridSpec(
            num_scalar_prefetch=1,
            grid=(count // BQ,),
            in_specs=[
                wide_block,
                pl.BlockSpec((2 * HD, span), lambda i, s: (0, 0)),
                pl.BlockSpec((1, BQ), lambda i, s: (0, i)),
                wide_block,
                pl.BlockSpec((8, BQ), lambda i, s: (0, i)),
                wide_block,
            ]
            + [wide_block] * len(prior),
            out_specs=[wide_block, pl.BlockSpec((2 * HD, span), lambda i, s: (0, 0))],
            scratch_shapes=[
                pltpu.VMEM((span, HD), WIDE),
                pltpu.VMEM((span, HD), WIDE),
                pltpu.VMEM((GROUP * BQ, HD), WIDE),
                pltpu.VMEM((GROUP * BQ, HD), WIDE),
                pltpu.VMEM((span, HD), F32),
                pltpu.VMEM((span, HD), F32),
                pltpu.VMEM((KB, GROUP * BQ), WIDE),
                pltpu.VMEM((KB, GROUP * BQ), WIDE),
                pltpu.VMEM((GROUP, HD, BQ), F32),
            ],
        ),
        out_shape=[
            jax.ShapeDtypeStruct((GROUP * HD, count), F32),
            jax.ShapeDtypeStruct((2 * HD, span), F32),
        ],
        compiler_params=pltpu.CompilerParams(vmem_limit_bytes=VMEM_BYTES),
        cost_estimate=pl.CostEstimate(flops=10**6, bytes_accessed=10**5, transcendentals=0),
    )(bounds, q_cols, kv_cols, starts, out_cols, logs, grad_cols, *prior)


TINY = pl.CostEstimate(flops=10**6, bytes_accessed=10**5, transcendentals=0)
ANY = pl.BlockSpec(memory_space=pl.ANY)


def params():
    return pltpu.CompilerParams(vmem_limit_bytes=VMEM_BYTES)


def join_kernel(*refs):
    *parts, out, whole, sems = refs
    pairs, first = [], 0
    for k, part in enumerate(parts):
        rows = pl.ds(first, part.shape[0])
        pairs.append(
            (
                pltpu.make_async_copy(part, whole.at[rows, :], sems.at[0, k]),
                pltpu.make_async_copy(whole.at[rows, :], out.at[rows, :], sems.at[1, k]),
            )
        )
        first += part.shape[0]
    for copy_in, _ in pairs:
        copy_in.start()
    for copy_in, copy_out in pairs:
        copy_in.wait()
        copy_out.start()
    for _, copy_out in pairs:
        copy_out.wait()


def join(parts):
    rows = sum(part.shape[0] for part in parts)
    return pl.pallas_call(
        join_kernel,
        in_specs=[ANY] * len(parts),
        out_specs=ANY,
        out_shape=jax.ShapeDtypeStruct((rows, parts[0].shape[1]), parts[0].dtype),
        scratch_shapes=[
            pltpu.VMEM((rows, parts[0].shape[1]), parts[0].dtype),
            pltpu.SemaphoreType.DMA((2, len(parts))),
        ],
        compiler_params=params(),
        cost_estimate=TINY,
    )(*parts)


def project_kernel(x_ref, gain_ref, weight_ref, h_ref, out_ref):
    x = x_ref[...].astype(F32)
    inverse = lax.rsqrt(jnp.mean(x * x, axis=-1, keepdims=True) + eps)
    h = (x * inverse * gain_ref[...]).astype(WIDE)
    h_ref[...] = h
    out_ref[...] = dot(h, weight_ref[...], 1, 0)


def project(x_all, gain_row, weights, rows=256):
    count, model = x_all.shape
    width = weights.shape[1]
    return pl.pallas_call(
        project_kernel,
        grid=(count // rows,),
        in_specs=[
            pl.BlockSpec((rows, model), lambda i: (i, 0)),
            pl.BlockSpec((1, model), lambda i: (0, 0)),
            pl.BlockSpec(weights.shape, lambda i: (0, 0), pipeline_mode=pl.Buffered(1)),
        ],
        out_specs=[
            pl.BlockSpec((rows, model), lambda i: (i, 0)),
            pl.BlockSpec((rows, width), lambda i: (i, 0)),
        ],
        out_shape=[
            jax.ShapeDtypeStruct((count, model), WIDE),
            jax.ShapeDtypeStruct((count, width), F32),
        ],
        compiler_params=pltpu.CompilerParams(vmem_limit_bytes=VMEM_BYTES),
        cost_estimate=pl.CostEstimate(flops=10**6, bytes_accessed=10**5, transcendentals=0),
    )(x_all, gain_row, weights)


def narrow_kernel(a_ref, weight_ref, out_ref):
    out_ref[...] = dot(a_ref[...], weight_ref[...], 1, 0).astype(out_ref.dtype)


def whole(array):
    return pl.BlockSpec(array.shape, lambda i: (0, 0), pipeline_mode=pl.Buffered(1))


def narrow(a, weight, rows=256):
    count, model = a.shape
    return pl.pallas_call(
        narrow_kernel,
        grid=(count // rows,),
        in_specs=[pl.BlockSpec((rows, model), lambda i: (i, 0)), whole(weight)],
        out_specs=pl.BlockSpec((rows, weight.shape[1]), lambda i: (i, 0)),
        out_shape=jax.ShapeDtypeStruct((count, weight.shape[1]), WIDE),
        compiler_params=params(),
        cost_estimate=TINY,
    )(a, weight)


def units_kernel(has_prior, h_ref, cot_ref, weight_ref, *refs):
    *prior, acts_ref, back_ref, out_ref = refs
    width = weight_ref.shape[1] // 3
    down_w, gate_w, up_w = [weight_ref[:, k * width : (k + 1) * width] for k in range(3)]
    gate = dot(h_ref[...], gate_w, 1, 0)
    up = dot(h_ref[...], up_w, 1, 0)
    grad = dot(cot_ref[...], down_w, 1, 0)
    sigma = 1.0 / (1.0 + jnp.exp(-gate))
    silu = gate * sigma
    hidden = (silu * up).astype(WIDE)
    grad_gate = (grad * up * sigma * (1.0 + gate * (1.0 - sigma))).astype(WIDE)
    grad_up = (grad * silu).astype(WIDE)
    acts_ref[:, :width] = hidden
    acts_ref[:, width : 2 * width] = grad_gate
    acts_ref[:, 2 * width :] = grad_up
    back = dot(grad_gate, gate_w, 1, 1) + dot(grad_up, up_w, 1, 1)
    out = dot(hidden, down_w, 1, 1)
    if has_prior:
        back, out = back + prior[0][...].astype(F32), out + prior[1][...].astype(F32)
    back_ref[...] = back.astype(WIDE)
    out_ref[...] = out.astype(WIDE)


def hidden_units(h_two, cot, weights, first, count, prior=(), rows=256):
    model, width = h_two.shape[1], weights.shape[1]
    at = first // rows
    block = lambda n: pl.BlockSpec((rows, n), lambda i: (i, 0))
    shape = lambda n: jax.ShapeDtypeStruct((count, n), WIDE)
    return pl.pallas_call(
        functools.partial(units_kernel, bool(prior)),
        grid=(count // rows,),
        in_specs=[pl.BlockSpec((rows, model), lambda i: (i + at, 0))] * 2
        + [whole(weights)]
        + [block(model)] * len(prior),
        out_specs=[block(width), block(model), block(model)],
        out_shape=[shape(width), shape(model), shape(model)],
        compiler_params=params(),
        cost_estimate=TINY,
    )(h_two, cot, weights, *prior)


def unit_grads_kernel(h_ref, cot_ref, mine_ref, other_ref, out_ref):
    half, width = mine_ref.shape[0], mine_ref.shape[1] // 3
    for a_ref, columns in ((cot_ref, slice(0, width)), (h_ref, slice(width, 3 * width))):
        out_ref[:, columns] = (
            dot(a_ref[:half, :], mine_ref[:, columns], 0, 0)
            + dot(a_ref[half:, :], other_ref[:, columns], 0, 0)
        ).astype(WIDE)


def unit_grads(h_two, cot, mine, other, rows=256):
    count, model = h_two.shape
    width = mine.shape[1]
    return pl.pallas_call(
        unit_grads_kernel,
        grid=(model // rows,),
        in_specs=[pl.BlockSpec((count, rows), lambda i: (0, i))] * 2 + [whole(mine), whole(other)],
        out_specs=pl.BlockSpec((rows, width), lambda i: (i, 0)),
        out_shape=jax.ShapeDtypeStruct((model, width), WIDE),
        compiler_params=params(),
        cost_estimate=TINY,
    )(h_two, cot, mine, other)


def grads_kernel(a_ref, b_ref, out_ref):
    out_ref[...] = dot(a_ref[...], b_ref[...], 0, 0).astype(WIDE)


def weight_grads(a, b, rows=256):
    count, model = a.shape
    width = b.shape[1]
    return pl.pallas_call(
        grads_kernel,
        grid=(model // rows,),
        in_specs=[pl.BlockSpec((count, rows), lambda i: (0, i)), whole(b)],
        out_specs=pl.BlockSpec((rows, width), lambda i: (i, 0)),
        out_shape=jax.ShapeDtypeStruct((model, width), WIDE),
        compiler_params=params(),
        cost_estimate=TINY,
    )(a, b)


def tied(value, *others):
    return lax.optimization_barrier((value, *others))[0]


def together(*values):
    return lax.optimization_barrier(values)


def shifted(block, distance, period):
    count = lax.axis_size("z")
    route = [
        (i - distance, i)
        for i in range(count)
        if 0 <= i - distance < count and (i - distance) // period == i // period
    ]
    return lax.ppermute(block, "z", route)


def over(block, axis):
    return lax.ppermute(block, axis, SWAP)


def across(block):
    return lax.ppermute(block, ("y", "x"), [(i, 3 - i) for i in range(4)])


def plane_step_one(block):
    return over(block, "x"), over(block, "y")


def plane_step_two(over_x, over_y):
    half = over_x.shape[0] // 2
    return over(over_y[:half], "x"), over(over_x[half:], "y")


def plane_join(*mine):
    return join(list(mine) + [over(part, "c") for part in mine])


def added_pair(one, two):
    return (one.astype(F32) + two.astype(F32)).astype(WIDE)


def landed(values, *flights):
    held = [getattr(holder, field) for holder, field in flights]
    values, held = lax.optimization_barrier((values, held))
    for (holder, field), value in zip(flights, held):
        setattr(holder, field, value)
    return values


def plane_sum_one(total):
    own = total.shape[0] // 4
    half = own // 2
    return over(total[3 * own : 3 * own + half], "x"), over(total[3 * own + half :], "y")


def plane_sum_two(total, top, bottom):
    own = total.shape[0] // 4
    half = own // 2
    wide = lambda a, b: (a.astype(F32) + b.astype(F32)).astype(WIDE)
    to_x = jnp.concatenate(
        [total[own : own + half], wide(total[own + half : 2 * own], bottom)], axis=0
    )
    to_y = jnp.concatenate(
        [wide(total[2 * own : 2 * own + half], top), total[2 * own + half : 3 * own]], axis=0
    )
    return over(to_x, "x"), over(to_y, "y")


def added(total, *parts):
    own = total.shape[0] // 4
    return sum((part.astype(F32) for part in parts), total[:own].astype(F32))


def kept_columns(block, first_y):
    half = block.shape[1] // 2
    keep = jnp.where(first_y, block[:, :half], block[:, half:])
    give = jnp.where(first_y, block[:, half:], block[:, :half])
    return keep, give


def both_rows(keep, got, first_y):
    return jnp.concatenate([jnp.where(first_y, keep, got), jnp.where(first_y, got, keep)], axis=0)


def share_columns(block, first_y, *after):
    keep, give = kept_columns(block, first_y)
    if after:
        give = tied(give, *after)
    return both_rows(keep, over(give, "y"), first_y)


class Unshare:
    def __init__(self, block, first_y):
        half = block.shape[0] // 2
        self.first_y = first_y
        self.keep = jnp.where(first_y, block[:half], block[half:])
        self.got = over(jnp.where(first_y, block[half:], block[:half]), "y")

    def both(self):
        return (
            jnp.where(self.first_y, self.keep, self.got),
            jnp.where(self.first_y, self.got, self.keep),
        )


class SpreadGather:
    def __init__(self, block, first_y):
        self.rows, self.first_y = block.shape[0], first_y
        whole = gather_z(block)
        half = whole.shape[1] // 2
        self.keep = jnp.where(first_y, whole[:, :half], whole[:, half:])
        self.got = over(jnp.where(first_y, whole[:, half:], whole[:, :half]), "y")

    def total(self):
        count, width = self.keep.shape[0] // self.rows, self.keep.shape[1]
        sides = [
            jnp.where(self.first_y, a, b).reshape(count, self.rows, width)
            for a, b in ((self.keep, self.got), (self.got, self.keep))
        ]
        return jnp.concatenate(sides, axis=1).reshape(2 * count * self.rows, width)


def spread_sum(term, rows, first_y):
    blocks = term.reshape(-1, 2, rows, term.shape[1])
    pick = lambda a, b: jnp.where(first_y, a, b).reshape(-1, term.shape[1])
    keep = pick(blocks[:, 0], blocks[:, 1])
    got = over(pick(blocks[:, 1], blocks[:, 0]), "y")
    both = jnp.where(
        first_y,
        jnp.concatenate([keep, got], axis=1),
        jnp.concatenate([got, keep], axis=1),
    )
    return both


def gather_z(block):
    return lax.all_gather(block, "z", axis=0, tiled=True)


def sum_z(block):
    return lax.psum_scatter(block.astype(WIDE), "z", scatter_dimension=0, tiled=True)


def padded(block, multiple=128):
    extra = -block.shape[1] % multiple
    return jnp.pad(block, ((0, 0), (0, extra))) if extra else block


def norm_back(gradient, normed, inverse, gain_vec):
    scaled = gradient * gain_vec
    return inverse * (scaled - normed * jnp.mean(scaled * normed, axis=-1, keepdims=True))


def per_device(
    inputs,
    segments,
    positions,
    gain_attn,
    query_weight,
    key_weight,
    value_weight,
    out_weight,
    gain_mlp,
    gate_weight,
    up_weight,
    down_weight,
    cotangent,
):
    own = inputs.shape[0]
    half, count = 4 * own, 8 * own
    length = segments.shape[0] // SEQS
    reach = (DOC_MOST - 2) // count + 1
    period = lax.axis_size("z")
    if length % count == 0:
        period = length // count
        reach = min(reach, period - 1)
    span = (reach + 1) * count
    z, y = lax.axis_index("z"), lax.axis_index("y")
    x, c = lax.axis_index("x"), lax.axis_index("c")
    first_y = y == 0

    w_q, w_k, w_v, w_g, w_u = [
        w.astype(WIDE) for w in (query_weight, key_weight, value_weight, gate_weight, up_weight)
    ]
    w_o, w_d = out_weight.T.astype(WIDE), down_weight.T.astype(WIDE)
    nq, nk, nf = w_q.shape[1] // 2, w_k.shape[1] // 2, w_g.shape[1] // 2
    rows_w = w_q.shape[0]
    halves = lambda w: (w[:, : w.shape[1] // 2], w[:, w.shape[1] // 2 :])
    gain_pair = jnp.stack([gain_attn, gain_mlp] * 2, 1).astype(WIDE)
    chunks = (slice(0, CHUNK), slice(CHUNK, nf))
    triple = lambda cut: jnp.concatenate(
        [padded(halves(w)[i][:, cut]) for i in range(2) for w in (w_d, w_g, w_u)], axis=1
    )
    flow_o = SpreadGather(w_o, first_y)
    near_a = share_columns(
        jnp.concatenate(
            [
                padded(jnp.concatenate([halves(w)[i] for w in (w_q, w_k, w_v, gain_pair)], axis=1))
                for i in range(2)
            ],
            axis=1,
        ),
        first_y,
    )
    full_a = gather_z(near_a)
    x_one = over(inputs, "x"), over(tied(inputs, near_a), "y")
    x_two = plane_step_two(*x_one)
    x_all = plane_join(inputs, *x_one, *x_two)
    near_c = [share_columns(triple(chunks[0]), first_y, x_all)]
    full_c = [gather_z(near_c[0])]
    first_gain = nq + 2 * nk
    gains = full_a[:, first_gain : first_gain + 2].astype(F32)
    gain_first, gain_second = gains[:, 0], gains[:, 1]

    other_positions = lax.ppermute(positions, "y", SWAP)
    token_positions = jnp.where(
        first_y,
        jnp.concatenate([positions, other_positions]),
        jnp.concatenate([other_positions, positions]),
    )
    frequency = rope_base ** (-(jnp.arange(HD // 2, dtype=F32) * 2.0 / HD))
    angles = frequency[:, None] * token_positions.astype(F32)[None, :]
    cos_tab, sin_tab = jnp.cos(angles), jnp.sin(angles)
    places = jnp.arange(8, dtype=jnp.int32)
    flips = places ^ (y * 4 + x * 2 + c).astype(jnp.int32)
    index = (flips % 2) * 4 + flips // 2
    padded_segs = jnp.concatenate([jnp.full((reach * count,), -1, jnp.int32), segments])
    key_segs = lax.dynamic_slice_in_dim(padded_segs, z * count, span, 0)
    query_segs = lax.dynamic_slice_in_dim(segments, z * count, count, 0)
    starts = jnp.sum((key_segs[:, None] < query_segs[None, :]).astype(jnp.int32), axis=0)
    first_rows = jnp.arange(count // BQ, dtype=jnp.int32) * BQ
    lo = starts[first_rows] // KB
    hi = (reach * count + first_rows + BQ + KB - 1) // KB
    full_lo = jnp.clip((starts[first_rows + BQ - 1] + KB - 1) // KB, lo, hi)
    full_hi = jnp.clip((reach * count + first_rows + 1) // KB, full_lo, hi)
    bounds = jnp.stack([lo, full_lo, full_hi, hi])
    own_key = reach * count
    own_bounds = jnp.maximum(bounds, own_key // KB)
    far_bounds = jnp.minimum(bounds, own_key // KB)
    starts = starts[None, :]

    h_one, qkv = project(x_all, gain_first[None, :], full_a)
    near_c.append(share_columns(triple(chunks[1]), first_y, qkv))
    full_c.append(gather_z(near_c[1]))
    turned = to_columns(qkv, index, cos_tab, sin_tab, GROUP + 1, GROUP + 2)
    q_cols, kv_own = turned[: GROUP * HD], turned[GROUP * HD :]
    far_kv = [shifted(kv_own, distance, period) for distance in range(reach, 0, -1)]
    far_kv = [shifted(kv_own, distance, period) for distance in range(reach, 0, -1)]
    kv_own = landed(kv_own, (flow_o, "got"))
    cot_one = plane_step_one(tied(cotangent, kv_own))
    own_part = attend(q_cols, kv_own, starts, own_bounds, (own_key, own_key), (), F32)
    own_part, far_kv, near_0 = lax.optimization_barrier((own_part, far_kv, near_c[0]))
    if reach:
        far_kv = jnp.concatenate(far_kv, axis=1)
        out_cols, logs = attend(q_cols, far_kv, starts, far_bounds, (own_key, 0), own_part, WIDE)
    else:
        out_cols, logs = own_part[0].astype(WIDE), own_part[1]
    out_cols, cot_one, _ = lax.optimization_barrier((out_cols, cot_one, near_c[1]))
    cot_two = plane_step_two(*cot_one)
    full_o = flow_o.total()
    attended = to_rows(out_cols, index, cos_tab, sin_tab, 0, GROUP, GROUP * HD)
    input_f32 = inputs.astype(F32)
    inverse_one = lax.rsqrt(jnp.mean(input_f32 * input_f32, axis=-1, keepdims=True) + eps)
    normed_one = input_f32 * inverse_one
    mid_got = over(dot(attended[half:], full_o, 1, 1).astype(WIDE), "c")
    mid_total = (dot(attended[:half], full_o, 1, 1) + mid_got.astype(F32)).astype(WIDE)
    mid_total, *cot_two = together(mid_total, *cot_two)
    mid_far = plane_sum_one(mid_total)
    mid_near = plane_sum_two(mid_total, *mid_far)
    grad_mix = plane_join(cotangent, *cot_one, *cot_two)
    x_mid = input_f32 + added(mid_total, *mid_near)

    inverse_two = lax.rsqrt(jnp.mean(x_mid * x_mid, axis=-1, keepdims=True) + eps)
    normed_two = x_mid * inverse_two
    h_own = (normed_two * gain_second).astype(WIDE)
    h_step = plane_step_one(h_own)
    h_two = plane_join(h_own, *h_step, *plane_step_two(*h_step))
    h_two, grad_mix = together(h_two, grad_mix)
    other_1 = hidden_units(h_two, grad_mix, full_c[0], half, half)
    mine_1 = hidden_units(h_two, grad_mix, full_c[0], 0, half)
    term_1 = unit_grads(h_two, grad_mix, mine_1[0], other_1[0])
    full_c[1], other_1, mine_1, term_1 = lax.optimization_barrier(
        (full_c[1], other_1, mine_1, term_1)
    )
    sums = [sum_z(term_1)]
    acts_other, back_other, out_other = hidden_units(
        h_two, grad_mix, full_c[1], half, half, other_1[1:]
    )
    back_got, out_got = over(back_other, "c"), over(out_other, "c")
    acts_mine, back_mine, out_mine = hidden_units(h_two, grad_mix, full_c[1], 0, half, mine_1[1:])
    back_total = added_pair(back_mine, back_got)
    back_far = plane_sum_one(back_total)
    term_2 = unit_grads(h_two, grad_mix, acts_mine, acts_other)
    back_near = plane_sum_two(back_total, *back_far)
    *back_near, term_2 = together(*back_near, term_2)
    sums.append(sum_z(term_2))
    grad_h_two = added(back_total, *back_near)
    grad_mid = cotangent.astype(F32) + norm_back(grad_h_two, normed_two, inverse_two, gain_second)
    branch_own = grad_mid.astype(WIDE)
    branch_one = plane_step_one(branch_own)
    branch_two = plane_step_two(*branch_one)
    out_total = added_pair(out_mine, out_got)
    grad_branch = plane_join(branch_own, *branch_one, *branch_two)
    owned = [Unshare(tied(sums[0], *branch_two), first_y)]
    grad_branch, out_total = together(grad_branch, out_total)

    grad_attended = narrow(grad_branch, full_o)
    grad_cols = to_columns(grad_attended, index, cos_tab, sin_tab, 0, GROUP)
    grad_cols, out_total = landed((grad_cols, out_total), (owned[0], "got"))
    out_sends = [
        over(out_total[own : 2 * own], "x"),
        over(out_total[2 * own : 3 * own], "y"),
        across(out_total[3 * own :]),
    ]
    back = functools.partial(attend_back, q_cols)
    prior, far_got = (), []
    if reach:
        dq_far, dkv_far = back(
            far_kv, starts, far_bounds, (own_key, 0), out_cols, logs, grad_cols
        )
        prior = (dq_far,)
        far_got = [
            shifted(
                dkv_far[:, (reach - d) * count : (reach - d + 1) * count].astype(WIDE), -d, period
            )
            for d in range(1, reach + 1)
        ]
    out_term = weight_grads(grad_branch, tied(attended, *prior))
    kv_own, out_term = together(kv_own, out_term)
    dq_cols, dkv_cols = back(
        kv_own, starts, own_bounds, (own_key, own_key), out_cols, logs, grad_cols, prior
    )
    dkv_cols, out_sends, far_got = lax.optimization_barrier((dkv_cols, out_sends, far_got))
    output = (x_mid + added(out_total, *out_sends)).astype(WIDE)
    dkv_own = sum((part.astype(F32) for part in far_got), dkv_cols)
    out_term = spread_sum(tied(out_term, dkv_cols), w_o.shape[0], first_y)
    grad_qkv = to_rows(
        jnp.concatenate([dq_cols, dkv_own], axis=0),
        index,
        cos_tab,
        sin_tab,
        GROUP + 1,
        GROUP + 2,
        full_a.shape[1],
    )
    qkv_part = weight_grads(h_one, grad_qkv)
    grad_qkv, qkv_part, out_term = together(grad_qkv, qkv_part, out_term)
    one_got = over(dot(grad_qkv[half:], full_a, 1, 1).astype(WIDE), "c")
    one_total = (dot(grad_qkv[:half], full_a, 1, 1) + one_got.astype(F32)).astype(WIDE)
    one_total, qkv_part, sums[1] = together(one_total, qkv_part, sums[1])
    qkv_grad = sum_z(qkv_part)
    owned.append(Unshare(sums[1], first_y))
    one_far = plane_sum_one(one_total)
    one_far = landed(one_far, (owned[1], "got"))
    one_near = plane_sum_two(one_total, *one_far)
    out_grad = sum_z(tied(out_term, qkv_grad))
    owned_a = Unshare(qkv_grad, first_y)
    *one_near, qkv_grad = together(*one_near, qkv_grad)
    grad_h_one = added(one_total, *one_near)
    input_grad = (grad_mid + norm_back(grad_h_one, normed_one, inverse_one, gain_first)).astype(
        WIDE
    )

    input_grad = landed(input_grad, (owned_a, "got"))
    owned = [part.both() for part in owned]
    kept = [CHUNK, nf - CHUNK]
    width = [full.shape[1] // 3 for full in full_c]

    def unit_columns(k):
        return jnp.concatenate(
            [
                owned[j][i][:, k * width[j] : k * width[j] + kept[j]]
                for i in range(2)
                for j in range(2)
            ],
            axis=1,
        ).astype(F32)

    down_out, gate_out, up_out = unit_columns(0).T, unit_columns(1), unit_columns(2)
    one, two = owned_a.both()
    pick = lambda a, b: jnp.concatenate([one[:, a:b], two[:, a:b]], axis=1).astype(F32)
    q_out, k_out, v_out = pick(0, nq), pick(nq, nq + nk), pick(nq + nk, nq + 2 * nk)

    def row_sums(weight, grad):
        return jnp.sum(weight.astype(F32) * grad, axis=1)

    gain_sums = jnp.stack(
        [
            row_sums(w_q, q_out) + row_sums(w_k, k_out) + row_sums(w_v, v_out),
            row_sums(w_g, gate_out) + row_sums(w_u, up_out),
        ]
    )
    gain_sums = gain_sums + lax.ppermute(gain_sums, "x", SWAP)
    gain_sums, out_grad = together(gain_sums, out_grad)
    gain_sums = gain_sums + lax.ppermute(gain_sums, "c", SWAP)
    o_out = out_grad.T.astype(F32)
    gain_one_out = gain_sums[0] / gain_attn.astype(WIDE).astype(F32)
    gain_two_out = gain_sums[1] / gain_mlp.astype(WIDE).astype(F32)
    return (
        output,
        input_grad,
        gain_one_out,
        q_out,
        k_out,
        v_out,
        o_out,
        gain_two_out,
        gate_out,
        up_out,
        down_out,
    )


def solution(mesh):
    seq, tensor = mesh.shape["seq"], mesh.shape["tensor"]
    grid = Mesh(
        mesh.devices.reshape(seq // 2, 2, tensor // 2, 2), ("z", "y", "x", "c")
    )
    rows, cols = ("z", "y"), ("x", "c")
    tokens, weight, weight_t = P(rows + cols, None), P(rows, cols), P(cols, rows)
    in_specs = (
        tokens,
        P(),
        P(rows),
        P(rows),
        weight,
        weight,
        weight,
        weight_t,
        P(rows),
        weight,
        weight,
        weight_t,
        tokens,
    )
    out_specs = (
        tokens,
        tokens,
        P(rows),
        weight,
        weight,
        weight,
        weight_t,
        P(rows),
        weight,
        weight,
        weight_t,
    )
    return jax.shard_map(
        per_device, mesh=grid, in_specs=in_specs, out_specs=out_specs, check_vma=False
    )
```

```python
import functools

import jax
import jax.numpy as jnp
from jax import lax
from jax.experimental import pallas as pl
from jax.experimental.pallas import tpu as pltpu
from jax.sharding import Mesh
from jax.sharding import PartitionSpec as P

HEADS = 32
KV = 8
HD = 80
SEQS = 2
DOC_MOST = 2000
GROUP = HEADS // KV

eps = 1e-05
rope_base = 10000.0
LOG2E = 1.4426950408889634
SCORE_LOG2 = HD ** (-0.5) * LOG2E
SCORE_SCALE = HD ** (-0.5)
LOW = -1e30
BQ = 256
CHUNK = 384
KB = 256
WIDE = jnp.bfloat16
F32 = jnp.float32
VMEM_BYTES = 48 * 1024 * 1024

SWAP = [(0, 1), (1, 0)]


def dot(a, b, ca, cb):
    return lax.dot_general(a, b, (((ca,), (cb,)), ((), ())), preferred_element_type=F32)


def turn_kernel(rotary, heads, index_ref, rows_ref, cos_ref, sin_ref, out_ref):
    own = rows_ref.shape[0] // 8
    half = HD // 2
    for pair in range(4):
        parts = [
            rows_ref[pl.ds(pl.multiple_of(index_ref[2 * pair + k] * own, own), own), :].astype(F32)
            for k in range(2)
        ]
        turned = jnp.concatenate(parts, axis=0).T
        lanes = slice(pair * 2 * own, (pair + 1) * 2 * own)
        cos_tab, sin_tab = cos_ref[:, lanes], sin_ref[:, lanes]
        for h in range(heads):
            front, back = turned[h * HD : h * HD + half], turned[h * HD + half : (h + 1) * HD]
            if h < rotary:
                front, back = front * cos_tab - back * sin_tab, back * cos_tab + front * sin_tab
            out_ref[h * HD : (h + 1) * HD, lanes] = jnp.concatenate([front, back], axis=0).astype(
                out_ref.dtype
            )


def to_columns(rows, index, cos_tab, sin_tab, rotary, heads):
    count = rows.shape[0]
    full = lambda shape: pl.BlockSpec(shape, lambda i, s: (0, 0))
    return pl.pallas_call(
        functools.partial(turn_kernel, rotary, heads),
        grid_spec=pltpu.PrefetchScalarGridSpec(
            num_scalar_prefetch=1,
            grid=(1,),
            in_specs=[full(rows.shape), full(cos_tab.shape), full(sin_tab.shape)],
            out_specs=full((heads * HD, count)),
        ),
        out_shape=jax.ShapeDtypeStruct((heads * HD, count), WIDE),
        compiler_params=pltpu.CompilerParams(vmem_limit_bytes=VMEM_BYTES),
        cost_estimate=pl.CostEstimate(flops=10**6, bytes_accessed=10**5, transcendentals=0),
    )(index, rows, cos_tab, sin_tab)


def back_kernel(rotary, heads, index_ref, cols_ref, cos_ref, sin_ref, out_ref):
    own = cols_ref.shape[1] // 8
    half = HD // 2
    width = out_ref.shape[1]
    for pair in range(4):
        lanes = slice(pair * 2 * own, (pair + 1) * 2 * own)
        cos_tab, sin_tab = cos_ref[:, lanes], sin_ref[:, lanes]
        parts = []
        for h in range(heads):
            front = cols_ref[h * HD : h * HD + half, lanes].astype(F32)
            back = cols_ref[h * HD + half : (h + 1) * HD, lanes].astype(F32)
            if h < rotary:
                front, back = front * cos_tab + back * sin_tab, back * cos_tab - front * sin_tab
            parts += [front, back]
        if width > heads * HD:
            parts.append(jnp.zeros((width - heads * HD, 2 * own), F32))
        rows = jnp.concatenate(parts, axis=0).T.astype(out_ref.dtype)
        for k in range(2):
            first = pl.multiple_of(index_ref[2 * pair + k] * own, own)
            out_ref[pl.ds(first, own), :] = rows[k * own : (k + 1) * own]


def to_rows(cols, index, cos_tab, sin_tab, rotary, heads, width):
    count = cols.shape[1]
    full = lambda shape: pl.BlockSpec(shape, lambda i, s: (0, 0))
    return pl.pallas_call(
        functools.partial(back_kernel, rotary, heads),
        grid_spec=pltpu.PrefetchScalarGridSpec(
            num_scalar_prefetch=1,
            grid=(1,),
            in_specs=[full(cols.shape), full(cos_tab.shape), full(sin_tab.shape)],
            out_specs=full((count, width)),
        ),
        out_shape=jax.ShapeDtypeStruct((count, width), WIDE),
        compiler_params=pltpu.CompilerParams(vmem_limit_bytes=VMEM_BYTES),
        cost_estimate=pl.CostEstimate(flops=10**6, bytes_accessed=10**5, transcendentals=0),
    )(index, cols, cos_tab, sin_tab)


def allowed_mask(block, starts, own_places):
    places = block * KB + lax.broadcasted_iota(jnp.int32, (KB, 1), 0)
    return (places >= starts) & (places <= own_places)


def attend_kernel(places, bounds_ref, q_ref, kv_ref, start_ref, *refs):
    first_query, first_key = places
    *prior, out_ref, log_ref, k_rows, acc = refs
    step = pl.program_id(0)
    span = kv_ref.shape[1]

    @pl.when(step == 0)
    def _():
        for j in range(span // KB):
            k_rows[j * KB : (j + 1) * KB, :] = (
                kv_ref[0:HD, j * KB : (j + 1) * KB].astype(F32).T.astype(WIDE)
            )

    starts = start_ref[0:1, :]
    own_places = first_query + step * BQ + lax.broadcasted_iota(jnp.int32, (1, BQ), 1)
    if prior:
        for h in range(GROUP):
            acc[h] = prior[0][h * HD : (h + 1) * HD, :]
    else:
        acc[...] = jnp.zeros_like(acc)

    def one(masked, block, carry):
        first = pl.multiple_of(block * KB - first_key, KB)
        keys = k_rows[pl.ds(first, KB), :]
        values = kv_ref[HD : 2 * HD, pl.ds(first, KB)]
        if masked:
            mask = allowed_mask(block, starts, own_places)
        fresh = []
        for h in range(GROUP):
            top, total = carry[2 * h], carry[2 * h + 1]
            scores = dot(keys, q_ref[h * HD : (h + 1) * HD, :], 1, 0) * SCORE_LOG2
            if masked:
                scores = jnp.where(mask, scores, LOW)
            new_top = jnp.maximum(top, jnp.max(scores, axis=0, keepdims=True))
            probs = jnp.exp2(scores - new_top)
            fade = jnp.exp2(top - new_top)
            total = fade * total + jnp.sum(probs, axis=0, keepdims=True)
            acc[h] = fade * acc[h] + dot(values, probs.astype(WIDE), 1, 0)
            fresh += [new_top, total]
        return tuple(fresh)

    carry = (jnp.full((1, BQ), LOW, F32), jnp.zeros((1, BQ), F32)) * GROUP
    if prior:
        carry = sum(((prior[1][h : h + 1, :], jnp.ones((1, BQ), F32)) for h in range(GROUP)), ())
    lo, full_lo, full_hi, hi = [bounds_ref[k, step] for k in range(4)]
    carry = lax.fori_loop(lo, full_lo, functools.partial(one, True), carry)
    carry = lax.fori_loop(full_lo, full_hi, functools.partial(one, False), carry)
    carry = lax.fori_loop(full_hi, hi, functools.partial(one, True), carry)
    for h in range(GROUP):
        top, total = carry[2 * h], carry[2 * h + 1]
        out_ref[h * HD : (h + 1) * HD, :] = (acc[h] / total).astype(out_ref.dtype)
        log_ref[h : h + 1, :] = top + jnp.log2(total)


def attend(q_cols, kv_cols, starts, bounds, places, prior, out_type):
    count, span = q_cols.shape[1], kv_cols.shape[1]
    wide_block = pl.BlockSpec((GROUP * HD, BQ), lambda i, s: (0, i))
    log_block = pl.BlockSpec((8, BQ), lambda i, s: (0, i))
    return pl.pallas_call(
        functools.partial(attend_kernel, places),
        grid_spec=pltpu.PrefetchScalarGridSpec(
            num_scalar_prefetch=1,
            grid=(count // BQ,),
            in_specs=[
                wide_block,
                pl.BlockSpec((2 * HD, span), lambda i, s: (0, 0)),
                pl.BlockSpec((1, BQ), lambda i, s: (0, i)),
            ]
            + [wide_block, log_block][: len(prior)],
            out_specs=[wide_block, log_block],
            scratch_shapes=[pltpu.VMEM((span, HD), WIDE), pltpu.VMEM((GROUP, HD, BQ), F32)],
        ),
        out_shape=[
            jax.ShapeDtypeStruct((GROUP * HD, count), out_type),
            jax.ShapeDtypeStruct((8, count), F32),
        ],
        compiler_params=pltpu.CompilerParams(vmem_limit_bytes=VMEM_BYTES),
        cost_estimate=pl.CostEstimate(flops=10**6, bytes_accessed=10**5, transcendentals=0),
    )(bounds, q_cols, kv_cols, starts, *prior)


def attend_back_kernel(places, bounds_ref, q_ref, kv_ref, start_ref, out_ref, log_ref, grad_ref, *refs):
    first_query, first_key = places
    *prior, dq_ref, dkv_ref, k_rows, v_rows, q_rows, g_rows, dk, dv, probs_all, grads_all, dq = refs
    step = pl.program_id(0)
    span = kv_ref.shape[1]

    @pl.when(step == 0)
    def _():
        for j in range(span // KB):
            lanes = slice(j * KB, (j + 1) * KB)
            k_rows[lanes, :] = kv_ref[0:HD, lanes].astype(F32).T.astype(WIDE)
            v_rows[lanes, :] = kv_ref[HD : 2 * HD, lanes].astype(F32).T.astype(WIDE)
        dk[...] = jnp.zeros_like(dk)
        dv[...] = jnp.zeros_like(dv)

    starts = start_ref[0:1, :]
    own_places = first_query + step * BQ + lax.broadcasted_iota(jnp.int32, (1, BQ), 1)
    dq[...] = jnp.zeros_like(dq)
    deltas = []
    for h in range(GROUP):
        part = slice(h * HD, (h + 1) * HD)
        q_f32, g_f32 = q_ref[part, :].astype(F32), grad_ref[part, :].astype(F32)
        q_rows[h * BQ : (h + 1) * BQ, :] = q_f32.T.astype(WIDE)
        g_rows[h * BQ : (h + 1) * BQ, :] = g_f32.T.astype(WIDE)
        deltas.append(jnp.sum(g_f32 * out_ref[part, :].astype(F32), axis=0, keepdims=True))

    def one(masked, block, carry):
        first = pl.multiple_of(block * KB - first_key, KB)
        rows = pl.ds(first, KB)
        keys, values = k_rows[rows, :], v_rows[rows, :]
        key_cols = kv_ref[0:HD, rows]
        if masked:
            mask = allowed_mask(block, starts, own_places)
        for h in range(GROUP):
            part = slice(h * HD, (h + 1) * HD)
            lanes = slice(h * BQ, (h + 1) * BQ)
            scores = dot(keys, q_ref[part, :], 1, 0) * SCORE_LOG2 - log_ref[h : h + 1, :]
            if masked:
                scores = jnp.where(mask, scores, LOW)
            probs = jnp.exp2(scores)
            grad_probs = dot(values, grad_ref[part, :], 1, 0)
            grad_scores = (probs * (grad_probs - deltas[h])).astype(WIDE)
            probs_all[:, lanes] = probs.astype(WIDE)
            grads_all[:, lanes] = grad_scores
            dq[h] += dot(key_cols, grad_scores, 1, 0)
        dv[rows, :] += dot(probs_all[...], g_rows[...], 1, 0)
        dk[rows, :] += dot(grads_all[...], q_rows[...], 1, 0)
        return carry

    lo, full_lo, full_hi, hi = [bounds_ref[k, step] for k in range(4)]
    lax.fori_loop(lo, full_lo, functools.partial(one, True), 0)
    lax.fori_loop(full_lo, full_hi, functools.partial(one, False), 0)
    lax.fori_loop(full_hi, hi, functools.partial(one, True), 0)
    for h in range(GROUP):
        part = slice(h * HD, (h + 1) * HD)
        dq_ref[part, :] = dq[h] * SCORE_SCALE + (prior[0][part, :] if prior else 0.0)

    @pl.when(step == pl.num_programs(0) - 1)
    def _():
        for j in range(span // KB):
            lanes = slice(j * KB, (j + 1) * KB)
            dkv_ref[0:HD, lanes] = dk[lanes, :].T * SCORE_SCALE
            dkv_ref[HD : 2 * HD, lanes] = dv[lanes, :].T


def attend_back(q_cols, kv_cols, starts, bounds, places, out_cols, logs, grad_cols, prior=()):
    count, span = q_cols.shape[1], kv_cols.shape[1]
    wide_block = pl.BlockSpec((GROUP * HD, BQ), lambda i, s: (0, i))
    return pl.pallas_call(
        functools.partial(attend_back_kernel, places),
        grid_spec=pltpu.PrefetchScalarGridSpec(
            num_scalar_prefetch=1,
            grid=(count // BQ,),
            in_specs=[
                wide_block,
                pl.BlockSpec((2 * HD, span), lambda i, s: (0, 0)),
                pl.BlockSpec((1, BQ), lambda i, s: (0, i)),
                wide_block,
                pl.BlockSpec((8, BQ), lambda i, s: (0, i)),
                wide_block,
            ]
            + [wide_block] * len(prior),
            out_specs=[wide_block, pl.BlockSpec((2 * HD, span), lambda i, s: (0, 0))],
            scratch_shapes=[
                pltpu.VMEM((span, HD), WIDE),
                pltpu.VMEM((span, HD), WIDE),
                pltpu.VMEM((GROUP * BQ, HD), WIDE),
                pltpu.VMEM((GROUP * BQ, HD), WIDE),
                pltpu.VMEM((span, HD), F32),
                pltpu.VMEM((span, HD), F32),
                pltpu.VMEM((KB, GROUP * BQ), WIDE),
                pltpu.VMEM((KB, GROUP * BQ), WIDE),
                pltpu.VMEM((GROUP, HD, BQ), F32),
            ],
        ),
        out_shape=[
            jax.ShapeDtypeStruct((GROUP * HD, count), F32),
            jax.ShapeDtypeStruct((2 * HD, span), F32),
        ],
        compiler_params=pltpu.CompilerParams(vmem_limit_bytes=VMEM_BYTES),
        cost_estimate=pl.CostEstimate(flops=10**6, bytes_accessed=10**5, transcendentals=0),
    )(bounds, q_cols, kv_cols, starts, out_cols, logs, grad_cols, *prior)


TINY = pl.CostEstimate(flops=10**6, bytes_accessed=10**5, transcendentals=0)
ANY = pl.BlockSpec(memory_space=pl.ANY)


def params():
    return pltpu.CompilerParams(vmem_limit_bytes=VMEM_BYTES)


def join_kernel(*refs):
    *parts, out, whole, sems = refs
    pairs, first = [], 0
    for k, part in enumerate(parts):
        rows = pl.ds(first, part.shape[0])
        pairs.append(
            (
                pltpu.make_async_copy(part, whole.at[rows, :], sems.at[0, k]),
                pltpu.make_async_copy(whole.at[rows, :], out.at[rows, :], sems.at[1, k]),
            )
        )
        first += part.shape[0]
    for copy_in, _ in pairs:
        copy_in.start()
    for copy_in, copy_out in pairs:
        copy_in.wait()
        copy_out.start()
    for _, copy_out in pairs:
        copy_out.wait()


def join(parts):
    rows = sum(part.shape[0] for part in parts)
    return pl.pallas_call(
        join_kernel,
        in_specs=[ANY] * len(parts),
        out_specs=ANY,
        out_shape=jax.ShapeDtypeStruct((rows, parts[0].shape[1]), parts[0].dtype),
        scratch_shapes=[
            pltpu.VMEM((rows, parts[0].shape[1]), parts[0].dtype),
            pltpu.SemaphoreType.DMA((2, len(parts))),
        ],
        compiler_params=params(),
        cost_estimate=TINY,
    )(*parts)


def project_kernel(x_ref, gain_ref, weight_ref, h_ref, out_ref):
    x = x_ref[...].astype(F32)
    inverse = lax.rsqrt(jnp.mean(x * x, axis=-1, keepdims=True) + eps)
    h = (x * inverse * gain_ref[...]).astype(WIDE)
    h_ref[...] = h
    out_ref[...] = dot(h, weight_ref[...], 1, 0)


def project(x_all, gain_row, weights, rows=256):
    count, model = x_all.shape
    width = weights.shape[1]
    return pl.pallas_call(
        project_kernel,
        grid=(count // rows,),
        in_specs=[
            pl.BlockSpec((rows, model), lambda i: (i, 0)),
            pl.BlockSpec((1, model), lambda i: (0, 0)),
            pl.BlockSpec(weights.shape, lambda i: (0, 0), pipeline_mode=pl.Buffered(1)),
        ],
        out_specs=[
            pl.BlockSpec((rows, model), lambda i: (i, 0)),
            pl.BlockSpec((rows, width), lambda i: (i, 0)),
        ],
        out_shape=[
            jax.ShapeDtypeStruct((count, model), WIDE),
            jax.ShapeDtypeStruct((count, width), F32),
        ],
        compiler_params=pltpu.CompilerParams(vmem_limit_bytes=VMEM_BYTES),
        cost_estimate=pl.CostEstimate(flops=10**6, bytes_accessed=10**5, transcendentals=0),
    )(x_all, gain_row, weights)


def narrow_kernel(a_ref, weight_ref, out_ref):
    out_ref[...] = dot(a_ref[...], weight_ref[...], 1, 0).astype(out_ref.dtype)


def whole(array):
    return pl.BlockSpec(array.shape, lambda i: (0, 0), pipeline_mode=pl.Buffered(1))


def narrow(a, weight, rows=256):
    count, model = a.shape
    return pl.pallas_call(
        narrow_kernel,
        grid=(count // rows,),
        in_specs=[pl.BlockSpec((rows, model), lambda i: (i, 0)), whole(weight)],
        out_specs=pl.BlockSpec((rows, weight.shape[1]), lambda i: (i, 0)),
        out_shape=jax.ShapeDtypeStruct((count, weight.shape[1]), WIDE),
        compiler_params=params(),
        cost_estimate=TINY,
    )(a, weight)


def units_kernel(has_prior, h_ref, cot_ref, weight_ref, *refs):
    *prior, acts_ref, back_ref, out_ref = refs
    width = weight_ref.shape[1] // 3
    down_w, gate_w, up_w = [weight_ref[:, k * width : (k + 1) * width] for k in range(3)]
    gate = dot(h_ref[...], gate_w, 1, 0)
    up = dot(h_ref[...], up_w, 1, 0)
    grad = dot(cot_ref[...], down_w, 1, 0)
    sigma = 1.0 / (1.0 + jnp.exp(-gate))
    silu = gate * sigma
    hidden = (silu * up).astype(WIDE)
    grad_gate = (grad * up * sigma * (1.0 + gate * (1.0 - sigma))).astype(WIDE)
    grad_up = (grad * silu).astype(WIDE)
    acts_ref[:, :width] = hidden
    acts_ref[:, width : 2 * width] = grad_gate
    acts_ref[:, 2 * width :] = grad_up
    back = dot(grad_gate, gate_w, 1, 1) + dot(grad_up, up_w, 1, 1)
    out = dot(hidden, down_w, 1, 1)
    if has_prior:
        back, out = back + prior[0][...].astype(F32), out + prior[1][...].astype(F32)
    back_ref[...] = back.astype(WIDE)
    out_ref[...] = out.astype(WIDE)


def hidden_units(h_two, cot, weights, first, count, prior=(), rows=256):
    model, width = h_two.shape[1], weights.shape[1]
    at = first // rows
    block = lambda n: pl.BlockSpec((rows, n), lambda i: (i, 0))
    shape = lambda n: jax.ShapeDtypeStruct((count, n), WIDE)
    return pl.pallas_call(
        functools.partial(units_kernel, bool(prior)),
        grid=(count // rows,),
        in_specs=[pl.BlockSpec((rows, model), lambda i: (i + at, 0))] * 2
        + [whole(weights)]
        + [block(model)] * len(prior),
        out_specs=[block(width), block(model), block(model)],
        out_shape=[shape(width), shape(model), shape(model)],
        compiler_params=params(),
        cost_estimate=TINY,
    )(h_two, cot, weights, *prior)


def unit_grads_kernel(h_ref, cot_ref, mine_ref, other_ref, out_ref):
    half, width = mine_ref.shape[0], mine_ref.shape[1] // 3
    for a_ref, columns in ((cot_ref, slice(0, width)), (h_ref, slice(width, 3 * width))):
        out_ref[:, columns] = (
            dot(a_ref[:half, :], mine_ref[:, columns], 0, 0)
            + dot(a_ref[half:, :], other_ref[:, columns], 0, 0)
        ).astype(WIDE)


def unit_grads(h_two, cot, mine, other, rows=256):
    count, model = h_two.shape
    width = mine.shape[1]
    return pl.pallas_call(
        unit_grads_kernel,
        grid=(model // rows,),
        in_specs=[pl.BlockSpec((count, rows), lambda i: (0, i))] * 2 + [whole(mine), whole(other)],
        out_specs=pl.BlockSpec((rows, width), lambda i: (i, 0)),
        out_shape=jax.ShapeDtypeStruct((model, width), WIDE),
        compiler_params=params(),
        cost_estimate=TINY,
    )(h_two, cot, mine, other)


def as_f32_kernel(a_ref, out_ref):
    out_ref[...] = a_ref[...].astype(F32)


def as_f32(a):
    return pl.pallas_call(
        as_f32_kernel,
        out_shape=jax.ShapeDtypeStruct(a.shape, F32),
        compiler_params=pltpu.CompilerParams(vmem_limit_bytes=VMEM_BYTES // 2),
        cost_estimate=pl.CostEstimate(flops=3 * 10**10, bytes_accessed=10**5, transcendentals=0),
    )(a)


def grads_kernel(a_ref, b_ref, out_ref):
    out_ref[...] = dot(a_ref[...], b_ref[...], 0, 0).astype(WIDE)


def weight_grads(a, b, rows=256):
    count, model = a.shape
    width = b.shape[1]
    return pl.pallas_call(
        grads_kernel,
        grid=(model // rows,),
        in_specs=[pl.BlockSpec((count, rows), lambda i: (0, i)), whole(b)],
        out_specs=pl.BlockSpec((rows, width), lambda i: (i, 0)),
        out_shape=jax.ShapeDtypeStruct((model, width), WIDE),
        compiler_params=params(),
        cost_estimate=TINY,
    )(a, b)


def tied(value, *others):
    return lax.optimization_barrier((value, *others))[0]


def together(*values):
    return lax.optimization_barrier(values)


def shifted(block, distance, period):
    count = lax.axis_size("z")
    route = [
        (i - distance, i)
        for i in range(count)
        if 0 <= i - distance < count and (i - distance) // period == i // period
    ]
    return lax.ppermute(block, "z", route)


def over(block, axis):
    return lax.ppermute(block, axis, SWAP)


def across(block):
    return lax.ppermute(block, ("y", "x"), [(i, 3 - i) for i in range(4)])


def plane_step_one(block):
    return over(block, "x"), over(block, "y")


def plane_step_two(over_x, over_y):
    half = over_x.shape[0] // 2
    return over(over_y[:half], "x"), over(over_x[half:], "y")


def plane_join(*mine):
    return join(list(mine) + [over(part, "c") for part in mine])


def added_pair(one, two):
    return (one.astype(F32) + two.astype(F32)).astype(WIDE)


def landed(values, *flights):
    held = [getattr(holder, field) for holder, field in flights]
    values, held = lax.optimization_barrier((values, held))
    for (holder, field), value in zip(flights, held):
        setattr(holder, field, value)
    return values


def plane_sum_one(total):
    own = total.shape[0] // 4
    half = own // 2
    return over(total[3 * own : 3 * own + half], "x"), over(total[3 * own + half :], "y")


def plane_sum_two(total, top, bottom):
    own = total.shape[0] // 4
    half = own // 2
    wide = lambda a, b: (a.astype(F32) + b.astype(F32)).astype(WIDE)
    to_x = jnp.concatenate(
        [total[own : own + half], wide(total[own + half : 2 * own], bottom)], axis=0
    )
    to_y = jnp.concatenate(
        [wide(total[2 * own : 2 * own + half], top), total[2 * own + half : 3 * own]], axis=0
    )
    return over(to_x, "x"), over(to_y, "y")


def added(total, *parts):
    own = total.shape[0] // 4
    return sum((part.astype(F32) for part in parts), total[:own].astype(F32))


def kept_columns(block, first_y):
    half = block.shape[1] // 2
    keep = jnp.where(first_y, block[:, :half], block[:, half:])
    give = jnp.where(first_y, block[:, half:], block[:, :half])
    return keep, give


def both_rows(keep, got, first_y):
    return jnp.concatenate([jnp.where(first_y, keep, got), jnp.where(first_y, got, keep)], axis=0)


def share_columns(block, first_y, *after):
    keep, give = kept_columns(block, first_y)
    if after:
        give = tied(give, *after)
    return both_rows(keep, over(give, "y"), first_y)


class Unshare:
    def __init__(self, block, first_y):
        half = block.shape[0] // 2
        self.first_y = first_y
        self.keep = jnp.where(first_y, block[:half], block[half:])
        self.got = over(jnp.where(first_y, block[half:], block[:half]), "y")

    def both(self):
        return (
            jnp.where(self.first_y, self.keep, self.got),
            jnp.where(self.first_y, self.got, self.keep),
        )


class SpreadGather:
    def __init__(self, block, first_y):
        self.rows, self.first_y = block.shape[0], first_y
        whole = gather_z(block)
        half = whole.shape[1] // 2
        self.keep = jnp.where(first_y, whole[:, :half], whole[:, half:])
        self.got = over(jnp.where(first_y, whole[:, half:], whole[:, :half]), "y")

    def total(self):
        count, width = self.keep.shape[0] // self.rows, self.keep.shape[1]
        sides = [
            jnp.where(self.first_y, a, b).reshape(count, self.rows, width)
            for a, b in ((self.keep, self.got), (self.got, self.keep))
        ]
        return jnp.concatenate(sides, axis=1).reshape(2 * count * self.rows, width)


def spread_sum(term, rows, first_y):
    blocks = term.reshape(-1, 2, rows, term.shape[1])
    pick = lambda a, b: jnp.where(first_y, a, b).reshape(-1, term.shape[1])
    keep = pick(blocks[:, 0], blocks[:, 1])
    got = over(pick(blocks[:, 1], blocks[:, 0]), "y")
    both = jnp.where(
        first_y,
        jnp.concatenate([keep, got], axis=1),
        jnp.concatenate([got, keep], axis=1),
    )
    return both


def gather_z(block):
    return lax.all_gather(block, "z", axis=0, tiled=True)


def sum_z(block):
    return lax.psum_scatter(block.astype(WIDE), "z", scatter_dimension=0, tiled=True)


def padded(block, multiple=128):
    extra = -block.shape[1] % multiple
    return jnp.pad(block, ((0, 0), (0, extra))) if extra else block


def norm_back(gradient, normed, inverse, gain_vec):
    scaled = gradient * gain_vec
    return inverse * (scaled - normed * jnp.mean(scaled * normed, axis=-1, keepdims=True))


def per_device(
    inputs,
    segments,
    positions,
    gain_attn,
    query_weight,
    key_weight,
    value_weight,
    out_weight,
    gain_mlp,
    gate_weight,
    up_weight,
    down_weight,
    cotangent,
):
    own = inputs.shape[0]
    half, count = 4 * own, 8 * own
    length = segments.shape[0] // SEQS
    reach = (DOC_MOST - 2) // count + 1
    period = lax.axis_size("z")
    if length % count == 0:
        period = length // count
        reach = min(reach, period - 1)
    span = (reach + 1) * count
    z, y = lax.axis_index("z"), lax.axis_index("y")
    x, c = lax.axis_index("x"), lax.axis_index("c")
    first_y = y == 0

    w_q, w_k, w_v, w_g, w_u = [
        w.astype(WIDE) for w in (query_weight, key_weight, value_weight, gate_weight, up_weight)
    ]
    w_o, w_d = out_weight.T.astype(WIDE), down_weight.T.astype(WIDE)
    nq, nk, nf = w_q.shape[1] // 2, w_k.shape[1] // 2, w_g.shape[1] // 2
    rows_w = w_q.shape[0]
    halves = lambda w: (w[:, : w.shape[1] // 2], w[:, w.shape[1] // 2 :])
    gain_pair = jnp.stack([gain_attn, gain_mlp] * 2, 1).astype(WIDE)
    chunks = (slice(0, CHUNK), slice(CHUNK, nf))
    triple = lambda cut: jnp.concatenate(
        [padded(halves(w)[i][:, cut]) for i in range(2) for w in (w_d, w_g, w_u)], axis=1
    )
    flow_o = SpreadGather(w_o, first_y)
    near_a = share_columns(
        jnp.concatenate(
            [
                padded(jnp.concatenate([halves(w)[i] for w in (w_q, w_k, w_v, gain_pair)], axis=1))
                for i in range(2)
            ],
            axis=1,
        ),
        first_y,
    )
    full_a = gather_z(near_a)
    x_one = over(inputs, "x"), over(tied(inputs, near_a), "y")
    x_two = plane_step_two(*x_one)
    x_all = plane_join(inputs, *x_one, *x_two)
    near_c = [share_columns(triple(chunks[0]), first_y, x_all)]
    full_c = [gather_z(near_c[0])]
    first_gain = nq + 2 * nk
    gains = full_a[:, first_gain : first_gain + 2].astype(F32)
    gain_first, gain_second = gains[:, 0], gains[:, 1]

    other_positions = lax.ppermute(positions, "y", SWAP)
    token_positions = jnp.where(
        first_y,
        jnp.concatenate([positions, other_positions]),
        jnp.concatenate([other_positions, positions]),
    )
    frequency = rope_base ** (-(jnp.arange(HD // 2, dtype=F32) * 2.0 / HD))
    angles = frequency[:, None] * token_positions.astype(F32)[None, :]
    cos_tab, sin_tab = jnp.cos(angles), jnp.sin(angles)
    places = jnp.arange(8, dtype=jnp.int32)
    flips = places ^ (y * 4 + x * 2 + c).astype(jnp.int32)
    index = (flips % 2) * 4 + flips // 2
    padded_segs = jnp.concatenate([jnp.full((reach * count,), -1, jnp.int32), segments])
    key_segs = lax.dynamic_slice_in_dim(padded_segs, z * count, span, 0)
    query_segs = lax.dynamic_slice_in_dim(segments, z * count, count, 0)
    starts = jnp.sum((key_segs[:, None] < query_segs[None, :]).astype(jnp.int32), axis=0)
    first_rows = jnp.arange(count // BQ, dtype=jnp.int32) * BQ
    lo = starts[first_rows] // KB
    hi = (reach * count + first_rows + BQ + KB - 1) // KB
    full_lo = jnp.clip((starts[first_rows + BQ - 1] + KB - 1) // KB, lo, hi)
    full_hi = jnp.clip((reach * count + first_rows + 1) // KB, full_lo, hi)
    bounds = jnp.stack([lo, full_lo, full_hi, hi])
    own_key = reach * count
    own_bounds = jnp.maximum(bounds, own_key // KB)
    far_bounds = jnp.minimum(bounds, own_key // KB)
    starts = starts[None, :]

    h_one, qkv = project(x_all, gain_first[None, :], full_a)
    near_c.append(share_columns(triple(chunks[1]), first_y, qkv))
    full_c.append(gather_z(near_c[1]))
    turned = to_columns(qkv, index, cos_tab, sin_tab, GROUP + 1, GROUP + 2)
    q_cols, kv_own = turned[: GROUP * HD], turned[GROUP * HD :]
    far_kv = [shifted(kv_own, distance, period) for distance in range(reach, 0, -1)]
    far_kv = [shifted(kv_own, distance, period) for distance in range(reach, 0, -1)]
    kv_own = landed(kv_own, (flow_o, "got"))
    cot_one = plane_step_one(tied(cotangent, kv_own))
    own_part = attend(q_cols, kv_own, starts, own_bounds, (own_key, own_key), (), F32)
    own_part, far_kv, near_0 = lax.optimization_barrier((own_part, far_kv, near_c[0]))
    if reach:
        far_kv = jnp.concatenate(far_kv, axis=1)
        out_cols, logs = attend(q_cols, far_kv, starts, far_bounds, (own_key, 0), own_part, WIDE)
    else:
        out_cols, logs = own_part[0].astype(WIDE), own_part[1]
    out_cols, cot_one, _ = lax.optimization_barrier((out_cols, cot_one, near_c[1]))
    cot_two = plane_step_two(*cot_one)
    full_o = flow_o.total()
    attended = to_rows(out_cols, index, cos_tab, sin_tab, 0, GROUP, GROUP * HD)
    input_f32 = inputs.astype(F32)
    inverse_one = lax.rsqrt(jnp.mean(input_f32 * input_f32, axis=-1, keepdims=True) + eps)
    normed_one = input_f32 * inverse_one
    mid_got = over(dot(attended[half:], full_o, 1, 1).astype(WIDE), "c")
    mid_total = (dot(attended[:half], full_o, 1, 1) + mid_got.astype(F32)).astype(WIDE)
    mid_total, *cot_two = together(mid_total, *cot_two)
    mid_far = plane_sum_one(mid_total)
    mid_near = plane_sum_two(mid_total, *mid_far)
    grad_mix = plane_join(cotangent, *cot_one, *cot_two)
    x_mid = input_f32 + added(mid_total, *mid_near)

    inverse_two = lax.rsqrt(jnp.mean(x_mid * x_mid, axis=-1, keepdims=True) + eps)
    normed_two = x_mid * inverse_two
    h_own = (normed_two * gain_second).astype(WIDE)
    h_step = plane_step_one(h_own)
    h_two = plane_join(h_own, *h_step, *plane_step_two(*h_step))
    h_two, grad_mix = together(h_two, grad_mix)
    other_1 = hidden_units(h_two, grad_mix, full_c[0], half, half)
    mine_1 = hidden_units(h_two, grad_mix, full_c[0], 0, half)
    term_1 = unit_grads(h_two, grad_mix, mine_1[0], other_1[0])
    full_c[1], other_1, mine_1, term_1 = lax.optimization_barrier(
        (full_c[1], other_1, mine_1, term_1)
    )
    sums = [sum_z(term_1)]
    acts_other, back_other, out_other = hidden_units(
        h_two, grad_mix, full_c[1], half, half, other_1[1:]
    )
    back_got, out_got = over(back_other, "c"), over(out_other, "c")
    acts_mine, back_mine, out_mine = hidden_units(h_two, grad_mix, full_c[1], 0, half, mine_1[1:])
    back_total = added_pair(back_mine, back_got)
    back_far = plane_sum_one(back_total)
    term_2 = unit_grads(h_two, grad_mix, acts_mine, acts_other)
    back_near = plane_sum_two(back_total, *back_far)
    *back_near, term_2 = together(*back_near, term_2)
    sums.append(sum_z(term_2))
    grad_h_two = added(back_total, *back_near)
    grad_mid = cotangent.astype(F32) + norm_back(grad_h_two, normed_two, inverse_two, gain_second)
    branch_own = grad_mid.astype(WIDE)
    branch_one = plane_step_one(branch_own)
    branch_two = plane_step_two(*branch_one)
    out_total = added_pair(out_mine, out_got)
    grad_branch = plane_join(branch_own, *branch_one, *branch_two)
    owned = [Unshare(tied(sums[0], *branch_two), first_y)]
    grad_branch, out_total = together(grad_branch, out_total)

    grad_attended = narrow(grad_branch, full_o)
    grad_cols = to_columns(grad_attended, index, cos_tab, sin_tab, 0, GROUP)
    grad_cols, out_total = landed((grad_cols, out_total), (owned[0], "got"))
    out_sends = [
        over(out_total[own : 2 * own], "x"),
        over(out_total[2 * own : 3 * own], "y"),
        across(out_total[3 * own :]),
    ]
    back = functools.partial(attend_back, q_cols)
    prior, far_got = (), []
    if reach:
        dq_far, dkv_far = back(
            far_kv, starts, far_bounds, (own_key, 0), out_cols, logs, grad_cols
        )
        prior = (dq_far,)
        far_got = [
            shifted(
                dkv_far[:, (reach - d) * count : (reach - d + 1) * count].astype(WIDE), -d, period
            )
            for d in range(1, reach + 1)
        ]
    out_term = weight_grads(grad_branch, tied(attended, *prior))
    kv_own, out_term = together(kv_own, out_term)
    dq_cols, dkv_cols = back(
        kv_own, starts, own_bounds, (own_key, own_key), out_cols, logs, grad_cols, prior
    )
    dkv_cols, out_sends, far_got = lax.optimization_barrier((dkv_cols, out_sends, far_got))
    output = (x_mid + added(out_total, *out_sends)).astype(WIDE)
    dkv_own = sum((part.astype(F32) for part in far_got), dkv_cols)
    out_term = spread_sum(tied(out_term, dkv_cols), w_o.shape[0], first_y)
    grad_qkv = to_rows(
        jnp.concatenate([dq_cols, dkv_own], axis=0),
        index,
        cos_tab,
        sin_tab,
        GROUP + 1,
        GROUP + 2,
        full_a.shape[1],
    )
    qkv_part = weight_grads(h_one, grad_qkv)
    grad_qkv, qkv_part, out_term = together(grad_qkv, qkv_part, out_term)
    one_got = over(dot(grad_qkv[half:], full_a, 1, 1).astype(WIDE), "c")
    qkv_part, sums[1], one_got = together(qkv_part, sums[1], one_got)
    one_total = (dot(grad_qkv[:half], full_a, 1, 1) + one_got.astype(F32)).astype(WIDE)
    qkv_grad = sum_z(qkv_part)
    owned.append(Unshare(sums[1], first_y))
    one_far = plane_sum_one(one_total)
    one_far = landed(one_far, (owned[1], "got"))
    one_near = plane_sum_two(one_total, *one_far)
    out_grad = sum_z(tied(out_term, qkv_grad))
    owned_a = Unshare(qkv_grad, first_y)
    *one_near, qkv_grad = together(*one_near, qkv_grad)
    grad_h_one = added(one_total, *one_near)
    input_grad = (grad_mid + norm_back(grad_h_one, normed_one, inverse_one, gain_first)).astype(
        WIDE
    )

    input_grad = landed(input_grad, (owned_a, "got"))
    owned = [part.both() for part in owned]
    kept = [CHUNK, nf - CHUNK]
    width = [full.shape[1] // 3 for full in full_c]

    def unit_columns(k):
        return jnp.concatenate(
            [
                owned[j][i][:, k * width[j] : k * width[j] + kept[j]]
                for i in range(2)
                for j in range(2)
            ],
            axis=1,
        ).astype(F32)

    down_out, gate_out, up_out = unit_columns(0).T, unit_columns(1), unit_columns(2)
    one, two = owned_a.both()
    pick = lambda a, b: jnp.concatenate([one[:, a:b], two[:, a:b]], axis=1).astype(F32)
    q_out, k_out, v_out = pick(0, nq), pick(nq, nq + nk), pick(nq + nk, nq + 2 * nk)

    def row_sums(weight, grad):
        return jnp.sum(weight.astype(F32) * grad, axis=1)

    gain_sums = jnp.stack(
        [
            row_sums(w_q, q_out) + row_sums(w_k, k_out) + row_sums(w_v, v_out),
            row_sums(w_g, gate_out) + row_sums(w_u, up_out),
        ]
    )
    gain_sums = gain_sums + lax.ppermute(gain_sums, "x", SWAP)
    gain_sums = gain_sums + lax.ppermute(gain_sums, "c", SWAP)
    gain_sums, out_grad = together(gain_sums, out_grad)
    o_out = as_f32(out_grad).T
    gain_one_out = gain_sums[0] / gain_attn.astype(WIDE).astype(F32)
    gain_two_out = gain_sums[1] / gain_mlp.astype(WIDE).astype(F32)
    return (
        output,
        input_grad,
        gain_one_out,
        q_out,
        k_out,
        v_out,
        o_out,
        gain_two_out,
        gate_out,
        up_out,
        down_out,
    )


def solution(mesh):
    seq, tensor = mesh.shape["seq"], mesh.shape["tensor"]
    grid = Mesh(
        mesh.devices.reshape(seq // 2, 2, tensor // 2, 2), ("z", "y", "x", "c")
    )
    rows, cols = ("z", "y"), ("x", "c")
    tokens, weight, weight_t = P(rows + cols, None), P(rows, cols), P(cols, rows)
    in_specs = (
        tokens,
        P(),
        P(rows),
        P(rows),
        weight,
        weight,
        weight,
        weight_t,
        P(rows),
        weight,
        weight,
        weight_t,
        tokens,
    )
    out_specs = (
        tokens,
        tokens,
        P(rows),
        weight,
        weight,
        weight,
        weight_t,
        P(rows),
        weight,
        weight,
        weight_t,
    )
    return jax.shard_map(
        per_device, mesh=grid, in_specs=in_specs, out_specs=out_specs, check_vma=False
    )
```

```python
import functools

import jax
import jax.numpy as jnp
from jax import lax
from jax.experimental import pallas as pl
from jax.experimental.pallas import tpu as pltpu
from jax.sharding import Mesh
from jax.sharding import PartitionSpec as P

HEADS = 32
KV = 8
HD = 80
SEQS = 2
DOC_MOST = 2000
GROUP = HEADS // KV

eps = 1e-05
rope_base = 10000.0
LOG2E = 1.4426950408889634
SCORE_LOG2 = HD ** (-0.5) * LOG2E
SCORE_SCALE = HD ** (-0.5)
LOW = -1e30
BQ = 256
CHUNK = 384
KB = 256
WIDE = jnp.bfloat16
F32 = jnp.float32
VMEM_BYTES = 48 * 1024 * 1024

SWAP = [(0, 1), (1, 0)]


def dot(a, b, ca, cb):
    return lax.dot_general(a, b, (((ca,), (cb,)), ((), ())), preferred_element_type=F32)


def turn_kernel(rotary, heads, index_ref, rows_ref, cos_ref, sin_ref, out_ref):
    own = rows_ref.shape[0] // 8
    half = HD // 2
    for pair in range(4):
        parts = [
            rows_ref[pl.ds(pl.multiple_of(index_ref[2 * pair + k] * own, own), own), :].astype(F32)
            for k in range(2)
        ]
        turned = jnp.concatenate(parts, axis=0).T
        lanes = slice(pair * 2 * own, (pair + 1) * 2 * own)
        cos_tab, sin_tab = cos_ref[:, lanes], sin_ref[:, lanes]
        for h in range(heads):
            front, back = turned[h * HD : h * HD + half], turned[h * HD + half : (h + 1) * HD]
            if h < rotary:
                front, back = front * cos_tab - back * sin_tab, back * cos_tab + front * sin_tab
            out_ref[h * HD : (h + 1) * HD, lanes] = jnp.concatenate([front, back], axis=0).astype(
                out_ref.dtype
            )


def to_columns(rows, index, cos_tab, sin_tab, rotary, heads):
    count = rows.shape[0]
    full = lambda shape: pl.BlockSpec(shape, lambda i, s: (0, 0))
    return pl.pallas_call(
        functools.partial(turn_kernel, rotary, heads),
        grid_spec=pltpu.PrefetchScalarGridSpec(
            num_scalar_prefetch=1,
            grid=(1,),
            in_specs=[full(rows.shape), full(cos_tab.shape), full(sin_tab.shape)],
            out_specs=full((heads * HD, count)),
        ),
        out_shape=jax.ShapeDtypeStruct((heads * HD, count), WIDE),
        compiler_params=pltpu.CompilerParams(vmem_limit_bytes=VMEM_BYTES),
        cost_estimate=pl.CostEstimate(flops=10**6, bytes_accessed=10**5, transcendentals=0),
    )(index, rows, cos_tab, sin_tab)


def back_kernel(rotary, heads, index_ref, cols_ref, cos_ref, sin_ref, out_ref):
    own = cols_ref.shape[1] // 8
    half = HD // 2
    width = out_ref.shape[1]
    for pair in range(4):
        lanes = slice(pair * 2 * own, (pair + 1) * 2 * own)
        cos_tab, sin_tab = cos_ref[:, lanes], sin_ref[:, lanes]
        parts = []
        for h in range(heads):
            front = cols_ref[h * HD : h * HD + half, lanes].astype(F32)
            back = cols_ref[h * HD + half : (h + 1) * HD, lanes].astype(F32)
            if h < rotary:
                front, back = front * cos_tab + back * sin_tab, back * cos_tab - front * sin_tab
            parts += [front, back]
        if width > heads * HD:
            parts.append(jnp.zeros((width - heads * HD, 2 * own), F32))
        rows = jnp.concatenate(parts, axis=0).T.astype(out_ref.dtype)
        for k in range(2):
            first = pl.multiple_of(index_ref[2 * pair + k] * own, own)
            out_ref[pl.ds(first, own), :] = rows[k * own : (k + 1) * own]


def to_rows(cols, index, cos_tab, sin_tab, rotary, heads, width):
    count = cols.shape[1]
    full = lambda shape: pl.BlockSpec(shape, lambda i, s: (0, 0))
    return pl.pallas_call(
        functools.partial(back_kernel, rotary, heads),
        grid_spec=pltpu.PrefetchScalarGridSpec(
            num_scalar_prefetch=1,
            grid=(1,),
            in_specs=[full(cols.shape), full(cos_tab.shape), full(sin_tab.shape)],
            out_specs=full((count, width)),
        ),
        out_shape=jax.ShapeDtypeStruct((count, width), WIDE),
        compiler_params=pltpu.CompilerParams(vmem_limit_bytes=VMEM_BYTES),
        cost_estimate=pl.CostEstimate(flops=10**6, bytes_accessed=10**5, transcendentals=0),
    )(index, cols, cos_tab, sin_tab)


def allowed_mask(block, starts, own_places):
    places = block * KB + lax.broadcasted_iota(jnp.int32, (KB, 1), 0)
    return (places >= starts) & (places <= own_places)


def attend_kernel(places, bounds_ref, q_ref, kv_ref, start_ref, *refs):
    first_query, first_key = places
    *prior, out_ref, log_ref, k_rows, acc = refs
    step = pl.program_id(0)
    span = kv_ref.shape[1]

    @pl.when(step == 0)
    def _():
        for j in range(span // KB):
            k_rows[j * KB : (j + 1) * KB, :] = (
                kv_ref[0:HD, j * KB : (j + 1) * KB].astype(F32).T.astype(WIDE)
            )

    starts = start_ref[0:1, :]
    own_places = first_query + step * BQ + lax.broadcasted_iota(jnp.int32, (1, BQ), 1)
    if prior:
        for h in range(GROUP):
            acc[h] = prior[0][h * HD : (h + 1) * HD, :]
    else:
        acc[...] = jnp.zeros_like(acc)

    def one(masked, block, carry):
        first = pl.multiple_of(block * KB - first_key, KB)
        keys = k_rows[pl.ds(first, KB), :]
        values = kv_ref[HD : 2 * HD, pl.ds(first, KB)]
        if masked:
            mask = allowed_mask(block, starts, own_places)
        fresh = []
        for h in range(GROUP):
            top, total = carry[2 * h], carry[2 * h + 1]
            scores = dot(keys, q_ref[h * HD : (h + 1) * HD, :], 1, 0) * SCORE_LOG2
            if masked:
                scores = jnp.where(mask, scores, LOW)
            new_top = jnp.maximum(top, jnp.max(scores, axis=0, keepdims=True))
            probs = jnp.exp2(scores - new_top)
            fade = jnp.exp2(top - new_top)
            total = fade * total + jnp.sum(probs, axis=0, keepdims=True)
            acc[h] = fade * acc[h] + dot(values, probs.astype(WIDE), 1, 0)
            fresh += [new_top, total]
        return tuple(fresh)

    carry = (jnp.full((1, BQ), LOW, F32), jnp.zeros((1, BQ), F32)) * GROUP
    if prior:
        carry = sum(((prior[1][h : h + 1, :], jnp.ones((1, BQ), F32)) for h in range(GROUP)), ())
    lo, full_lo, full_hi, hi = [bounds_ref[k, step] for k in range(4)]
    carry = lax.fori_loop(lo, full_lo, functools.partial(one, True), carry)
    carry = lax.fori_loop(full_lo, full_hi, functools.partial(one, False), carry)
    carry = lax.fori_loop(full_hi, hi, functools.partial(one, True), carry)
    for h in range(GROUP):
        top, total = carry[2 * h], carry[2 * h + 1]
        out_ref[h * HD : (h + 1) * HD, :] = (acc[h] / total).astype(out_ref.dtype)
        log_ref[h : h + 1, :] = top + jnp.log2(total)


def attend(q_cols, kv_cols, starts, bounds, places, prior, out_type):
    count, span = q_cols.shape[1], kv_cols.shape[1]
    wide_block = pl.BlockSpec((GROUP * HD, BQ), lambda i, s: (0, i))
    log_block = pl.BlockSpec((8, BQ), lambda i, s: (0, i))
    return pl.pallas_call(
        functools.partial(attend_kernel, places),
        grid_spec=pltpu.PrefetchScalarGridSpec(
            num_scalar_prefetch=1,
            grid=(count // BQ,),
            in_specs=[
                wide_block,
                pl.BlockSpec((2 * HD, span), lambda i, s: (0, 0)),
                pl.BlockSpec((1, BQ), lambda i, s: (0, i)),
            ]
            + [wide_block, log_block][: len(prior)],
            out_specs=[wide_block, log_block],
            scratch_shapes=[pltpu.VMEM((span, HD), WIDE), pltpu.VMEM((GROUP, HD, BQ), F32)],
        ),
        out_shape=[
            jax.ShapeDtypeStruct((GROUP * HD, count), out_type),
            jax.ShapeDtypeStruct((8, count), F32),
        ],
        compiler_params=pltpu.CompilerParams(vmem_limit_bytes=VMEM_BYTES),
        cost_estimate=pl.CostEstimate(flops=10**6, bytes_accessed=10**5, transcendentals=0),
    )(bounds, q_cols, kv_cols, starts, *prior)


def attend_back_kernel(places, bounds_ref, q_ref, kv_ref, start_ref, out_ref, log_ref, grad_ref, *refs):
    first_query, first_key = places
    *prior, dq_ref, dkv_ref, k_rows, v_rows, q_rows, g_rows, dk, dv, probs_all, grads_all, dq = refs
    step = pl.program_id(0)
    span = kv_ref.shape[1]

    @pl.when(step == 0)
    def _():
        for j in range(span // KB):
            lanes = slice(j * KB, (j + 1) * KB)
            k_rows[lanes, :] = kv_ref[0:HD, lanes].astype(F32).T.astype(WIDE)
            v_rows[lanes, :] = kv_ref[HD : 2 * HD, lanes].astype(F32).T.astype(WIDE)
        dk[...] = jnp.zeros_like(dk)
        dv[...] = jnp.zeros_like(dv)

    starts = start_ref[0:1, :]
    own_places = first_query + step * BQ + lax.broadcasted_iota(jnp.int32, (1, BQ), 1)
    dq[...] = jnp.zeros_like(dq)
    deltas = []
    for h in range(GROUP):
        part = slice(h * HD, (h + 1) * HD)
        q_f32, g_f32 = q_ref[part, :].astype(F32), grad_ref[part, :].astype(F32)
        q_rows[h * BQ : (h + 1) * BQ, :] = q_f32.T.astype(WIDE)
        g_rows[h * BQ : (h + 1) * BQ, :] = g_f32.T.astype(WIDE)
        deltas.append(jnp.sum(g_f32 * out_ref[part, :].astype(F32), axis=0, keepdims=True))

    def one(masked, block, carry):
        first = pl.multiple_of(block * KB - first_key, KB)
        rows = pl.ds(first, KB)
        keys, values = k_rows[rows, :], v_rows[rows, :]
        key_cols = kv_ref[0:HD, rows]
        if masked:
            mask = allowed_mask(block, starts, own_places)
        for h in range(GROUP):
            part = slice(h * HD, (h + 1) * HD)
            lanes = slice(h * BQ, (h + 1) * BQ)
            scores = dot(keys, q_ref[part, :], 1, 0) * SCORE_LOG2 - log_ref[h : h + 1, :]
            if masked:
                scores = jnp.where(mask, scores, LOW)
            probs = jnp.exp2(scores)
            grad_probs = dot(values, grad_ref[part, :], 1, 0)
            grad_scores = (probs * (grad_probs - deltas[h])).astype(WIDE)
            probs_all[:, lanes] = probs.astype(WIDE)
            grads_all[:, lanes] = grad_scores
            dq[h] += dot(key_cols, grad_scores, 1, 0)
        dv[rows, :] += dot(probs_all[...], g_rows[...], 1, 0)
        dk[rows, :] += dot(grads_all[...], q_rows[...], 1, 0)
        return carry

    lo, full_lo, full_hi, hi = [bounds_ref[k, step] for k in range(4)]
    lax.fori_loop(lo, full_lo, functools.partial(one, True), 0)
    lax.fori_loop(full_lo, full_hi, functools.partial(one, False), 0)
    lax.fori_loop(full_hi, hi, functools.partial(one, True), 0)
    for h in range(GROUP):
        part = slice(h * HD, (h + 1) * HD)
        dq_ref[part, :] = dq[h] * SCORE_SCALE + (prior[0][part, :] if prior else 0.0)

    @pl.when(step == pl.num_programs(0) - 1)
    def _():
        for j in range(span // KB):
            lanes = slice(j * KB, (j + 1) * KB)
            dkv_ref[0:HD, lanes] = dk[lanes, :].T * SCORE_SCALE
            dkv_ref[HD : 2 * HD, lanes] = dv[lanes, :].T


def attend_back(q_cols, kv_cols, starts, bounds, places, out_cols, logs, grad_cols, prior=()):
    count, span = q_cols.shape[1], kv_cols.shape[1]
    wide_block = pl.BlockSpec((GROUP * HD, BQ), lambda i, s: (0, i))
    return pl.pallas_call(
        functools.partial(attend_back_kernel, places),
        grid_spec=pltpu.PrefetchScalarGridSpec(
            num_scalar_prefetch=1,
            grid=(count // BQ,),
            in_specs=[
                wide_block,
                pl.BlockSpec((2 * HD, span), lambda i, s: (0, 0)),
                pl.BlockSpec((1, BQ), lambda i, s: (0, i)),
                wide_block,
                pl.BlockSpec((8, BQ), lambda i, s: (0, i)),
                wide_block,
            ]
            + [wide_block] * len(prior),
            out_specs=[wide_block, pl.BlockSpec((2 * HD, span), lambda i, s: (0, 0))],
            scratch_shapes=[
                pltpu.VMEM((span, HD), WIDE),
                pltpu.VMEM((span, HD), WIDE),
                pltpu.VMEM((GROUP * BQ, HD), WIDE),
                pltpu.VMEM((GROUP * BQ, HD), WIDE),
                pltpu.VMEM((span, HD), F32),
                pltpu.VMEM((span, HD), F32),
                pltpu.VMEM((KB, GROUP * BQ), WIDE),
                pltpu.VMEM((KB, GROUP * BQ), WIDE),
                pltpu.VMEM((GROUP, HD, BQ), F32),
            ],
        ),
        out_shape=[
            jax.ShapeDtypeStruct((GROUP * HD, count), F32),
            jax.ShapeDtypeStruct((2 * HD, span), F32),
        ],
        compiler_params=pltpu.CompilerParams(vmem_limit_bytes=VMEM_BYTES),
        cost_estimate=pl.CostEstimate(flops=10**6, bytes_accessed=10**5, transcendentals=0),
    )(bounds, q_cols, kv_cols, starts, out_cols, logs, grad_cols, *prior)


TINY = pl.CostEstimate(flops=10**6, bytes_accessed=10**5, transcendentals=0)
ANY = pl.BlockSpec(memory_space=pl.ANY)


def params():
    return pltpu.CompilerParams(vmem_limit_bytes=VMEM_BYTES)


def join_kernel(*refs):
    *parts, out, whole, sems = refs
    pairs, first = [], 0
    for k, part in enumerate(parts):
        rows = pl.ds(first, part.shape[0])
        pairs.append(
            (
                pltpu.make_async_copy(part, whole.at[rows, :], sems.at[0, k]),
                pltpu.make_async_copy(whole.at[rows, :], out.at[rows, :], sems.at[1, k]),
            )
        )
        first += part.shape[0]
    for copy_in, _ in pairs:
        copy_in.start()
    for copy_in, copy_out in pairs:
        copy_in.wait()
        copy_out.start()
    for _, copy_out in pairs:
        copy_out.wait()


def join(parts):
    rows = sum(part.shape[0] for part in parts)
    return pl.pallas_call(
        join_kernel,
        in_specs=[ANY] * len(parts),
        out_specs=ANY,
        out_shape=jax.ShapeDtypeStruct((rows, parts[0].shape[1]), parts[0].dtype),
        scratch_shapes=[
            pltpu.VMEM((rows, parts[0].shape[1]), parts[0].dtype),
            pltpu.SemaphoreType.DMA((2, len(parts))),
        ],
        compiler_params=params(),
        cost_estimate=TINY,
    )(*parts)


def project_kernel(x_ref, gain_ref, weight_ref, h_ref, out_ref):
    x = x_ref[...].astype(F32)
    inverse = lax.rsqrt(jnp.mean(x * x, axis=-1, keepdims=True) + eps)
    h = (x * inverse * gain_ref[...]).astype(WIDE)
    h_ref[...] = h
    out_ref[...] = dot(h, weight_ref[...], 1, 0)


def project(x_all, gain_row, weights, rows=256):
    count, model = x_all.shape
    width = weights.shape[1]
    return pl.pallas_call(
        project_kernel,
        grid=(count // rows,),
        in_specs=[
            pl.BlockSpec((rows, model), lambda i: (i, 0)),
            pl.BlockSpec((1, model), lambda i: (0, 0)),
            pl.BlockSpec(weights.shape, lambda i: (0, 0), pipeline_mode=pl.Buffered(1)),
        ],
        out_specs=[
            pl.BlockSpec((rows, model), lambda i: (i, 0)),
            pl.BlockSpec((rows, width), lambda i: (i, 0)),
        ],
        out_shape=[
            jax.ShapeDtypeStruct((count, model), WIDE),
            jax.ShapeDtypeStruct((count, width), F32),
        ],
        compiler_params=pltpu.CompilerParams(vmem_limit_bytes=VMEM_BYTES),
        cost_estimate=pl.CostEstimate(flops=10**6, bytes_accessed=10**5, transcendentals=0),
    )(x_all, gain_row, weights)


def narrow_kernel(a_ref, weight_ref, out_ref):
    out_ref[...] = dot(a_ref[...], weight_ref[...], 1, 0).astype(out_ref.dtype)


def whole(array):
    return pl.BlockSpec(array.shape, lambda i: (0, 0), pipeline_mode=pl.Buffered(1))


def narrow(a, weight, rows=256):
    count, model = a.shape
    return pl.pallas_call(
        narrow_kernel,
        grid=(count // rows,),
        in_specs=[pl.BlockSpec((rows, model), lambda i: (i, 0)), whole(weight)],
        out_specs=pl.BlockSpec((rows, weight.shape[1]), lambda i: (i, 0)),
        out_shape=jax.ShapeDtypeStruct((count, weight.shape[1]), WIDE),
        compiler_params=params(),
        cost_estimate=TINY,
    )(a, weight)


def units_kernel(has_prior, h_ref, cot_ref, weight_ref, *refs):
    *prior, acts_ref, back_ref, out_ref = refs
    width = weight_ref.shape[1] // 3
    down_w, gate_w, up_w = [weight_ref[:, k * width : (k + 1) * width] for k in range(3)]
    gate = dot(h_ref[...], gate_w, 1, 0)
    up = dot(h_ref[...], up_w, 1, 0)
    grad = dot(cot_ref[...], down_w, 1, 0)
    sigma = 1.0 / (1.0 + jnp.exp(-gate))
    silu = gate * sigma
    hidden = (silu * up).astype(WIDE)
    grad_gate = (grad * up * sigma * (1.0 + gate * (1.0 - sigma))).astype(WIDE)
    grad_up = (grad * silu).astype(WIDE)
    acts_ref[:, :width] = hidden
    acts_ref[:, width : 2 * width] = grad_gate
    acts_ref[:, 2 * width :] = grad_up
    back = dot(grad_gate, gate_w, 1, 1) + dot(grad_up, up_w, 1, 1)
    out = dot(hidden, down_w, 1, 1)
    if has_prior:
        back, out = back + prior[0][...].astype(F32), out + prior[1][...].astype(F32)
    back_ref[...] = back.astype(WIDE)
    out_ref[...] = out.astype(WIDE)


def hidden_units(h_two, cot, weights, first, count, prior=(), rows=256):
    model, width = h_two.shape[1], weights.shape[1]
    at = first // rows
    block = lambda n: pl.BlockSpec((rows, n), lambda i: (i, 0))
    shape = lambda n: jax.ShapeDtypeStruct((count, n), WIDE)
    return pl.pallas_call(
        functools.partial(units_kernel, bool(prior)),
        grid=(count // rows,),
        in_specs=[pl.BlockSpec((rows, model), lambda i: (i + at, 0))] * 2
        + [whole(weights)]
        + [block(model)] * len(prior),
        out_specs=[block(width), block(model), block(model)],
        out_shape=[shape(width), shape(model), shape(model)],
        compiler_params=params(),
        cost_estimate=TINY,
    )(h_two, cot, weights, *prior)


def unit_grads_kernel(h_ref, cot_ref, mine_ref, other_ref, out_ref):
    half, width = mine_ref.shape[0], mine_ref.shape[1] // 3
    for a_ref, columns in ((cot_ref, slice(0, width)), (h_ref, slice(width, 3 * width))):
        out_ref[:, columns] = (
            dot(a_ref[:half, :], mine_ref[:, columns], 0, 0)
            + dot(a_ref[half:, :], other_ref[:, columns], 0, 0)
        ).astype(WIDE)


def unit_grads(h_two, cot, mine, other, rows=256):
    count, model = h_two.shape
    width = mine.shape[1]
    return pl.pallas_call(
        unit_grads_kernel,
        grid=(model // rows,),
        in_specs=[pl.BlockSpec((count, rows), lambda i: (0, i))] * 2 + [whole(mine), whole(other)],
        out_specs=pl.BlockSpec((rows, width), lambda i: (i, 0)),
        out_shape=jax.ShapeDtypeStruct((model, width), WIDE),
        compiler_params=params(),
        cost_estimate=TINY,
    )(h_two, cot, mine, other)


def as_f32_kernel(a_ref, out_ref):
    out_ref[...] = a_ref[...].astype(F32)


def as_f32(a):
    return pl.pallas_call(
        as_f32_kernel,
        out_shape=jax.ShapeDtypeStruct(a.shape, F32),
        compiler_params=pltpu.CompilerParams(vmem_limit_bytes=VMEM_BYTES // 2),
        cost_estimate=pl.CostEstimate(flops=2 * 10**11, bytes_accessed=10**5, transcendentals=0),
    )(a)


def grads_kernel(a_ref, b_ref, out_ref):
    out_ref[...] = dot(a_ref[...], b_ref[...], 0, 0).astype(WIDE)


def weight_grads(a, b, rows=256):
    count, model = a.shape
    width = b.shape[1]
    return pl.pallas_call(
        grads_kernel,
        grid=(model // rows,),
        in_specs=[pl.BlockSpec((count, rows), lambda i: (0, i)), whole(b)],
        out_specs=pl.BlockSpec((rows, width), lambda i: (i, 0)),
        out_shape=jax.ShapeDtypeStruct((model, width), WIDE),
        compiler_params=params(),
        cost_estimate=TINY,
    )(a, b)


def tied(value, *others):
    return lax.optimization_barrier((value, *others))[0]


def together(*values):
    return lax.optimization_barrier(values)


def shifted(block, distance, period):
    count = lax.axis_size("z")
    route = [
        (i - distance, i)
        for i in range(count)
        if 0 <= i - distance < count and (i - distance) // period == i // period
    ]
    return lax.ppermute(block, "z", route)


def over(block, axis):
    return lax.ppermute(block, axis, SWAP)


def across(block):
    return lax.ppermute(block, ("y", "x"), [(i, 3 - i) for i in range(4)])


def plane_step_one(block):
    return over(block, "x"), over(block, "y")


def plane_step_two(over_x, over_y):
    half = over_x.shape[0] // 2
    return over(over_y[:half], "x"), over(over_x[half:], "y")


def plane_join(*mine):
    return join(list(mine) + [over(part, "c") for part in mine])


def added_pair(one, two):
    return (one.astype(F32) + two.astype(F32)).astype(WIDE)


def landed(values, *flights):
    held = [getattr(holder, field) for holder, field in flights]
    values, held = lax.optimization_barrier((values, held))
    for (holder, field), value in zip(flights, held):
        setattr(holder, field, value)
    return values


def plane_sum_one(total):
    own = total.shape[0] // 4
    half = own // 2
    return over(total[3 * own : 3 * own + half], "x"), over(total[3 * own + half :], "y")


def plane_sum_two(total, top, bottom):
    own = total.shape[0] // 4
    half = own // 2
    wide = lambda a, b: (a.astype(F32) + b.astype(F32)).astype(WIDE)
    to_x = jnp.concatenate(
        [total[own : own + half], wide(total[own + half : 2 * own], bottom)], axis=0
    )
    to_y = jnp.concatenate(
        [wide(total[2 * own : 2 * own + half], top), total[2 * own + half : 3 * own]], axis=0
    )
    return over(to_x, "x"), over(to_y, "y")


def added(total, *parts):
    own = total.shape[0] // 4
    return sum((part.astype(F32) for part in parts), total[:own].astype(F32))


def kept_columns(block, first_y):
    half = block.shape[1] // 2
    keep = jnp.where(first_y, block[:, :half], block[:, half:])
    give = jnp.where(first_y, block[:, half:], block[:, :half])
    return keep, give


def both_rows(keep, got, first_y):
    return jnp.concatenate([jnp.where(first_y, keep, got), jnp.where(first_y, got, keep)], axis=0)


def share_columns(block, first_y, *after):
    keep, give = kept_columns(block, first_y)
    if after:
        give = tied(give, *after)
    return both_rows(keep, over(give, "y"), first_y)


class Unshare:
    def __init__(self, block, first_y):
        half = block.shape[0] // 2
        self.first_y = first_y
        self.keep = jnp.where(first_y, block[:half], block[half:])
        self.got = over(jnp.where(first_y, block[half:], block[:half]), "y")

    def both(self):
        return (
            jnp.where(self.first_y, self.keep, self.got),
            jnp.where(self.first_y, self.got, self.keep),
        )


class SpreadGather:
    def __init__(self, block, first_y):
        self.rows, self.first_y = block.shape[0], first_y
        whole = gather_z(block)
        half = whole.shape[1] // 2
        self.keep = jnp.where(first_y, whole[:, :half], whole[:, half:])
        self.got = over(jnp.where(first_y, whole[:, half:], whole[:, :half]), "y")

    def total(self):
        count, width = self.keep.shape[0] // self.rows, self.keep.shape[1]
        sides = [
            jnp.where(self.first_y, a, b).reshape(count, self.rows, width)
            for a, b in ((self.keep, self.got), (self.got, self.keep))
        ]
        return jnp.concatenate(sides, axis=1).reshape(2 * count * self.rows, width)


def spread_sum(term, rows, first_y):
    blocks = term.reshape(-1, 2, rows, term.shape[1])
    pick = lambda a, b: jnp.where(first_y, a, b).reshape(-1, term.shape[1])
    keep = pick(blocks[:, 0], blocks[:, 1])
    got = over(pick(blocks[:, 1], blocks[:, 0]), "y")
    both = jnp.where(
        first_y,
        jnp.concatenate([keep, got], axis=1),
        jnp.concatenate([got, keep], axis=1),
    )
    return both


def gather_z(block):
    return lax.all_gather(block, "z", axis=0, tiled=True)


def sum_z(block):
    return lax.psum_scatter(block.astype(WIDE), "z", scatter_dimension=0, tiled=True)


def padded(block, multiple=128):
    extra = -block.shape[1] % multiple
    return jnp.pad(block, ((0, 0), (0, extra))) if extra else block


def norm_back(gradient, normed, inverse, gain_vec):
    scaled = gradient * gain_vec
    return inverse * (scaled - normed * jnp.mean(scaled * normed, axis=-1, keepdims=True))


def per_device(
    inputs,
    segments,
    positions,
    gain_attn,
    query_weight,
    key_weight,
    value_weight,
    out_weight,
    gain_mlp,
    gate_weight,
    up_weight,
    down_weight,
    cotangent,
):
    own = inputs.shape[0]
    half, count = 4 * own, 8 * own
    length = segments.shape[0] // SEQS
    reach = (DOC_MOST - 2) // count + 1
    period = lax.axis_size("z")
    if length % count == 0:
        period = length // count
        reach = min(reach, period - 1)
    span = (reach + 1) * count
    z, y = lax.axis_index("z"), lax.axis_index("y")
    x, c = lax.axis_index("x"), lax.axis_index("c")
    first_y = y == 0

    w_q, w_k, w_v, w_g, w_u = [
        w.astype(WIDE) for w in (query_weight, key_weight, value_weight, gate_weight, up_weight)
    ]
    w_o, w_d = out_weight.T.astype(WIDE), down_weight.T.astype(WIDE)
    nq, nk, nf = w_q.shape[1] // 2, w_k.shape[1] // 2, w_g.shape[1] // 2
    rows_w = w_q.shape[0]
    halves = lambda w: (w[:, : w.shape[1] // 2], w[:, w.shape[1] // 2 :])
    gain_pair = jnp.stack([gain_attn, gain_mlp] * 2, 1).astype(WIDE)
    chunks = (slice(0, CHUNK), slice(CHUNK, nf))
    triple = lambda cut: jnp.concatenate(
        [padded(halves(w)[i][:, cut]) for i in range(2) for w in (w_d, w_g, w_u)], axis=1
    )
    flow_o = SpreadGather(w_o, first_y)
    near_a = share_columns(
        jnp.concatenate(
            [
                padded(jnp.concatenate([halves(w)[i] for w in (w_q, w_k, w_v, gain_pair)], axis=1))
                for i in range(2)
            ],
            axis=1,
        ),
        first_y,
    )
    full_a = gather_z(near_a)
    x_one = over(inputs, "x"), over(tied(inputs, near_a), "y")
    x_two = plane_step_two(*x_one)
    x_all = plane_join(inputs, *x_one, *x_two)
    near_c = [share_columns(triple(chunks[0]), first_y, x_all)]
    full_c = [gather_z(near_c[0])]
    first_gain = nq + 2 * nk
    gains = full_a[:, first_gain : first_gain + 2].astype(F32)
    gain_first, gain_second = gains[:, 0], gains[:, 1]

    other_positions = lax.ppermute(positions, "y", SWAP)
    token_positions = jnp.where(
        first_y,
        jnp.concatenate([positions, other_positions]),
        jnp.concatenate([other_positions, positions]),
    )
    frequency = rope_base ** (-(jnp.arange(HD // 2, dtype=F32) * 2.0 / HD))
    angles = frequency[:, None] * token_positions.astype(F32)[None, :]
    cos_tab, sin_tab = jnp.cos(angles), jnp.sin(angles)
    places = jnp.arange(8, dtype=jnp.int32)
    flips = places ^ (y * 4 + x * 2 + c).astype(jnp.int32)
    index = (flips % 2) * 4 + flips // 2
    padded_segs = jnp.concatenate([jnp.full((reach * count,), -1, jnp.int32), segments])
    key_segs = lax.dynamic_slice_in_dim(padded_segs, z * count, span, 0)
    query_segs = lax.dynamic_slice_in_dim(segments, z * count, count, 0)
    starts = jnp.sum((key_segs[:, None] < query_segs[None, :]).astype(jnp.int32), axis=0)
    first_rows = jnp.arange(count // BQ, dtype=jnp.int32) * BQ
    lo = starts[first_rows] // KB
    hi = (reach * count + first_rows + BQ + KB - 1) // KB
    full_lo = jnp.clip((starts[first_rows + BQ - 1] + KB - 1) // KB, lo, hi)
    full_hi = jnp.clip((reach * count + first_rows + 1) // KB, full_lo, hi)
    bounds = jnp.stack([lo, full_lo, full_hi, hi])
    own_key = reach * count
    own_bounds = jnp.maximum(bounds, own_key // KB)
    far_bounds = jnp.minimum(bounds, own_key // KB)
    starts = starts[None, :]

    h_one, qkv = project(x_all, gain_first[None, :], full_a)
    near_c.append(share_columns(triple(chunks[1]), first_y, qkv))
    full_c.append(gather_z(near_c[1]))
    turned = to_columns(qkv, index, cos_tab, sin_tab, GROUP + 1, GROUP + 2)
    q_cols, kv_own = turned[: GROUP * HD], turned[GROUP * HD :]
    far_kv = [shifted(kv_own, distance, period) for distance in range(reach, 0, -1)]
    far_kv = [shifted(kv_own, distance, period) for distance in range(reach, 0, -1)]
    kv_own = landed(kv_own, (flow_o, "got"))
    cot_one = plane_step_one(tied(cotangent, kv_own))
    own_part = attend(q_cols, kv_own, starts, own_bounds, (own_key, own_key), (), F32)
    own_part, far_kv, near_0 = lax.optimization_barrier((own_part, far_kv, near_c[0]))
    if reach:
        far_kv = jnp.concatenate(far_kv, axis=1)
        out_cols, logs = attend(q_cols, far_kv, starts, far_bounds, (own_key, 0), own_part, WIDE)
    else:
        out_cols, logs = own_part[0].astype(WIDE), own_part[1]
    out_cols, cot_one, _ = lax.optimization_barrier((out_cols, cot_one, near_c[1]))
    cot_two = plane_step_two(*cot_one)
    full_o = flow_o.total()
    attended = to_rows(out_cols, index, cos_tab, sin_tab, 0, GROUP, GROUP * HD)
    input_f32 = inputs.astype(F32)
    inverse_one = lax.rsqrt(jnp.mean(input_f32 * input_f32, axis=-1, keepdims=True) + eps)
    normed_one = input_f32 * inverse_one
    mid_got = over(dot(attended[half:], full_o, 1, 1).astype(WIDE), "c")
    mid_total = (dot(attended[:half], full_o, 1, 1) + mid_got.astype(F32)).astype(WIDE)
    mid_total, *cot_two = together(mid_total, *cot_two)
    mid_far = plane_sum_one(mid_total)
    mid_near = plane_sum_two(mid_total, *mid_far)
    grad_mix = plane_join(cotangent, *cot_one, *cot_two)
    *mid_near, grad_mix = together(*mid_near, grad_mix)
    x_mid = input_f32 + added(mid_total, *mid_near)

    inverse_two = lax.rsqrt(jnp.mean(x_mid * x_mid, axis=-1, keepdims=True) + eps)
    normed_two = x_mid * inverse_two
    h_own = (normed_two * gain_second).astype(WIDE)
    h_step = plane_step_one(h_own)
    h_two = plane_join(h_own, *h_step, *plane_step_two(*h_step))
    h_two, grad_mix = together(h_two, grad_mix)
    other_1 = hidden_units(h_two, grad_mix, full_c[0], half, half)
    mine_1 = hidden_units(h_two, grad_mix, full_c[0], 0, half)
    term_1 = unit_grads(h_two, grad_mix, mine_1[0], other_1[0])
    full_c[1], other_1, mine_1, term_1 = lax.optimization_barrier(
        (full_c[1], other_1, mine_1, term_1)
    )
    sums = [sum_z(term_1)]
    acts_other, back_other, out_other = hidden_units(
        h_two, grad_mix, full_c[1], half, half, other_1[1:]
    )
    back_got, out_got = over(back_other, "c"), over(out_other, "c")
    acts_mine, back_mine, out_mine = hidden_units(h_two, grad_mix, full_c[1], 0, half, mine_1[1:])
    back_total = added_pair(back_mine, back_got)
    back_far = plane_sum_one(back_total)
    term_2 = unit_grads(h_two, grad_mix, acts_mine, acts_other)
    back_near = plane_sum_two(back_total, *back_far)
    *back_near, term_2 = together(*back_near, term_2)
    sums.append(sum_z(term_2))
    grad_h_two = added(back_total, *back_near)
    grad_mid = cotangent.astype(F32) + norm_back(grad_h_two, normed_two, inverse_two, gain_second)
    branch_own = grad_mid.astype(WIDE)
    branch_one = plane_step_one(branch_own)
    branch_two = plane_step_two(*branch_one)
    out_total = added_pair(out_mine, out_got)
    grad_branch = plane_join(branch_own, *branch_one, *branch_two)
    owned = [Unshare(tied(sums[0], *branch_two), first_y)]
    grad_branch, out_total = together(grad_branch, out_total)

    grad_attended = narrow(grad_branch, full_o)
    grad_cols = to_columns(grad_attended, index, cos_tab, sin_tab, 0, GROUP)
    grad_cols, out_total = landed((grad_cols, out_total), (owned[0], "got"))
    out_sends = [
        over(out_total[own : 2 * own], "x"),
        over(out_total[2 * own : 3 * own], "y"),
        across(out_total[3 * own :]),
    ]
    back = functools.partial(attend_back, q_cols)
    prior, far_got = (), []
    if reach:
        dq_far, dkv_far = back(
            far_kv, starts, far_bounds, (own_key, 0), out_cols, logs, grad_cols
        )
        prior = (dq_far,)
        far_got = [
            shifted(
                dkv_far[:, (reach - d) * count : (reach - d + 1) * count].astype(WIDE), -d, period
            )
            for d in range(1, reach + 1)
        ]
    out_term = weight_grads(grad_branch, tied(attended, *prior))
    kv_own, out_term = together(kv_own, out_term)
    dq_cols, dkv_cols = back(
        kv_own, starts, own_bounds, (own_key, own_key), out_cols, logs, grad_cols, prior
    )
    dkv_cols, out_sends, far_got = lax.optimization_barrier((dkv_cols, out_sends, far_got))
    output = (x_mid + added(out_total, *out_sends)).astype(WIDE)
    dkv_own = sum((part.astype(F32) for part in far_got), dkv_cols)
    out_term = spread_sum(tied(out_term, dkv_cols), w_o.shape[0], first_y)
    grad_qkv = to_rows(
        jnp.concatenate([dq_cols, dkv_own], axis=0),
        index,
        cos_tab,
        sin_tab,
        GROUP + 1,
        GROUP + 2,
        full_a.shape[1],
    )
    qkv_part = weight_grads(h_one, grad_qkv)
    grad_qkv, qkv_part, out_term = together(grad_qkv, qkv_part, out_term)
    one_got = over(dot(grad_qkv[half:], full_a, 1, 1).astype(WIDE), "c")
    qkv_part, sums[1], one_got = together(qkv_part, sums[1], one_got)
    one_total = (dot(grad_qkv[:half], full_a, 1, 1) + one_got.astype(F32)).astype(WIDE)
    qkv_grad = sum_z(qkv_part)
    owned.append(Unshare(sums[1], first_y))
    one_far = plane_sum_one(one_total)
    one_far = landed(one_far, (owned[1], "got"))
    one_near = plane_sum_two(one_total, *one_far)
    qkv_raw = qkv_grad
    out_grad = sum_z(tied(out_term, qkv_raw))
    owned_a = Unshare(qkv_grad, first_y)
    *one_near, qkv_grad = together(*one_near, qkv_grad)
    grad_h_one = added(one_total, *one_near)
    input_grad = (grad_mid + norm_back(grad_h_one, normed_one, inverse_one, gain_first)).astype(
        WIDE
    )

    input_grad = landed(input_grad, (owned_a, "got"))
    for part in owned:
        part.keep, part.got, _ = lax.optimization_barrier((part.keep, part.got, qkv_raw))
    owned = [part.both() for part in owned]
    kept = [CHUNK, nf - CHUNK]
    width = [full.shape[1] // 3 for full in full_c]

    def unit_columns(k):
        return jnp.concatenate(
            [
                owned[j][i][:, k * width[j] : k * width[j] + kept[j]]
                for i in range(2)
                for j in range(2)
            ],
            axis=1,
        ).astype(F32)

    down_out, gate_out, up_out = unit_columns(0).T, unit_columns(1), unit_columns(2)
    one, two = owned_a.both()
    pick = lambda a, b: jnp.concatenate([one[:, a:b], two[:, a:b]], axis=1).astype(F32)
    q_out, k_out, v_out = pick(0, nq), pick(nq, nq + nk), pick(nq + nk, nq + 2 * nk)

    def row_sums(weight, grad):
        return jnp.sum(weight.astype(F32) * grad, axis=1)

    gain_sums = jnp.stack(
        [
            row_sums(w_q, q_out) + row_sums(w_k, k_out) + row_sums(w_v, v_out),
            row_sums(w_g, gate_out) + row_sums(w_u, up_out),
        ]
    )
    gain_sums = gain_sums + lax.ppermute(gain_sums, "x", SWAP)
    gain_sums = gain_sums + lax.ppermute(gain_sums, "c", SWAP)
    gain_sums, out_grad = together(gain_sums, out_grad)
    o_out = as_f32(out_grad).T
    gain_one_out = gain_sums[0] / gain_attn.astype(WIDE).astype(F32)
    gain_two_out = gain_sums[1] / gain_mlp.astype(WIDE).astype(F32)
    return (
        output,
        input_grad,
        gain_one_out,
        q_out,
        k_out,
        v_out,
        o_out,
        gain_two_out,
        gate_out,
        up_out,
        down_out,
    )


def solution(mesh):
    seq, tensor = mesh.shape["seq"], mesh.shape["tensor"]
    grid = Mesh(
        mesh.devices.reshape(seq // 2, 2, tensor // 2, 2), ("z", "y", "x", "c")
    )
    rows, cols = ("z", "y"), ("x", "c")
    tokens, weight, weight_t = P(rows + cols, None), P(rows, cols), P(cols, rows)
    in_specs = (
        tokens,
        P(),
        P(rows),
        P(rows),
        weight,
        weight,
        weight,
        weight_t,
        P(rows),
        weight,
        weight,
        weight_t,
        tokens,
    )
    out_specs = (
        tokens,
        tokens,
        P(rows),
        weight,
        weight,
        weight,
        weight_t,
        P(rows),
        weight,
        weight,
        weight_t,
    )
    return jax.shard_map(
        per_device, mesh=grid, in_specs=in_specs, out_specs=out_specs, check_vma=False
    )
```

```python
import functools

import jax
import jax.numpy as jnp
from jax import lax
from jax.experimental import pallas as pl
from jax.experimental.pallas import tpu as pltpu
from jax.sharding import Mesh
from jax.sharding import PartitionSpec as P

HEADS = 32
KV = 8
HD = 80
SEQS = 2
DOC_MOST = 2000
GROUP = HEADS // KV

eps = 1e-05
rope_base = 10000.0
LOG2E = 1.4426950408889634
SCORE_LOG2 = HD ** (-0.5) * LOG2E
SCORE_SCALE = HD ** (-0.5)
LOW = -1e30
BQ = 256
CHUNK = 384
KB = 256
WIDE = jnp.bfloat16
F32 = jnp.float32
VMEM_BYTES = 48 * 1024 * 1024

SWAP = [(0, 1), (1, 0)]


def dot(a, b, ca, cb):
    return lax.dot_general(a, b, (((ca,), (cb,)), ((), ())), preferred_element_type=F32)


def turn_kernel(rotary, heads, index_ref, rows_ref, cos_ref, sin_ref, out_ref):
    own = rows_ref.shape[0] // 8
    half = HD // 2
    for pair in range(4):
        parts = [
            rows_ref[pl.ds(pl.multiple_of(index_ref[2 * pair + k] * own, own), own), :].astype(F32)
            for k in range(2)
        ]
        turned = jnp.concatenate(parts, axis=0).T
        lanes = slice(pair * 2 * own, (pair + 1) * 2 * own)
        cos_tab, sin_tab = cos_ref[:, lanes], sin_ref[:, lanes]
        for h in range(heads):
            front, back = turned[h * HD : h * HD + half], turned[h * HD + half : (h + 1) * HD]
            if h < rotary:
                front, back = front * cos_tab - back * sin_tab, back * cos_tab + front * sin_tab
            out_ref[h * HD : (h + 1) * HD, lanes] = jnp.concatenate([front, back], axis=0).astype(
                out_ref.dtype
            )


def to_columns(rows, index, cos_tab, sin_tab, rotary, heads):
    count = rows.shape[0]
    full = lambda shape: pl.BlockSpec(shape, lambda i, s: (0, 0))
    return pl.pallas_call(
        functools.partial(turn_kernel, rotary, heads),
        grid_spec=pltpu.PrefetchScalarGridSpec(
            num_scalar_prefetch=1,
            grid=(1,),
            in_specs=[full(rows.shape), full(cos_tab.shape), full(sin_tab.shape)],
            out_specs=full((heads * HD, count)),
        ),
        out_shape=jax.ShapeDtypeStruct((heads * HD, count), WIDE),
        compiler_params=pltpu.CompilerParams(vmem_limit_bytes=VMEM_BYTES),
        cost_estimate=pl.CostEstimate(flops=10**6, bytes_accessed=10**5, transcendentals=0),
    )(index, rows, cos_tab, sin_tab)


def back_kernel(rotary, heads, index_ref, cols_ref, cos_ref, sin_ref, out_ref):
    own = cols_ref.shape[1] // 8
    half = HD // 2
    width = out_ref.shape[1]
    for pair in range(4):
        lanes = slice(pair * 2 * own, (pair + 1) * 2 * own)
        cos_tab, sin_tab = cos_ref[:, lanes], sin_ref[:, lanes]
        parts = []
        for h in range(heads):
            front = cols_ref[h * HD : h * HD + half, lanes].astype(F32)
            back = cols_ref[h * HD + half : (h + 1) * HD, lanes].astype(F32)
            if h < rotary:
                front, back = front * cos_tab + back * sin_tab, back * cos_tab - front * sin_tab
            parts += [front, back]
        if width > heads * HD:
            parts.append(jnp.zeros((width - heads * HD, 2 * own), F32))
        rows = jnp.concatenate(parts, axis=0).T.astype(out_ref.dtype)
        for k in range(2):
            first = pl.multiple_of(index_ref[2 * pair + k] * own, own)
            out_ref[pl.ds(first, own), :] = rows[k * own : (k + 1) * own]


def to_rows(cols, index, cos_tab, sin_tab, rotary, heads, width):
    count = cols.shape[1]
    full = lambda shape: pl.BlockSpec(shape, lambda i, s: (0, 0))
    return pl.pallas_call(
        functools.partial(back_kernel, rotary, heads),
        grid_spec=pltpu.PrefetchScalarGridSpec(
            num_scalar_prefetch=1,
            grid=(1,),
            in_specs=[full(cols.shape), full(cos_tab.shape), full(sin_tab.shape)],
            out_specs=full((count, width)),
        ),
        out_shape=jax.ShapeDtypeStruct((count, width), WIDE),
        compiler_params=pltpu.CompilerParams(vmem_limit_bytes=VMEM_BYTES),
        cost_estimate=pl.CostEstimate(flops=10**6, bytes_accessed=10**5, transcendentals=0),
    )(index, cols, cos_tab, sin_tab)


def allowed_mask(block, starts, own_places):
    places = block * KB + lax.broadcasted_iota(jnp.int32, (KB, 1), 0)
    return (places >= starts) & (places <= own_places)


def attend_kernel(places, bounds_ref, q_ref, kv_ref, start_ref, *refs):
    first_query, first_key = places
    *prior, out_ref, log_ref, k_rows, acc = refs
    step = pl.program_id(0)
    span = kv_ref.shape[1]

    @pl.when(step == 0)
    def _():
        for j in range(span // KB):
            k_rows[j * KB : (j + 1) * KB, :] = (
                kv_ref[0:HD, j * KB : (j + 1) * KB].astype(F32).T.astype(WIDE)
            )

    starts = start_ref[0:1, :]
    own_places = first_query + step * BQ + lax.broadcasted_iota(jnp.int32, (1, BQ), 1)
    if prior:
        for h in range(GROUP):
            acc[h] = prior[0][h * HD : (h + 1) * HD, :]
    else:
        acc[...] = jnp.zeros_like(acc)

    def one(masked, block, carry):
        first = pl.multiple_of(block * KB - first_key, KB)
        keys = k_rows[pl.ds(first, KB), :]
        values = kv_ref[HD : 2 * HD, pl.ds(first, KB)]
        if masked:
            mask = allowed_mask(block, starts, own_places)
        fresh = []
        for h in range(GROUP):
            top, total = carry[2 * h], carry[2 * h + 1]
            scores = dot(keys, q_ref[h * HD : (h + 1) * HD, :], 1, 0) * SCORE_LOG2
            if masked:
                scores = jnp.where(mask, scores, LOW)
            new_top = jnp.maximum(top, jnp.max(scores, axis=0, keepdims=True))
            probs = jnp.exp2(scores - new_top)
            fade = jnp.exp2(top - new_top)
            total = fade * total + jnp.sum(probs, axis=0, keepdims=True)
            acc[h] = fade * acc[h] + dot(values, probs.astype(WIDE), 1, 0)
            fresh += [new_top, total]
        return tuple(fresh)

    carry = (jnp.full((1, BQ), LOW, F32), jnp.zeros((1, BQ), F32)) * GROUP
    if prior:
        carry = sum(((prior[1][h : h + 1, :], jnp.ones((1, BQ), F32)) for h in range(GROUP)), ())
    lo, full_lo, full_hi, hi = [bounds_ref[k, step] for k in range(4)]
    carry = lax.fori_loop(lo, full_lo, functools.partial(one, True), carry)
    carry = lax.fori_loop(full_lo, full_hi, functools.partial(one, False), carry)
    carry = lax.fori_loop(full_hi, hi, functools.partial(one, True), carry)
    for h in range(GROUP):
        top, total = carry[2 * h], carry[2 * h + 1]
        out_ref[h * HD : (h + 1) * HD, :] = (acc[h] / total).astype(out_ref.dtype)
        log_ref[h : h + 1, :] = top + jnp.log2(total)


def attend(q_cols, kv_cols, starts, bounds, places, prior, out_type):
    count, span = q_cols.shape[1], kv_cols.shape[1]
    wide_block = pl.BlockSpec((GROUP * HD, BQ), lambda i, s: (0, i))
    log_block = pl.BlockSpec((8, BQ), lambda i, s: (0, i))
    return pl.pallas_call(
        functools.partial(attend_kernel, places),
        grid_spec=pltpu.PrefetchScalarGridSpec(
            num_scalar_prefetch=1,
            grid=(count // BQ,),
            in_specs=[
                wide_block,
                pl.BlockSpec((2 * HD, span), lambda i, s: (0, 0)),
                pl.BlockSpec((1, BQ), lambda i, s: (0, i)),
            ]
            + [wide_block, log_block][: len(prior)],
            out_specs=[wide_block, log_block],
            scratch_shapes=[pltpu.VMEM((span, HD), WIDE), pltpu.VMEM((GROUP, HD, BQ), F32)],
        ),
        out_shape=[
            jax.ShapeDtypeStruct((GROUP * HD, count), out_type),
            jax.ShapeDtypeStruct((8, count), F32),
        ],
        compiler_params=pltpu.CompilerParams(vmem_limit_bytes=VMEM_BYTES),
        cost_estimate=pl.CostEstimate(flops=10**6, bytes_accessed=10**5, transcendentals=0),
    )(bounds, q_cols, kv_cols, starts, *prior)


def attend_back_kernel(places, bounds_ref, q_ref, kv_ref, start_ref, out_ref, log_ref, grad_ref, *refs):
    first_query, first_key = places
    *prior, dq_ref, dkv_ref, k_rows, v_rows, q_rows, g_rows, dk, dv, probs_all, grads_all, dq = refs
    step = pl.program_id(0)
    span = kv_ref.shape[1]

    @pl.when(step == 0)
    def _():
        for j in range(span // KB):
            lanes = slice(j * KB, (j + 1) * KB)
            k_rows[lanes, :] = kv_ref[0:HD, lanes].astype(F32).T.astype(WIDE)
            v_rows[lanes, :] = kv_ref[HD : 2 * HD, lanes].astype(F32).T.astype(WIDE)
        dk[...] = jnp.zeros_like(dk)
        dv[...] = jnp.zeros_like(dv)

    starts = start_ref[0:1, :]
    own_places = first_query + step * BQ + lax.broadcasted_iota(jnp.int32, (1, BQ), 1)
    dq[...] = jnp.zeros_like(dq)
    deltas = []
    for h in range(GROUP):
        part = slice(h * HD, (h + 1) * HD)
        q_f32, g_f32 = q_ref[part, :].astype(F32), grad_ref[part, :].astype(F32)
        q_rows[h * BQ : (h + 1) * BQ, :] = q_f32.T.astype(WIDE)
        g_rows[h * BQ : (h + 1) * BQ, :] = g_f32.T.astype(WIDE)
        deltas.append(jnp.sum(g_f32 * out_ref[part, :].astype(F32), axis=0, keepdims=True))

    def one(masked, block, carry):
        first = pl.multiple_of(block * KB - first_key, KB)
        rows = pl.ds(first, KB)
        keys, values = k_rows[rows, :], v_rows[rows, :]
        key_cols = kv_ref[0:HD, rows]
        if masked:
            mask = allowed_mask(block, starts, own_places)
        for h in range(GROUP):
            part = slice(h * HD, (h + 1) * HD)
            lanes = slice(h * BQ, (h + 1) * BQ)
            scores = dot(keys, q_ref[part, :], 1, 0) * SCORE_LOG2 - log_ref[h : h + 1, :]
            if masked:
                scores = jnp.where(mask, scores, LOW)
            probs = jnp.exp2(scores)
            grad_probs = dot(values, grad_ref[part, :], 1, 0)
            grad_scores = (probs * (grad_probs - deltas[h])).astype(WIDE)
            probs_all[:, lanes] = probs.astype(WIDE)
            grads_all[:, lanes] = grad_scores
            dq[h] += dot(key_cols, grad_scores, 1, 0)
        dv[rows, :] += dot(probs_all[...], g_rows[...], 1, 0)
        dk[rows, :] += dot(grads_all[...], q_rows[...], 1, 0)
        return carry

    lo, full_lo, full_hi, hi = [bounds_ref[k, step] for k in range(4)]
    lax.fori_loop(lo, full_lo, functools.partial(one, True), 0)
    lax.fori_loop(full_lo, full_hi, functools.partial(one, False), 0)
    lax.fori_loop(full_hi, hi, functools.partial(one, True), 0)
    for h in range(GROUP):
        part = slice(h * HD, (h + 1) * HD)
        dq_ref[part, :] = dq[h] * SCORE_SCALE + (prior[0][part, :] if prior else 0.0)

    @pl.when(step == pl.num_programs(0) - 1)
    def _():
        for j in range(span // KB):
            lanes = slice(j * KB, (j + 1) * KB)
            dkv_ref[0:HD, lanes] = dk[lanes, :].T * SCORE_SCALE
            dkv_ref[HD : 2 * HD, lanes] = dv[lanes, :].T


def attend_back(q_cols, kv_cols, starts, bounds, places, out_cols, logs, grad_cols, prior=()):
    count, span = q_cols.shape[1], kv_cols.shape[1]
    wide_block = pl.BlockSpec((GROUP * HD, BQ), lambda i, s: (0, i))
    return pl.pallas_call(
        functools.partial(attend_back_kernel, places),
        grid_spec=pltpu.PrefetchScalarGridSpec(
            num_scalar_prefetch=1,
            grid=(count // BQ,),
            in_specs=[
                wide_block,
                pl.BlockSpec((2 * HD, span), lambda i, s: (0, 0)),
                pl.BlockSpec((1, BQ), lambda i, s: (0, i)),
                wide_block,
                pl.BlockSpec((8, BQ), lambda i, s: (0, i)),
                wide_block,
            ]
            + [wide_block] * len(prior),
            out_specs=[wide_block, pl.BlockSpec((2 * HD, span), lambda i, s: (0, 0))],
            scratch_shapes=[
                pltpu.VMEM((span, HD), WIDE),
                pltpu.VMEM((span, HD), WIDE),
                pltpu.VMEM((GROUP * BQ, HD), WIDE),
                pltpu.VMEM((GROUP * BQ, HD), WIDE),
                pltpu.VMEM((span, HD), F32),
                pltpu.VMEM((span, HD), F32),
                pltpu.VMEM((KB, GROUP * BQ), WIDE),
                pltpu.VMEM((KB, GROUP * BQ), WIDE),
                pltpu.VMEM((GROUP, HD, BQ), F32),
            ],
        ),
        out_shape=[
            jax.ShapeDtypeStruct((GROUP * HD, count), F32),
            jax.ShapeDtypeStruct((2 * HD, span), F32),
        ],
        compiler_params=pltpu.CompilerParams(vmem_limit_bytes=VMEM_BYTES),
        cost_estimate=pl.CostEstimate(flops=10**6, bytes_accessed=10**5, transcendentals=0),
    )(bounds, q_cols, kv_cols, starts, out_cols, logs, grad_cols, *prior)


TINY = pl.CostEstimate(flops=10**6, bytes_accessed=10**5, transcendentals=0)
ANY = pl.BlockSpec(memory_space=pl.ANY)


def params():
    return pltpu.CompilerParams(vmem_limit_bytes=VMEM_BYTES)


def join_kernel(*refs):
    *parts, out, whole, sems = refs
    pairs, first = [], 0
    for k, part in enumerate(parts):
        rows = pl.ds(first, part.shape[0])
        pairs.append(
            (
                pltpu.make_async_copy(part, whole.at[rows, :], sems.at[0, k]),
                pltpu.make_async_copy(whole.at[rows, :], out.at[rows, :], sems.at[1, k]),
            )
        )
        first += part.shape[0]
    for copy_in, _ in pairs:
        copy_in.start()
    for copy_in, copy_out in pairs:
        copy_in.wait()
        copy_out.start()
    for _, copy_out in pairs:
        copy_out.wait()


def join(parts):
    rows = sum(part.shape[0] for part in parts)
    return pl.pallas_call(
        join_kernel,
        in_specs=[ANY] * len(parts),
        out_specs=ANY,
        out_shape=jax.ShapeDtypeStruct((rows, parts[0].shape[1]), parts[0].dtype),
        scratch_shapes=[
            pltpu.VMEM((rows, parts[0].shape[1]), parts[0].dtype),
            pltpu.SemaphoreType.DMA((2, len(parts))),
        ],
        compiler_params=params(),
        cost_estimate=TINY,
    )(*parts)


def project_kernel(x_ref, gain_ref, weight_ref, h_ref, out_ref):
    x = x_ref[...].astype(F32)
    inverse = lax.rsqrt(jnp.mean(x * x, axis=-1, keepdims=True) + eps)
    h = (x * inverse * gain_ref[...]).astype(WIDE)
    h_ref[...] = h
    out_ref[...] = dot(h, weight_ref[...], 1, 0)


def project(x_all, gain_row, weights, rows=256):
    count, model = x_all.shape
    width = weights.shape[1]
    return pl.pallas_call(
        project_kernel,
        grid=(count // rows,),
        in_specs=[
            pl.BlockSpec((rows, model), lambda i: (i, 0)),
            pl.BlockSpec((1, model), lambda i: (0, 0)),
            pl.BlockSpec(weights.shape, lambda i: (0, 0), pipeline_mode=pl.Buffered(1)),
        ],
        out_specs=[
            pl.BlockSpec((rows, model), lambda i: (i, 0)),
            pl.BlockSpec((rows, width), lambda i: (i, 0)),
        ],
        out_shape=[
            jax.ShapeDtypeStruct((count, model), WIDE),
            jax.ShapeDtypeStruct((count, width), F32),
        ],
        compiler_params=pltpu.CompilerParams(vmem_limit_bytes=VMEM_BYTES),
        cost_estimate=pl.CostEstimate(flops=10**6, bytes_accessed=10**5, transcendentals=0),
    )(x_all, gain_row, weights)


def narrow_kernel(a_ref, weight_ref, out_ref):
    out_ref[...] = dot(a_ref[...], weight_ref[...], 1, 0).astype(out_ref.dtype)


def whole(array):
    return pl.BlockSpec(array.shape, lambda i: (0, 0), pipeline_mode=pl.Buffered(1))


def narrow(a, weight, rows=256):
    count, model = a.shape
    return pl.pallas_call(
        narrow_kernel,
        grid=(count // rows,),
        in_specs=[pl.BlockSpec((rows, model), lambda i: (i, 0)), whole(weight)],
        out_specs=pl.BlockSpec((rows, weight.shape[1]), lambda i: (i, 0)),
        out_shape=jax.ShapeDtypeStruct((count, weight.shape[1]), WIDE),
        compiler_params=params(),
        cost_estimate=TINY,
    )(a, weight)


def units_kernel(has_prior, h_ref, cot_ref, weight_ref, *refs):
    *prior, acts_ref, back_ref, out_ref = refs
    width = weight_ref.shape[1] // 3
    down_w, gate_w, up_w = [weight_ref[:, k * width : (k + 1) * width] for k in range(3)]
    gate = dot(h_ref[...], gate_w, 1, 0)
    up = dot(h_ref[...], up_w, 1, 0)
    grad = dot(cot_ref[...], down_w, 1, 0)
    sigma = 1.0 / (1.0 + jnp.exp(-gate))
    silu = gate * sigma
    hidden = (silu * up).astype(WIDE)
    grad_gate = (grad * up * sigma * (1.0 + gate * (1.0 - sigma))).astype(WIDE)
    grad_up = (grad * silu).astype(WIDE)
    acts_ref[:, :width] = hidden
    acts_ref[:, width : 2 * width] = grad_gate
    acts_ref[:, 2 * width :] = grad_up
    back = dot(grad_gate, gate_w, 1, 1) + dot(grad_up, up_w, 1, 1)
    out = dot(hidden, down_w, 1, 1)
    if has_prior:
        back, out = back + prior[0][...].astype(F32), out + prior[1][...].astype(F32)
    back_ref[...] = back.astype(WIDE)
    out_ref[...] = out.astype(WIDE)


def hidden_units(h_two, cot, weights, first, count, prior=(), rows=256):
    model, width = h_two.shape[1], weights.shape[1]
    at = first // rows
    block = lambda n: pl.BlockSpec((rows, n), lambda i: (i, 0))
    shape = lambda n: jax.ShapeDtypeStruct((count, n), WIDE)
    return pl.pallas_call(
        functools.partial(units_kernel, bool(prior)),
        grid=(count // rows,),
        in_specs=[pl.BlockSpec((rows, model), lambda i: (i + at, 0))] * 2
        + [whole(weights)]
        + [block(model)] * len(prior),
        out_specs=[block(width), block(model), block(model)],
        out_shape=[shape(width), shape(model), shape(model)],
        compiler_params=params(),
        cost_estimate=TINY,
    )(h_two, cot, weights, *prior)


def unit_grads_kernel(h_ref, cot_ref, mine_ref, other_ref, out_ref):
    half, width = mine_ref.shape[0], mine_ref.shape[1] // 3
    for a_ref, columns in ((cot_ref, slice(0, width)), (h_ref, slice(width, 3 * width))):
        out_ref[:, columns] = (
            dot(a_ref[:half, :], mine_ref[:, columns], 0, 0)
            + dot(a_ref[half:, :], other_ref[:, columns], 0, 0)
        ).astype(WIDE)


def unit_grads(h_two, cot, mine, other, rows=256):
    count, model = h_two.shape
    width = mine.shape[1]
    return pl.pallas_call(
        unit_grads_kernel,
        grid=(model // rows,),
        in_specs=[pl.BlockSpec((count, rows), lambda i: (0, i))] * 2 + [whole(mine), whole(other)],
        out_specs=pl.BlockSpec((rows, width), lambda i: (i, 0)),
        out_shape=jax.ShapeDtypeStruct((model, width), WIDE),
        compiler_params=params(),
        cost_estimate=TINY,
    )(h_two, cot, mine, other)


def as_f32_kernel(a_ref, out_ref):
    out_ref[...] = a_ref[...].astype(F32)


def as_f32(a):
    return pl.pallas_call(
        as_f32_kernel,
        out_shape=jax.ShapeDtypeStruct(a.shape, F32),
        compiler_params=pltpu.CompilerParams(vmem_limit_bytes=VMEM_BYTES // 2),
        cost_estimate=pl.CostEstimate(flops=3 * 10**10, bytes_accessed=10**5, transcendentals=0),
    )(a)


def grads_kernel(a_ref, b_ref, out_ref):
    out_ref[...] = dot(a_ref[...], b_ref[...], 0, 0).astype(WIDE)


def weight_grads(a, b, rows=256):
    count, model = a.shape
    width = b.shape[1]
    return pl.pallas_call(
        grads_kernel,
        grid=(model // rows,),
        in_specs=[pl.BlockSpec((count, rows), lambda i: (0, i)), whole(b)],
        out_specs=pl.BlockSpec((rows, width), lambda i: (i, 0)),
        out_shape=jax.ShapeDtypeStruct((model, width), WIDE),
        compiler_params=params(),
        cost_estimate=TINY,
    )(a, b)


def tied(value, *others):
    return lax.optimization_barrier((value, *others))[0]


def together(*values):
    return lax.optimization_barrier(values)


def shifted(block, distance, period):
    count = lax.axis_size("z")
    route = [
        (i - distance, i)
        for i in range(count)
        if 0 <= i - distance < count and (i - distance) // period == i // period
    ]
    return lax.ppermute(block, "z", route)


def over(block, axis):
    return lax.ppermute(block, axis, SWAP)


def across(block):
    return lax.ppermute(block, ("y", "x"), [(i, 3 - i) for i in range(4)])


def plane_step_one(block):
    return over(block, "x"), over(block, "y")


def plane_step_two(over_x, over_y):
    half = over_x.shape[0] // 2
    return over(over_y[:half], "x"), over(over_x[half:], "y")


def plane_join(*mine):
    return join(list(mine) + [over(part, "c") for part in mine])


def added_pair(one, two):
    return (one.astype(F32) + two.astype(F32)).astype(WIDE)


def landed(values, *flights):
    held = [getattr(holder, field) for holder, field in flights]
    values, held = lax.optimization_barrier((values, held))
    for (holder, field), value in zip(flights, held):
        setattr(holder, field, value)
    return values


def plane_sum_one(total):
    own = total.shape[0] // 4
    half = own // 2
    return over(total[3 * own : 3 * own + half], "x"), over(total[3 * own + half :], "y")


def plane_sum_two(total, top, bottom):
    own = total.shape[0] // 4
    half = own // 2
    wide = lambda a, b: (a.astype(F32) + b.astype(F32)).astype(WIDE)
    to_x = jnp.concatenate(
        [total[own : own + half], wide(total[own + half : 2 * own], bottom)], axis=0
    )
    to_y = jnp.concatenate(
        [wide(total[2 * own : 2 * own + half], top), total[2 * own + half : 3 * own]], axis=0
    )
    return over(to_x, "x"), over(to_y, "y")


def added(total, *parts):
    own = total.shape[0] // 4
    return sum((part.astype(F32) for part in parts), total[:own].astype(F32))


def kept_columns(block, first_y):
    half = block.shape[1] // 2
    keep = jnp.where(first_y, block[:, :half], block[:, half:])
    give = jnp.where(first_y, block[:, half:], block[:, :half])
    return keep, give


def both_rows(keep, got, first_y):
    return jnp.concatenate([jnp.where(first_y, keep, got), jnp.where(first_y, got, keep)], axis=0)


def share_columns(block, first_y, *after):
    keep, give = kept_columns(block, first_y)
    if after:
        give = tied(give, *after)
    return both_rows(keep, over(give, "y"), first_y)


class Unshare:
    def __init__(self, block, first_y):
        half = block.shape[0] // 2
        self.first_y = first_y
        self.keep = jnp.where(first_y, block[:half], block[half:])
        self.got = over(jnp.where(first_y, block[half:], block[:half]), "y")

    def both(self):
        return (
            jnp.where(self.first_y, self.keep, self.got),
            jnp.where(self.first_y, self.got, self.keep),
        )


class SpreadGather:
    def __init__(self, block, first_y):
        self.rows, self.first_y = block.shape[0], first_y
        whole = gather_z(block)
        half = whole.shape[1] // 2
        self.keep = jnp.where(first_y, whole[:, :half], whole[:, half:])
        self.got = over(jnp.where(first_y, whole[:, half:], whole[:, :half]), "y")

    def total(self):
        count, width = self.keep.shape[0] // self.rows, self.keep.shape[1]
        sides = [
            jnp.where(self.first_y, a, b).reshape(count, self.rows, width)
            for a, b in ((self.keep, self.got), (self.got, self.keep))
        ]
        return jnp.concatenate(sides, axis=1).reshape(2 * count * self.rows, width)


def spread_sum(term, rows, first_y):
    blocks = term.reshape(-1, 2, rows, term.shape[1])
    pick = lambda a, b: jnp.where(first_y, a, b).reshape(-1, term.shape[1])
    keep = pick(blocks[:, 0], blocks[:, 1])
    got = over(pick(blocks[:, 1], blocks[:, 0]), "y")
    both = jnp.where(
        first_y,
        jnp.concatenate([keep, got], axis=1),
        jnp.concatenate([got, keep], axis=1),
    )
    return both


def gather_z(block):
    return lax.all_gather(block, "z", axis=0, tiled=True)


def sum_z(block):
    return lax.psum_scatter(block.astype(WIDE), "z", scatter_dimension=0, tiled=True)


def padded(block, multiple=128):
    extra = -block.shape[1] % multiple
    return jnp.pad(block, ((0, 0), (0, extra))) if extra else block


def norm_back(gradient, normed, inverse, gain_vec):
    scaled = gradient * gain_vec
    return inverse * (scaled - normed * jnp.mean(scaled * normed, axis=-1, keepdims=True))


def per_device(
    inputs,
    segments,
    positions,
    gain_attn,
    query_weight,
    key_weight,
    value_weight,
    out_weight,
    gain_mlp,
    gate_weight,
    up_weight,
    down_weight,
    cotangent,
):
    own = inputs.shape[0]
    half, count = 4 * own, 8 * own
    length = segments.shape[0] // SEQS
    reach = (DOC_MOST - 2) // count + 1
    period = lax.axis_size("z")
    if length % count == 0:
        period = length // count
        reach = min(reach, period - 1)
    span = (reach + 1) * count
    z, y = lax.axis_index("z"), lax.axis_index("y")
    x, c = lax.axis_index("x"), lax.axis_index("c")
    first_y = y == 0

    w_q, w_k, w_v, w_g, w_u = [
        w.astype(WIDE) for w in (query_weight, key_weight, value_weight, gate_weight, up_weight)
    ]
    w_o, w_d = out_weight.T.astype(WIDE), down_weight.T.astype(WIDE)
    nq, nk, nf = w_q.shape[1] // 2, w_k.shape[1] // 2, w_g.shape[1] // 2
    rows_w = w_q.shape[0]
    halves = lambda w: (w[:, : w.shape[1] // 2], w[:, w.shape[1] // 2 :])
    gain_pair = jnp.stack([gain_attn, gain_mlp] * 2, 1).astype(WIDE)
    chunks = (slice(0, CHUNK), slice(CHUNK, nf))
    triple = lambda cut: jnp.concatenate(
        [padded(halves(w)[i][:, cut]) for i in range(2) for w in (w_d, w_g, w_u)], axis=1
    )
    flow_o = SpreadGather(w_o, first_y)
    near_a = share_columns(
        jnp.concatenate(
            [
                padded(jnp.concatenate([halves(w)[i] for w in (w_q, w_k, w_v, gain_pair)], axis=1))
                for i in range(2)
            ],
            axis=1,
        ),
        first_y,
    )
    full_a = gather_z(near_a)
    x_one = over(inputs, "x"), over(tied(inputs, near_a), "y")
    x_two = plane_step_two(*x_one)
    x_all = plane_join(inputs, *x_one, *x_two)
    near_c = [share_columns(triple(chunks[0]), first_y, x_all)]
    full_c = [gather_z(near_c[0])]
    first_gain = nq + 2 * nk
    gains = full_a[:, first_gain : first_gain + 2].astype(F32)
    gain_first, gain_second = gains[:, 0], gains[:, 1]

    other_positions = lax.ppermute(positions, "y", SWAP)
    token_positions = jnp.where(
        first_y,
        jnp.concatenate([positions, other_positions]),
        jnp.concatenate([other_positions, positions]),
    )
    frequency = rope_base ** (-(jnp.arange(HD // 2, dtype=F32) * 2.0 / HD))
    angles = frequency[:, None] * token_positions.astype(F32)[None, :]
    cos_tab, sin_tab = jnp.cos(angles), jnp.sin(angles)
    places = jnp.arange(8, dtype=jnp.int32)
    flips = places ^ (y * 4 + x * 2 + c).astype(jnp.int32)
    index = (flips % 2) * 4 + flips // 2
    padded_segs = jnp.concatenate([jnp.full((reach * count,), -1, jnp.int32), segments])
    key_segs = lax.dynamic_slice_in_dim(padded_segs, z * count, span, 0)
    query_segs = lax.dynamic_slice_in_dim(segments, z * count, count, 0)
    starts = jnp.sum((key_segs[:, None] < query_segs[None, :]).astype(jnp.int32), axis=0)
    first_rows = jnp.arange(count // BQ, dtype=jnp.int32) * BQ
    lo = starts[first_rows] // KB
    hi = (reach * count + first_rows + BQ + KB - 1) // KB
    full_lo = jnp.clip((starts[first_rows + BQ - 1] + KB - 1) // KB, lo, hi)
    full_hi = jnp.clip((reach * count + first_rows + 1) // KB, full_lo, hi)
    bounds = jnp.stack([lo, full_lo, full_hi, hi])
    own_key = reach * count
    own_bounds = jnp.maximum(bounds, own_key // KB)
    far_bounds = jnp.minimum(bounds, own_key // KB)
    starts = starts[None, :]

    h_one, qkv = project(x_all, gain_first[None, :], full_a)
    near_c.append(share_columns(triple(chunks[1]), first_y, qkv))
    full_c.append(gather_z(near_c[1]))
    turned = to_columns(qkv, index, cos_tab, sin_tab, GROUP + 1, GROUP + 2)
    q_cols, kv_own = turned[: GROUP * HD], turned[GROUP * HD :]
    far_kv = [shifted(kv_own, distance, period) for distance in range(reach, 0, -1)]
    far_kv = [shifted(kv_own, distance, period) for distance in range(reach, 0, -1)]
    kv_own = landed(kv_own, (flow_o, "got"))
    cot_one = plane_step_one(tied(cotangent, kv_own))
    own_part = attend(q_cols, kv_own, starts, own_bounds, (own_key, own_key), (), F32)
    own_part, far_kv, near_0 = lax.optimization_barrier((own_part, far_kv, near_c[0]))
    if reach:
        far_kv = jnp.concatenate(far_kv, axis=1)
        out_cols, logs = attend(q_cols, far_kv, starts, far_bounds, (own_key, 0), own_part, WIDE)
    else:
        out_cols, logs = own_part[0].astype(WIDE), own_part[1]
    out_cols, cot_one, _ = lax.optimization_barrier((out_cols, cot_one, near_c[1]))
    cot_two = plane_step_two(*cot_one)
    full_o = flow_o.total()
    attended = to_rows(out_cols, index, cos_tab, sin_tab, 0, GROUP, GROUP * HD)
    input_f32 = inputs.astype(F32)
    inverse_one = lax.rsqrt(jnp.mean(input_f32 * input_f32, axis=-1, keepdims=True) + eps)
    normed_one = input_f32 * inverse_one
    mid_got = over(dot(attended[half:], full_o, 1, 1).astype(WIDE), "c")
    mid_total = (dot(attended[:half], full_o, 1, 1) + mid_got.astype(F32)).astype(WIDE)
    mid_total, *cot_two = together(mid_total, *cot_two)
    mid_far = plane_sum_one(mid_total)
    mid_near = plane_sum_two(mid_total, *mid_far)
    grad_mix = plane_join(cotangent, *cot_one, *cot_two)
    x_mid = input_f32 + added(mid_total, *mid_near)

    inverse_two = lax.rsqrt(jnp.mean(x_mid * x_mid, axis=-1, keepdims=True) + eps)
    normed_two = x_mid * inverse_two
    h_own = (normed_two * gain_second).astype(WIDE)
    h_step = plane_step_one(h_own)
    h_two = plane_join(h_own, *h_step, *plane_step_two(*h_step))
    h_two, grad_mix = together(h_two, grad_mix)
    other_1 = hidden_units(h_two, grad_mix, full_c[0], half, half)
    mine_1 = hidden_units(h_two, grad_mix, full_c[0], 0, half)
    term_1 = unit_grads(h_two, grad_mix, mine_1[0], other_1[0])
    full_c[1], other_1, mine_1, term_1 = lax.optimization_barrier(
        (full_c[1], other_1, mine_1, term_1)
    )
    sums = [sum_z(term_1)]
    acts_other, back_other, out_other = hidden_units(
        h_two, grad_mix, full_c[1], half, half, other_1[1:]
    )
    back_got, out_got = over(back_other, "c"), over(out_other, "c")
    acts_mine, back_mine, out_mine = hidden_units(h_two, grad_mix, full_c[1], 0, half, mine_1[1:])
    back_total = added_pair(back_mine, back_got)
    back_far = plane_sum_one(back_total)
    term_2 = unit_grads(h_two, grad_mix, acts_mine, acts_other)
    back_near = plane_sum_two(back_total, *back_far)
    *back_near, term_2 = together(*back_near, term_2)
    sums.append(sum_z(term_2))
    grad_h_two = added(back_total, *back_near)
    grad_mid = cotangent.astype(F32) + norm_back(grad_h_two, normed_two, inverse_two, gain_second)
    branch_own = grad_mid.astype(WIDE)
    branch_one = plane_step_one(branch_own)
    branch_two = plane_step_two(*branch_one)
    out_total = added_pair(out_mine, out_got)
    grad_branch = plane_join(branch_own, *branch_one, *branch_two)
    owned = [Unshare(tied(sums[0], *branch_two), first_y)]
    grad_branch, out_total = together(grad_branch, out_total)

    grad_attended = narrow(grad_branch, full_o)
    grad_cols = to_columns(grad_attended, index, cos_tab, sin_tab, 0, GROUP)
    grad_cols, out_total = landed((grad_cols, out_total), (owned[0], "got"))
    out_sends = [
        over(out_total[own : 2 * own], "x"),
        over(out_total[2 * own : 3 * own], "y"),
        across(out_total[3 * own :]),
    ]
    back = functools.partial(attend_back, q_cols)
    prior, far_got = (), []
    if reach:
        dq_far, dkv_far = back(
            far_kv, starts, far_bounds, (own_key, 0), out_cols, logs, grad_cols
        )
        prior = (dq_far,)
        far_got = [
            shifted(
                dkv_far[:, (reach - d) * count : (reach - d + 1) * count].astype(WIDE), -d, period
            )
            for d in range(1, reach + 1)
        ]
    out_term = weight_grads(grad_branch, tied(attended, *prior))
    kv_own, out_term = together(kv_own, out_term)
    dq_cols, dkv_cols = back(
        kv_own, starts, own_bounds, (own_key, own_key), out_cols, logs, grad_cols, prior
    )
    dkv_cols, out_sends, far_got = lax.optimization_barrier((dkv_cols, out_sends, far_got))
    output = (x_mid + added(out_total, *out_sends)).astype(WIDE)
    dkv_own = sum((part.astype(F32) for part in far_got), dkv_cols)
    out_term = spread_sum(tied(out_term, dkv_cols), w_o.shape[0], first_y)
    grad_qkv = to_rows(
        jnp.concatenate([dq_cols, dkv_own], axis=0),
        index,
        cos_tab,
        sin_tab,
        GROUP + 1,
        GROUP + 2,
        full_a.shape[1],
    )
    qkv_part = weight_grads(h_one, grad_qkv)
    grad_qkv, qkv_part, out_term = together(grad_qkv, qkv_part, out_term)
    one_got = over(dot(grad_qkv[half:], full_a, 1, 1).astype(WIDE), "c")
    qkv_part, sums[1], one_got = together(qkv_part, sums[1], one_got)
    one_total = (dot(grad_qkv[:half], full_a, 1, 1) + one_got.astype(F32)).astype(WIDE)
    qkv_grad = sum_z(qkv_part)
    owned.append(Unshare(sums[1], first_y))
    one_far = plane_sum_one(one_total)
    one_far = landed(one_far, (owned[1], "got"))
    one_near = plane_sum_two(one_total, *one_far)
    qkv_raw = qkv_grad
    out_grad = sum_z(tied(out_term, qkv_raw))
    owned_a = Unshare(qkv_grad, first_y)
    *one_near, qkv_grad = together(*one_near, qkv_grad)
    grad_h_one = added(one_total, *one_near)
    input_grad = (grad_mid + norm_back(grad_h_one, normed_one, inverse_one, gain_first)).astype(
        WIDE
    )

    input_grad = landed(input_grad, (owned_a, "got"))
    owned = [part.both() for part in owned]
    kept = [CHUNK, nf - CHUNK]
    width = [full.shape[1] // 3 for full in full_c]

    def unit_columns(k, *after):
        parts = [
            owned[j][i][:, k * width[j] : k * width[j] + kept[j]] for i in range(2) for j in range(2)
        ]
        if after:
            parts = lax.optimization_barrier((parts, after))[0]
        return jnp.concatenate(parts, axis=1).astype(F32)

    down_out, gate_out, up_out = unit_columns(0, qkv_raw).T, unit_columns(1), unit_columns(2)
    one, two = owned_a.both()
    pick = lambda a, b: jnp.concatenate([one[:, a:b], two[:, a:b]], axis=1).astype(F32)
    q_out, k_out, v_out = pick(0, nq), pick(nq, nq + nk), pick(nq + nk, nq + 2 * nk)

    def row_sums(weight, grad):
        return jnp.sum(weight.astype(F32) * grad, axis=1)

    gain_sums = jnp.stack(
        [
            row_sums(w_q, q_out) + row_sums(w_k, k_out) + row_sums(w_v, v_out),
            row_sums(w_g, gate_out) + row_sums(w_u, up_out),
        ]
    )
    gain_sums = gain_sums + lax.ppermute(gain_sums, "x", SWAP)
    gain_sums = gain_sums + lax.ppermute(gain_sums, "c", SWAP)
    gain_sums, out_grad = together(gain_sums, out_grad)
    o_out = as_f32(out_grad).T
    gain_one_out = gain_sums[0] / gain_attn.astype(WIDE).astype(F32)
    gain_two_out = gain_sums[1] / gain_mlp.astype(WIDE).astype(F32)
    return (
        output,
        input_grad,
        gain_one_out,
        q_out,
        k_out,
        v_out,
        o_out,
        gain_two_out,
        gate_out,
        up_out,
        down_out,
    )


def solution(mesh):
    seq, tensor = mesh.shape["seq"], mesh.shape["tensor"]
    grid = Mesh(
        mesh.devices.reshape(seq // 2, 2, tensor // 2, 2), ("z", "y", "x", "c")
    )
    rows, cols = ("z", "y"), ("x", "c")
    tokens, weight, weight_t = P(rows + cols, None), P(rows, cols), P(cols, rows)
    in_specs = (
        tokens,
        P(),
        P(rows),
        P(rows),
        weight,
        weight,
        weight,
        weight_t,
        P(rows),
        weight,
        weight,
        weight_t,
        tokens,
    )
    out_specs = (
        tokens,
        tokens,
        P(rows),
        weight,
        weight,
        weight,
        weight_t,
        P(rows),
        weight,
        weight,
        weight_t,
    )
    return jax.shard_map(
        per_device, mesh=grid, in_specs=in_specs, out_specs=out_specs, check_vma=False
    )
```
